256 devices in a mesh: dp: 32 (over y, x, core), tensor: 8 (over z).
Axes of the slice: x: 4, y: 4, z: 8, core: 2. Of those that a mesh axis runs over, the one named last changes fastest.
Arguments:
- layer_out: bfloat16 [256, 5120], P('dp', 'tensor'), may hold values from -140 to 140
- resid_mid: bfloat16 [256, 5120], P('dp', 'tensor'), may hold values from -140 to 140
- final_gain: float32 [5120], replicated, may hold values from 0.5 to 1.5
- mlp_gain: float32 [5120], replicated, may hold values from 0.5 to 1.5
- head_weight: bfloat16 [98304, 5120], P(('tensor', 'dp')), may hold values from -0.28125 to 0.28125
- w_gate: bfloat16 [16384, 5120], P(('tensor', 'dp')), may hold values from -0.078125 to 0.078125
- w_up: bfloat16 [16384, 5120], P(('tensor', 'dp')), may hold values from -0.078125 to 0.078125
- w_down: bfloat16 [16384, 5120], P(('tensor', 'dp')), may hold values from -0.046875 to 0.046875
- teacher_logits: bfloat16 [256, 98304], P('dp', 'tensor'), may hold values from -15 to 15
- assign: int32 [32, 8], P('dp'), may hold values from 0 to 7, each once within a row
- lengths: int32 [32, 2], P('dp'), may hold values from 1 to 4
- token_ids: int32 [256], P('dp'), may hold values from 0 to 98303
Outputs:
- grad_resid: bfloat16 [256, 5120], P('dp', 'tensor')
- grad_head: bfloat16 [98304, 5120], P(('tensor', 'dp'))
- grad_gate: bfloat16 [16384, 5120], P(('tensor', 'dp'))
- grad_up: bfloat16 [16384, 5120], P(('tensor', 'dp'))
- grad_down: bfloat16 [16384, 5120], P(('tensor', 'dp'))
The draws below stay inside these ranges and needn't reach their ends.
Inputs may be any that keep to these rules, and one draw needn't show every extreme that they name: `assign`: each row is a permutation of the 8 slots.
All inputs are finite; a program needn't handle non-finite values.
Results may differ from the reference program's by a relative error of at most 0.02.
Values may be sent and summed in bfloat16 or wider, within the bound.
A program may use at most 128 MiB of HBM per device.

```python
import math
import jax
import jax.numpy as jnp
import numpy as np
from jax import lax

D = 5120
SEQS = 2
SLOT = 4
V = 98304
FF = 16384
GROUPS = 32
TOK_G = 8
TOKENS = 256


def scaled_field(key):
    key_base, key_rows, key_cols = jax.random.split(key, 3)
    base_values = jnp.clip(jax.random.normal(key_base, (TOKENS, D), jnp.float32), -5.0, 5.0)
    row_scales = jnp.exp(jax.random.uniform(key_rows, (TOKENS, 1), jnp.float32, math.log(0.3), math.log(3.0)))
    column_ramp = jnp.exp(math.log(3.0) * jnp.arange(D, dtype=jnp.float32) / D)[None, :]
    column_scales = jnp.exp(jax.random.uniform(key_cols, (1, D), jnp.float32, math.log(0.3), math.log(3.0))) * column_ramp
    mixed = base_values
    return mixed * row_scales * column_scales


def draw_layer_out(key, part):
    key = jax.random.fold_in(key, 5)
    field = scaled_field(key)
    return field.astype(jnp.bfloat16)


def draw_resid_mid(key, part):
    key = jax.random.fold_in(key, 7)
    field = scaled_field(key)
    return field.astype(jnp.bfloat16)


def draw_head_weight(key, part):
    key = jax.random.fold_in(key, 6)
    spread = 3.0 / math.sqrt(D)
    weights = jnp.clip(jax.random.normal(key, (V, D), jnp.float32), -5.0, 5.0) * spread
    return weights.astype(jnp.bfloat16)


def draw_lengths(key, part):
    key = jax.random.fold_in(key, 8)
    drawn = jax.random.randint(key, (GROUPS, SEQS), 1, SLOT + 1, jnp.int32)
    drawn = drawn.at[0, 0].set(SLOT)
    drawn = drawn.at[GROUPS - 1, SEQS - 1].set(1)
    return drawn


def set_ends(values, stream_key, low, largest):
    shape = values.shape
    place = [jax.random.randint(jax.random.fold_in(stream_key, axis), (), 0, shape[axis]) for axis in range(len(shape))]
    values = values.at[tuple(place)].set(low)
    longest = shape.index(max(shape))
    place[longest] = (place[longest] + 1) % shape[longest]
    return values.at[tuple(place)].set(largest)


def shard_levels(key, dims, pieces, smallest, top_value):
    loudness, own = 1.0, jax.random.fold_in(key, 6)
    for axis_at, shards_of in pieces:
        heights = jnp.exp(jax.random.uniform(jax.random.fold_in(own, axis_at), (shards_of,), jnp.float32, smallest / len(pieces), top_value / len(pieces)))
        loudness = loudness * jnp.repeat(heights, dims[axis_at] // shards_of).reshape([-1 if axis == axis_at else 1 for axis in range(len(dims))])
    return loudness


def skewed_wide(key, shape, amount, skew):
    portions = [min(1 << octave, amount + 1 - (1 << octave)) * (1 << 20) // math.isqrt((1 << octave) ** skew) + 1 for octave in range((amount + 1).bit_length()) if 1 << octave <= amount]
    width = 1 + sum(portions) // (1 << 30)
    listing = np.cumsum(np.array([max(1, weight // width) for weight in portions]))
    pick = jax.random.randint(jax.random.fold_in(key, 1), shape, 0, int(listing[len(portions) - 1]))
    start = jnp.left_shift(1, jnp.searchsorted(jnp.asarray(listing, jnp.int32), pick, side="right").astype(jnp.int32))
    rank = start - 1 + jax.random.randint(jax.random.fold_in(key, 4), shape, 0, 1 << 30) % jnp.minimum(start, amount + 1 - start)
    return jax.random.permutation(jax.random.fold_in(key, 2), amount)[rank].astype(jnp.int32)


def scatter_about(key, shape, scale, most, cuts=(), held_as=jnp.bfloat16):
    values = scale * jax.random.normal(key, shape, jnp.float32)
    if cuts:
        values = values * shard_levels(key, shape, cuts, -0.22, 0.18)
    return jnp.clip(values, -most, most).astype(held_as)


def setup_inputs(seed: int = 0) -> dict:
    key_list = jax.random.split(jax.random.key(seed), 13)
    layer_out = draw_layer_out(jax.random.fold_in(key_list[12], 71), 0)
    resid_mid = draw_resid_mid(jax.random.fold_in(key_list[12], 71), 0)
    final_gain = jnp.clip(1.0 + 0.1 * jax.random.normal(key_list[2], (D,), jnp.float32), 0.5, 1.5)
    mlp_gain = jnp.clip(1.0 + 0.1 * jax.random.normal(key_list[3], (D,), jnp.float32), 0.5, 1.5)
    head_weight = draw_head_weight(jax.random.fold_in(key_list[12], 71), 0)
    w_gate = scatter_about(key_list[5], (FF, D), D ** -0.5, 0.078125, ((0, 256),))
    w_up = scatter_about(key_list[6], (FF, D), D ** -0.5, 0.078125, ((0, 256),))
    w_down = scatter_about(key_list[7], (FF, D), FF ** -0.5, 0.046875, ((0, 256),))
    teacher_logits = scatter_about(key_list[8], (TOKENS, V), 3.0, 15.0, ((0, 32), (1, 8)))
    assign = jax.vmap(lambda own: jax.random.permutation(own, TOK_G))(jax.random.split(key_list[9], GROUPS)).reshape((GROUPS, TOK_G)).astype(jnp.int32)
    lengths = draw_lengths(jax.random.fold_in(key_list[12], 71), 0)
    token_ids = set_ends(skewed_wide(key_list[11], (TOKENS,), V, 2), jax.random.fold_in(key_list[11], 3), 0, V - 1).astype(jnp.int32)
    return dict(layer_out=layer_out, resid_mid=resid_mid, final_gain=final_gain, mlp_gain=mlp_gain, head_weight=head_weight, w_gate=w_gate, w_up=w_up, w_down=w_down, teacher_logits=teacher_logits, assign=assign, lengths=lengths, token_ids=token_ids)


EPS = 1e-06
CE_WEIGHT = 0.5
LOSS_SCALE = 4096.0

def rms_scale(values):
    return lax.rsqrt(lax.optimization_barrier(jnp.mean(values * values, axis=-1, keepdims=True)) + EPS)

def norm_back(values, gain_vector, out_grads):
    row_scale = rms_scale(values)
    weighted = gain_vector * out_grads
    inner_sum = lax.optimization_barrier(jnp.sum(values * weighted, axis=-1, keepdims=True)) / values.shape[-1]
    return row_scale * weighted - values * row_scale ** 3 * inner_sum

def reference(layer_out, resid_mid, final_gain, mlp_gain, head_weight, w_gate, w_up, w_down, teacher_logits, assign, lengths, token_ids):
    out_wide = layer_out.astype(jnp.float32)
    final_rows = (out_wide * rms_scale(out_wide) * final_gain).astype(jnp.bfloat16)
    teacher_grid = teacher_logits.reshape(GROUPS, TOK_G, V)
    picked = jnp.take_along_axis(teacher_grid, assign[:, :, None], axis=1).reshape(TOKENS, V)
    teacher = picked.astype(jnp.float32)
    logits = jnp.dot(final_rows, head_weight.T, preferred_element_type=jnp.float32)
    row_max = lax.optimization_barrier(jnp.max(logits, axis=1, keepdims=True))
    expd = jnp.exp(logits - row_max)
    totals = lax.optimization_barrier(jnp.sum(expd, axis=1, keepdims=True))
    moments = lax.optimization_barrier(jnp.sum(expd * (logits - teacher), axis=1, keepdims=True))
    probs_all = expd / totals
    slot_index = jnp.arange(SLOT, dtype=jnp.int32)
    live_mask = (slot_index[None, None, :] < lengths[:, :, None]).reshape(TOKENS).astype(jnp.float32)
    live_count = jnp.sum(lengths).astype(jnp.float32)
    token_weight = live_mask * (LOSS_SCALE / live_count)
    target = (token_ids[:, None] == jnp.arange(V, dtype=jnp.int32)[None, :]).astype(jnp.float32)
    dlogits = token_weight[:, None] * (probs_all * (logits - teacher - moments / totals + CE_WEIGHT) - CE_WEIGHT * target)
    dlog_b = dlogits.astype(jnp.bfloat16)
    grad_head = jnp.dot(dlog_b.T, final_rows, preferred_element_type=jnp.float32).astype(jnp.bfloat16)
    dfinal = jnp.dot(dlog_b, head_weight, preferred_element_type=jnp.float32)
    grad_out = norm_back(out_wide, final_gain, dfinal)
    grad_out_b = grad_out.astype(jnp.bfloat16)
    mid_wide = resid_mid.astype(jnp.float32)
    normed = (mid_wide * rms_scale(mid_wide) * mlp_gain).astype(jnp.bfloat16)
    gate_pre = jnp.dot(normed, w_gate.T, preferred_element_type=jnp.float32)
    up_pre = jnp.dot(normed, w_up.T, preferred_element_type=jnp.float32)
    gate_sigmoid = jax.nn.sigmoid(gate_pre)
    activated = (gate_pre * gate_sigmoid * up_pre).astype(jnp.bfloat16)
    act_grad = jnp.dot(grad_out_b, w_down.T, preferred_element_type=jnp.float32)
    grad_down = jnp.dot(activated.T, grad_out_b, preferred_element_type=jnp.float32).astype(jnp.bfloat16)
    up_grad = (act_grad * gate_pre * gate_sigmoid).astype(jnp.bfloat16)
    gate_grad = (act_grad * up_pre * gate_sigmoid * (1.0 + gate_pre * (1.0 - gate_sigmoid))).astype(jnp.bfloat16)
    grad_gate = jnp.dot(gate_grad.T, normed, preferred_element_type=jnp.float32).astype(jnp.bfloat16)
    grad_up = jnp.dot(up_grad.T, normed, preferred_element_type=jnp.float32).astype(jnp.bfloat16)
    grad_normed = jnp.dot(gate_grad, w_gate, preferred_element_type=jnp.float32) + jnp.dot(up_grad, w_up, preferred_element_type=jnp.float32)
    grad_resid = (grad_out + norm_back(mid_wide, mlp_gain, grad_normed)).astype(jnp.bfloat16)
    return (grad_resid, grad_head, grad_gate, grad_up, grad_down)
```

```python
import jax
import jax.numpy as jnp
from jax import lax
from jax.experimental import pallas as pl
from jax.experimental.pallas import tpu as pltpu
from jax.sharding import PartitionSpec as P

D = 5120
SLOT = 4
EPS = 1e-06
CE_WEIGHT = 0.5
LOSS_SCALE = 4096.0

BLOCK = 640
SLICE = 1280
CHIPS = 16
F32 = jnp.float32
BF16 = jnp.bfloat16
VMEM_LIMIT = 52 * 1024 * 1024
GRADS_VMEM = 20 * 1024 * 1024


def contract_cols(left, right):
    return lax.dot_general(left, right, (((1,), (1,)), ((), ())), preferred_element_type=F32)


def wrap(v, size):
    return jnp.where(v >= size, v - size, v)


def ring_bits(v):
    high = v // 2
    return v % 2 + high - 2 * (v % 2) * high, high


class Spot:
    def __init__(self):
        self.d = lax.axis_index("dp")
        self.z = lax.axis_index("tensor")
        self.chip = lax.div(self.d, 2)
        self.c = self.d - 2 * self.chip
        self.y = lax.div(self.chip, 4)
        self.x = self.chip - 4 * self.y
        c, other = self.c, 1 - self.c
        xv, yv = lax.div(self.x, 2), lax.div(self.y, 2)
        x_low, y_low = self.x - 2 * xv, self.y - 2 * yv
        xu, yu = x_low + xv - 2 * x_low * xv, y_low + yv - 2 * y_low * yv
        x_near, y_near = self.x + 1 - 2 * x_low, self.y + 1 - 2 * y_low
        x_far, y_far = 3 - self.x, 3 - self.y
        self.half = lax.div(self.z, 4)
        self.z_low = self.z - 4 * self.half
        bits = (xu, yu, xv, yv)
        moved = (x_near, y_near, x_far, y_far)
        self.own_bits = [bits[i] * other + bits[(i + 2) % 4] * c for i in range(4)]
        self.sib_bits = [bits[i] * c + bits[(i + 2) % 4] * other for i in range(4)]
        self.moved = [moved[i] * other + moved[(i + 2) % 4] * c for i in range(4)]
        self.own_base = [self.bases(self.own_bits, kk) for kk in range(2)]
        self.sib_base = [self.bases(self.sib_bits, kk) for kk in range(2)]

    def bases(self, bits, kk):
        out = [jnp.int32(0)]
        for s in range(4):
            out.append(out[-1] + bits[(kk + s) % 4] * (8 >> s))
        return out

    def bit(self, kk, s):
        return self.own_bits[(kk + s) % 4]

    def sib_bit(self, kk, s):
        return self.sib_bits[(kk + s) % 4]

    def place(self, kk):
        return self.own_base[kk][4]

    def partner(self, kk, s):
        i = (kk + s) % 4
        chip = self.y * 4 + self.moved[i] if i % 2 == 0 else self.moved[i] * 4 + self.x
        return (chip * 2 + self.c, self.z)

    def diagonal(self, kk, s):
        i, j = (kk + s) % 4, (kk + s + 1) % 4
        x, y = (self.moved[i], self.moved[j]) if i % 2 == 0 else (self.moved[j], self.moved[i])
        return ((y * 4 + x) * 2 + self.c, self.z)

    def sibling(self):
        return (self.chip * 2 + 1 - self.c, self.z)

    def column_peer(self, i):
        core = self.c if i % 2 == 0 else 1 - self.c
        return (self.chip * 2 + core, wrap(self.z + i // 2, 8) if i > 1 else self.z)


def greet(spot):
    barrier = pltpu.get_barrier_semaphore()
    for i in range(1, 16):
        pl.semaphore_signal(barrier, inc=1, device_id=spot.column_peer(i), device_id_type=pl.DeviceIdType.MESH)

    def body(j, carry):
        chip = wrap(spot.chip + j, CHIPS)
        for core in range(2):
            pl.semaphore_signal(
                barrier, inc=1, device_id=(chip * 2 + core, spot.z), device_id_type=pl.DeviceIdType.MESH
            )
        return carry

    lax.fori_loop(1, CHIPS, body, 0)


def greeted():
    pl.semaphore_wait(pltpu.get_barrier_semaphore(), 45)


def remote(src, dst, send_sem, recv_sem, target):
    return pltpu.make_async_remote_copy(
        src_ref=src,
        dst_ref=dst,
        send_sem=send_sem,
        recv_sem=recv_sem,
        device_id=target,
        device_id_type=pl.DeviceIdType.MESH,
    )


def row_scale(raw, core):
    total = jnp.zeros((8, BLOCK), F32)
    for zb in range(8):
        part = raw[8 * core + zb].astype(F32)
        total = total + part * part
    return lax.rsqrt(jnp.sum(total, axis=1, keepdims=True) / D + EPS)


def wait_bytes(ref, sem):
    pltpu.make_async_copy(ref, ref, sem).wait()


class Gather:
    def __init__(self, spot, full, xy_send, xy_recv, sib_send, sib_recv):
        self.spot, self.full = spot, full
        self.xy_send, self.xy_recv, self.sib_send, self.sib_recv = xy_send, xy_recv, sib_send, sib_recv

    def view(self, kk, off, n, core=None):
        core = self.spot.c if core is None else core
        return self.full.at[2 * core + kk, pl.ds(off, n)]

    def send(self, kk, target, idx, off, n):
        view = self.view(kk, off, n)
        remote(view, view, self.xy_send.at[kk], self.xy_recv.at[kk, idx], target).start()

    def arrived(self, kk, idx, off, n):
        wait_bytes(self.view(kk, off, n), self.xy_recv.at[kk, idx])

    def pass_on(self, kk, idx, off, n):
        view = self.view(kk, off, n)
        remote(view, view, self.sib_send.at[kk], self.sib_recv.at[kk, idx], self.spot.sibling()).start()

    def step(self, stage, kk):
        spot = self.spot
        flip = [(8 >> s) * (1 - 2 * spot.bit(kk, s)) for s in range(4)]
        own, four = spot.place(kk), spot.own_base[kk][2]
        if stage == 0:
            self.send(kk, spot.diagonal(kk, 2), 2, own, 1)
            self.send(kk, spot.partner(kk, 3), 0, own, 1)
            self.send(kk, spot.partner(kk, 2), 1, own, 1)
        elif stage == 1:
            self.arrived(kk, 0, own + flip[3], 1)
            self.arrived(kk, 1, own + flip[2], 1)
            self.arrived(kk, 2, own + flip[2] + flip[3], 1)
            self.send(kk, spot.partner(kk, 1), 3, four, 2)
            self.send(kk, spot.partner(kk, 1), 4, four + 2, 2)
            self.send(kk, spot.partner(kk, 0), 5, four, 4)
            self.pass_on(kk, 0, four, 4)
        elif stage == 2:
            new = four + flip[1]
            for i in range(2):
                self.arrived(kk, 3 + i, new + 2 * i, 2)
                self.send(kk, spot.partner(kk, 0), 6 + i, new + 2 * i, 2)
            self.pass_on(kk, 1, new, 4)
        elif stage == 3:
            new = four + flip[0]
            self.arrived(kk, 5, new, 4)
            self.pass_on(kk, 2, new, 4)
            new = new + flip[1]
            for i in range(2):
                self.arrived(kk, 6 + i, new + 2 * i, 2)
                self.pass_on(kk, 3 + i, new + 2 * i, 2)
        else:
            other = 1 - spot.c
            four = spot.sib_base[kk][2]
            over_1 = four + 4 * (1 - 2 * spot.sib_bit(kk, 1))
            over_0 = 8 * (1 - 2 * spot.sib_bit(kk, 0))
            last = over_1 + over_0
            pieces = ((four, 4), (over_1, 4), (four + over_0, 4), (last, 2), (last + 2, 2))
            for idx, (off, n) in enumerate(pieces):
                wait_bytes(self.view(kk, off, n, other), self.sib_recv.at[kk, idx])

    def finish(self):
        for kk in range(2):
            wait_bytes(self.full.at[kk, pl.ds(0, 15)], self.xy_send.at[kk])
            wait_bytes(self.full.at[kk], self.sib_send.at[kk])


def block_place(k, chip):
    xu, xv = ring_bits(chip % 4)
    yu, yv = ring_bits(chip // 4)
    bits = (xu, yu, xv, yv)
    return sum(bits[(k + s) % 4] * (8 >> s) for s in range(4))


def slice_columns(kk, core):
    return pl.ds(pl.multiple_of((2 * core + kk) * SLICE, SLICE), SLICE)


def lay_out(full, out, kk, core):
    for chip in range(CHIPS):
        low, high = block_place(kk, chip), block_place(2 + kk, chip)
        out[16 * chip : 16 * chip + 16, slice_columns(kk, core)] = full[2 * core + kk, low + (high - low) * core]


REDUCE_SCRATCH = [
    pltpu.VMEM((4, 16, 16, SLICE), BF16),
    pltpu.VMEM((2, 16, 16, SLICE), BF16),
    pltpu.VMEM((2, 15, 16, SLICE), BF16),
    pltpu.VMEM((8, 8, BLOCK), BF16),
    pltpu.VMEM((8, 8, BLOCK), BF16),
    pltpu.VMEM((2, 1, 128), F32),
    pltpu.VMEM((9, 1, 128), F32),
    pltpu.SemaphoreType.DMA((2,)),
    pltpu.SemaphoreType.DMA((2, 2)),
    pltpu.SemaphoreType.DMA((2,)),
    pltpu.SemaphoreType.DMA((2, 7)),
    pltpu.SemaphoreType.DMA((6,)),
]


class Reduce:
    def __init__(self, spot, scratch):
        self.spot = spot
        (
            self.partial,
            self.from_sib,
            self.from_xy,
            self.to_col,
            self.from_col,
            self.inner_to,
            self.inner_from,
            self.sib_send,
            self.sib_recv,
            self.xy_send,
            self.xy_recv,
            self.col_sems,
        ) = scratch

    def sib_copy(self, kk, sub, core, bit):
        half = (1 - bit) if sub == 0 else bit
        return remote(
            self.partial.at[2 * core + kk, pl.ds(half * 8, 8)],
            self.from_sib.at[kk, pl.ds(half * 8, 8)],
            self.sib_send.at[kk],
            self.sib_recv.at[kk, sub],
            self.spot.sibling(),
        )

    def start(self, kk, sub):
        self.sib_copy(kk, sub, 1 - self.spot.c, self.spot.sib_bit(kk, 0)).start()

    def from_sibling(self, kk, sub):
        self.sib_copy(kk, sub, self.spot.c, self.spot.bit(kk, 0)).wait_recv()

    def add(self, kk, off, ref, ref_off, n):
        k = 2 * self.spot.c + kk

        def body(i, carry):
            self.partial[k, off + i] = self.partial[k, off + i] + ref[kk, ref_off + i]
            return carry

        if n == 1:
            body(0, 0)
        else:
            lax.fori_loop(0, n, body, 0)

    def plan(self, kk, s):
        n = 8 >> s
        landing = 16 - 2 * n
        bit = self.spot.bit(kk, s)
        gone = self.spot.own_base[kk][s] + (1 - bit) * n
        kept = self.spot.own_base[kk][s] + bit * n
        half = n // 2
        after = self.spot.bit(kk, s + 1)
        pieces = []
        for sub in range(2):
            shift = ((1 - after) if sub == 0 else after) * half
            pieces.append((gone + shift, kept + shift, landing + sub * half, half, 2 * s + sub))
        return pieces

    def xy_copy(self, kk, s, piece):
        gone, _, landing, n, idx = piece
        return remote(
            self.partial.at[2 * self.spot.c + kk, pl.ds(gone, n)],
            self.from_xy.at[kk, pl.ds(landing, n)],
            self.xy_send.at[kk],
            self.xy_recv.at[kk, idx],
            self.spot.partner(kk, s),
        )

    def xy_start(self, kk, s, piece):
        self.xy_copy(kk, s, piece).start()

    def plane(self, beside=None):
        beside = beside or {}
        spot = self.spot
        for kk in range(2):
            self.from_sibling(kk, 0)
            for piece in self.plan(kk, 0):
                self.add(kk, piece[0], self.from_sib, piece[0], piece[3])
                self.xy_start(kk, 0, piece)
        for kk in range(2):
            self.from_sibling(kk, 1)
            self.add(kk, spot.bit(kk, 0) * 8, self.from_sib, spot.bit(kk, 0) * 8, 8)
        for work in beside.get(-1, ()):
            work()
        for kk in range(2):
            piece = self.plan(kk, 0)[0]
            self.xy_copy(kk, 0, piece).wait_recv()
            self.add(kk, piece[1], self.from_xy, piece[2], piece[3])
            for follow in self.plan(kk, 1):
                self.xy_start(kk, 1, follow)
        for kk in range(2):
            piece = self.plan(kk, 0)[1]
            self.xy_copy(kk, 0, piece).wait_recv()
            self.add(kk, piece[1], self.from_xy, piece[2], piece[3])
        for work in beside.get(0, ()):
            work()
        places = []
        for kk in range(2):
            own = spot.place(kk)
            by_2 = own + 2 * (1 - 2 * spot.bit(kk, 2))
            flip_3 = 1 - 2 * spot.bit(kk, 3)
            places.append((own, by_2, flip_3))
        for kk in range(2):
            piece = self.plan(kk, 1)[0]
            own, by_2, flip_3 = places[kk]
            self.xy_copy(kk, 1, piece).wait_recv()
            self.add(kk, piece[1], self.from_xy, piece[2], piece[3])
            self.tail_copy(kk, by_2 + flip_3, 2, spot.diagonal(kk, 2)).start()
            self.tail_copy(kk, by_2, 0, spot.partner(kk, 2)).start()
        for kk in range(2):
            piece = self.plan(kk, 1)[1]
            own, by_2, flip_3 = places[kk]
            self.xy_copy(kk, 1, piece).wait_recv()
            self.add(kk, piece[1], self.from_xy, piece[2], piece[3])
            self.tail_copy(kk, own + flip_3, 1, spot.partner(kk, 3)).start()
        for work in beside.get(1, ()):
            work()
        sums = []
        for kk in range(2):
            total = self.partial[2 * spot.c + kk, places[kk][0]].astype(F32)
            for i in range(3):
                self.tail_copy(kk, places[kk][0], i, spot.sibling()).wait_recv()
                total = total + self.from_xy[kk, 12 + i].astype(F32)
            sums.append(total)
        return sums

    def tail_copy(self, kk, block, i, target):
        return remote(
            self.partial.at[2 * self.spot.c + kk, pl.ds(block, 1)],
            self.from_xy.at[kk, pl.ds(12 + i, 1)],
            self.xy_send.at[kk],
            self.xy_recv.at[kk, 4 + i],
            target,
        )

    def column(self, sums, raw, gain, scale, beside=()):
        spot = self.spot
        for kk in range(2):
            for j in range(2):
                for core in range(2):
                    part = sums[kk][8 * core : 8 * core + 8, j * BLOCK : (j + 1) * BLOCK]
                    self.to_col[2 * (2 * kk + j) + core] = part.astype(BF16)
        row = lax.broadcasted_iota(jnp.int32, (8, 128), 0)
        diagonal = row == lax.broadcasted_iota(jnp.int32, (8, 128), 1)
        for core in range(2):
            total = jnp.zeros((8, BLOCK), F32)
            for kk in range(2):
                for j in range(2):
                    zb = 4 * spot.c + 2 * kk + j
                    part = sums[kk][8 * core : 8 * core + 8, j * BLOCK : (j + 1) * BLOCK]
                    total = total + raw[8 * core + zb].astype(F32) * gain[zb] * part
            inner = jnp.where(diagonal, jnp.sum(total, axis=1, keepdims=True), 0.0)
            self.inner_to[core] = jnp.sum(inner, axis=0, keepdims=True)
        to_sibling = remote(
            self.inner_to.at[1 - spot.c],
            self.inner_from.at[8],
            self.col_sems.at[4],
            self.col_sems.at[5],
            spot.sibling(),
        )
        to_sibling.start()
        for i in range(8):
            zdst = 4 * spot.c + i // 2
            mine = jnp.logical_and(zdst == spot.z, spot.c == i % 2)

            @pl.when(jnp.logical_not(mine))
            def _(i=i, zdst=zdst):
                remote(
                    self.to_col.at[i],
                    self.from_col.at[spot.z],
                    self.col_sems.at[0],
                    self.col_sems.at[1],
                    (spot.chip * 2 + i % 2, zdst),
                ).start()

            @pl.when(mine)
            def _(i=i):
                self.from_col[spot.z] = self.to_col[i]

        to_sibling.wait_recv()
        self.inner_from[0] = self.inner_to[spot.c] + self.inner_from[8]
        for i in range(1, 8):
            remote(
                self.inner_from.at[0],
                self.inner_from.at[i],
                self.col_sems.at[2],
                self.col_sems.at[3],
                spot.column_peer(2 * i),
            ).start()
        for work in beside:
            work()
        own = raw[8 * spot.c + spot.z].astype(F32)
        own_gain = gain[spot.z]
        wait_column(spot, self.from_col, self.col_sems.at[1])
        grad = jnp.zeros((8, BLOCK), F32)
        for zsrc in range(8):
            grad = grad + self.from_col[zsrc].astype(F32)
        wait_bytes(self.inner_from.at[pl.ds(1, 7)], self.col_sems.at[3])
        inner = jnp.zeros((1, 128), F32)
        for i in range(8):
            inner = inner + self.inner_from[i]
        inner = jnp.sum(jnp.where(diagonal, inner, 0.0), axis=1, keepdims=True) / D
        return scale * own_gain * grad - own * (scale * scale * scale) * inner

    def finish(self):
        for kk in range(2):
            wait_bytes(self.partial.at[kk], self.sib_send.at[kk])
            wait_bytes(self.partial.at[kk, pl.ds(0, 15)], self.xy_send.at[kk])
        wait_column(self.spot, self.to_col, self.col_sems.at[0])
        wait_bytes(self.inner_from.at[pl.ds(1, 7)], self.col_sems.at[2])
        wait_bytes(self.inner_from.at[pl.ds(8, 1)], self.col_sems.at[4])


def wait_column(spot, ref, sem):
    own = spot.half == spot.c

    @pl.when(own)
    def _():
        wait_bytes(ref.at[pl.ds(0, 7)], sem)

    @pl.when(jnp.logical_not(own))
    def _():
        wait_bytes(ref, sem)


def program(
    layer_out,
    resid_mid,
    final_gain,
    mlp_gain,
    teacher_in,
    assign,
    lengths,
    token_ids,
    head_hbm,
    gate_hbm,
    up_hbm,
    down_hbm,
    grad_first,
    grad_second,
    final_rows,
    normed,
    grad_rows,
    dlog_t,
    hidden_t,
    activated_t,
    head,
    w_gate_up,
    w_down,
    dlog,
    dlog_turned,
    hidden_turned,
    raw_out,
    raw_mid,
    full_out,
    full_mid,
    full_grad,
    packed,
    got,
    logits_ref,
    gate_up_pre,
    act_grad,
    first,
    second,
    stats_pad,
    own_b,
    own_from,
    scale_ref,
    load_sem,
    raw_sems,
    plane_sems,
    stat_sems,
    own_sems,
    xy_send,
    xy_recv,
    sib_send,
    sib_recv,
    *scratch,
):
    spot = Spot()
    c, other = spot.c, 1 - spot.c
    loads = [
        pltpu.make_async_copy(src, dst, load_sem.at[i])
        for i, (src, dst) in enumerate(
            (
                (head_hbm, head),
                (gate_hbm, w_gate_up.at[pl.ds(0, 64)]),
                (up_hbm, w_gate_up.at[pl.ds(64, 64)]),
                (down_hbm, w_down),
            )
        )
    ]
    for load in loads:
        load.start()
    reduces = [Reduce(spot, scratch[: len(REDUCE_SCRATCH)]), Reduce(spot, scratch[len(REDUCE_SCRATCH) :])]
    gathers = [
        Gather(spot, full, xy_send.at[a], xy_recv.at[a], sib_send.at[a], sib_recv.at[a])
        for a, full in enumerate((full_out, full_mid, full_grad))
    ]
    gather_out, gather_mid, gather_grad = gathers

    greet(spot)
    mine = 8 * c + spot.z
    raw_out[mine] = layer_out[...]
    raw_mid[mine] = resid_mid[...]

    row = lax.broadcasted_iota(jnp.int32, (8, 128), 0)
    lane = lax.broadcasted_iota(jnp.int32, (8, 128), 1)

    def by_row(values):
        out = jnp.zeros((8, 128), jnp.int32)
        for r, value in enumerate(values):
            out = jnp.where(row == r, value, out)
        return out

    order = by_row([assign[0, r] for r in range(8)])[:, 0:1]
    ids = by_row([token_ids[r] for r in range(8)])
    slots = by_row([lengths[0, r // SLOT] for r in range(8)])
    live = (lax.rem(row, SLOT) < slots).astype(jnp.int32)
    picked = jnp.zeros((8, teacher_in.shape[1]), F32)
    for r in range(8):
        picked = picked + jnp.where(order == r, teacher_in[r : r + 1, :].astype(F32), 0.0)
    picked = picked.astype(BF16)
    digits = jnp.where(lane == 0, ids >> 12, jnp.where(lane == 1, (ids >> 6) & 63, ids & 63))
    digits = jnp.where(lane == 3, live, digits)
    extras = digits.astype(F32).astype(BF16)
    for peer in range(32):
        packed[peer, :, 0:384] = picked[:, peer * 384 : (peer + 1) * 384]
        packed[peer, :, 384:512] = extras
    got[spot.d] = packed[spot.d]
    greeted()

    def send_raw(a, own, raw):
        for i in range(1, 8):
            remote(own, raw.at[mine], raw_sems.at[a, 0], raw_sems.at[a, 1], spot.column_peer(2 * i)).start()

    def pass_raw(a, raw):
        wait_bytes(raw.at[pl.ds(0, 7)], raw_sems.at[a, 1])
        rows = raw.at[pl.ds(8 * c, 8)]
        remote(rows, rows, raw_sems.at[a, 2], raw_sems.at[a, 3], spot.sibling()).start()

    def plane_start(i, carry):
        peer = wrap(spot.d + i, 32)
        remote(packed.at[peer], got.at[spot.d], plane_sems.at[0], plane_sems.at[1], (peer, spot.z)).start()
        return carry

    def normalise(a, raw, full, gain):
        wait_bytes(raw.at[pl.ds(0, 8)], raw_sems.at[a, 3])
        scales = [row_scale(raw, core) for core in range(2)]
        for kk in range(2):
            place = spot.place(kk)
            for j in range(2):
                zb = 4 * c + 2 * kk + j
                rows = jnp.concatenate(
                    [raw[8 * core + zb].astype(F32) * scales[core] * gain[zb] for core in range(2)], axis=0
                )
                full[2 * c + kk, place, :, j * BLOCK : (j + 1) * BLOCK] = rows.astype(BF16)
        for core in range(2):
            scale_ref[a, core] = jnp.broadcast_to(scales[core], (8, 128))

    def both(gather, stage):
        for kk in range(2):
            gather.step(stage, kk)

    send_raw(0, layer_out, raw_out)
    lax.fori_loop(1, 32, plane_start, 0)
    send_raw(1, resid_mid, raw_mid)
    pass_raw(0, raw_out)
    normalise(0, raw_out, full_out, final_gain)
    both(gather_out, 0)
    pass_raw(1, raw_mid)
    both(gather_out, 1)
    normalise(1, raw_mid, full_mid, mlp_gain)
    both(gather_out, 2)
    both(gather_out, 3)
    both(gather_mid, 0)

    def products(left, right, out, core, kks=(0, 1)):
        for kk in kks:
            columns = slice_columns(kk, core)
            out[...] += contract_cols(left[:, columns], right[:, columns])

    for kk in range(2):
        lay_out(full_out, final_rows, kk, c)
    loads[0].wait()
    logits_ref[...] = jnp.zeros_like(logits_ref)
    products(final_rows, head, logits_ref, c)
    both(gather_mid, 1)
    both(gather_out, 4)
    for kk in range(2):
        lay_out(full_out, final_rows, kk, other)
    products(final_rows, head, logits_ref, other)
    both(gather_mid, 2)

    wait_bytes(got.at[pl.ds(0, 31)], plane_sems.at[1])
    logits = logits_ref[...]
    packed_rows = got[...].astype(F32).reshape(256, 512)
    teacher = packed_rows[:, :384]
    digits = packed_rows[:, 384:]
    local_max = jnp.max(logits, axis=1, keepdims=True)
    expd = jnp.exp(logits - local_max)
    total = jnp.sum(expd, axis=1, keepdims=True)
    moment = jnp.sum(expd * (logits - teacher), axis=1, keepdims=True)
    lanes = lax.broadcasted_iota(jnp.int32, (256, 128), 1)
    columns = jnp.where(lanes == 0, local_max, jnp.where(lanes == 1, total, moment))
    first[0] = jnp.transpose(columns)[0:4]
    for i in range(1, 16):
        remote(first.at[0], first.at[i], stat_sems.at[0], stat_sems.at[1], spot.column_peer(i)).start()
    both(gather_mid, 3)

    def combine(ref):
        top = ref[0, 0:1]
        for i in range(1, 16):
            top = jnp.maximum(top, ref[i, 0:1])
        total = jnp.zeros_like(top)
        moment = jnp.zeros_like(top)
        for i in range(16):
            weight = jnp.exp(ref[i, 0:1] - top)
            total = total + ref[i, 1:2] * weight
            moment = moment + ref[i, 2:3] * weight
        return jnp.concatenate([top, total, moment, moment], axis=0)

    wait_bytes(first.at[pl.ds(1, 15)], stat_sems.at[1])
    second[0] = combine(first)
    for i in range(1, 16):
        target = (wrap(spot.chip + i, CHIPS) * 2 + c, spot.z)
        remote(second.at[0], second.at[i], stat_sems.at[2], stat_sems.at[3], target).start()
    ids_all = (digits[:, 0:1] * 4096 + digits[:, 1:2] * 64 + digits[:, 2:3]).astype(jnp.int32)
    live_mask = digits[:, 3:4]
    token_weight = live_mask * (LOSS_SCALE / jnp.sum(live_mask, axis=0, keepdims=True))
    vocab_start = (spot.z * 32 + spot.d) * 384
    vocab = lax.broadcasted_iota(jnp.int32, (256, 384), 1)
    target = (ids_all - vocab_start == vocab).astype(F32)
    stats_pad[...] = jnp.zeros_like(stats_pad)
    wait_bytes(second.at[pl.ds(1, 15)], stat_sems.at[3])
    stats_pad[0:4] = combine(second)
    columns = jnp.transpose(stats_pad[...])
    global_max, totals, moments = columns[:, 0:1], columns[:, 1:2], columns[:, 2:3]
    probs_all = jnp.exp(logits - global_max) / totals
    dlogits = token_weight * (
        probs_all * (logits - teacher - moments / totals + CE_WEIGHT) - CE_WEIGHT * target
    )
    def turn(rows, out):
        for k in range(4):
            for chip in range(CHIPS):
                place = 16 * block_place(k, chip)
                out[k, place : place + 16, :] = rows[16 * chip : 16 * chip + 16]

    def spread(reduce, kk, core, half, left, right):
        k = 2 * core + kk
        rows = left[k, pl.ds(pl.multiple_of(half * 128, 128), 128)]
        part = jnp.dot(rows, right[:, slice_columns(kk, core)], preferred_element_type=F32).astype(BF16)
        reduce.partial[k, pl.ds(half * 8, 8)] = part.reshape(8, 16, SLICE)

    def send_partial(reduce, left, right):
        for sub in range(2):
            for kk in range(2):
                bit = spot.sib_bit(kk, 0)
                spread(reduce, kk, other, (1 - bit) if sub == 0 else bit, left, right)
                reduce.start(kk, sub)
        for sub in range(2):
            for kk in range(2):
                bit = spot.bit(kk, 0)
                spread(reduce, kk, c, (1 - bit) if sub == 0 else bit, left, right)

    dlog_b = dlogits.astype(BF16)
    turn(dlog_b, dlog_turned)
    dlog[...] = dlog_b

    def mid_rows(core):
        for kk in range(2):
            lay_out(full_mid, normed, kk, core)

    def mid_first():
        for load in loads[1:]:
            load.wait()
        gate_up_pre[...] = jnp.zeros_like(gate_up_pre)
        act_grad[...] = jnp.zeros_like(act_grad)
        mid_rows(c)
        products(w_gate_up, normed, gate_up_pre, c)

    def mid_second():
        both(gather_mid, 4)
        mid_rows(other)
        products(w_gate_up, normed, gate_up_pre, other)

    def activate():
        gate = gate_up_pre[0:64]
        activated_t[...] = (gate * jax.nn.sigmoid(gate) * gate_up_pre[64:128]).astype(BF16)

    def turn_dlog():
        dlog_t[...] = jnp.transpose(dlog[...].astype(F32)).astype(BF16)

    send_partial(reduces[0], dlog_turned, head)
    sums = reduces[0].plane({-1: [mid_first], 0: [mid_second], 1: [activate]})
    grad_out = reduces[0].column(sums, raw_out, final_gain, scale_ref[0, c][:, 0:1])
    own_b[...] = grad_out.astype(BF16)
    grad_first[...] = grad_out

    target_core = spot.half
    own_place = spot.z_low * 2 + c
    for zdst in range(8):
        mine = jnp.logical_and(spot.z == zdst, target_core == c)

        @pl.when(jnp.logical_not(mine))
        def _(zdst=zdst):
            target = (spot.chip * 2 + target_core, zdst)
            remote(own_b, own_from.at[own_place], own_sems.at[0], own_sems.at[1], target).start()

        @pl.when(mine)
        def _():
            own_from[own_place] = own_b[...]

    turn_dlog()
    wait_column(spot, own_from, own_sems.at[1])
    for kk in range(2):
        for j in range(2):
            zz = 2 * kk + j
            rows = jnp.concatenate([own_from[2 * zz + core].astype(F32) for core in range(2)], axis=0)
            full_grad[2 * c + kk, spot.place(kk), :, j * BLOCK : (j + 1) * BLOCK] = rows.astype(BF16)
        gather_grad.step(0, kk)
    for stage in range(1, 4):
        both(gather_grad, stage)
    for kk in range(2):
        lay_out(full_grad, grad_rows, kk, c)
    products(w_down, grad_rows, act_grad, c)
    both(gather_grad, 4)
    for kk in range(2):
        lay_out(full_grad, grad_rows, kk, other)
    products(w_down, grad_rows, act_grad, other)

    gate, up, act = gate_up_pre[0:64], gate_up_pre[64:128], act_grad[...]
    gate_sigmoid = jax.nn.sigmoid(gate)
    gate_grad = act * up * gate_sigmoid * (1.0 + gate * (1.0 - gate_sigmoid))
    both_grads = jnp.concatenate([gate_grad, act * gate * gate_sigmoid], axis=0)
    turn(jnp.transpose(both_grads).astype(BF16), hidden_turned)
    hidden_t[...] = both_grads.astype(BF16)
    send_partial(reduces[1], hidden_turned, w_gate_up)

    for a in range(2):
        wait_bytes(raw_out.at[pl.ds(0, 7)], raw_sems.at[a, 0])
        wait_bytes(raw_out.at[pl.ds(0, 8)], raw_sems.at[a, 2])
    wait_bytes(got.at[pl.ds(0, 31)], plane_sems.at[0])
    wait_bytes(first.at[pl.ds(1, 15)], stat_sems.at[0])
    wait_bytes(second.at[pl.ds(1, 15)], stat_sems.at[2])
    for gather in gathers:
        gather.finish()
    reduces[0].finish()
    wait_column(spot, own_from, own_sems.at[0])

    sums = reduces[1].plane()
    grad_second[...] = reduces[1].column(sums, raw_mid, mlp_gain, scale_ref[1, c][:, 0:1])
    reduces[1].finish()


def weight_grads(
    grad_first,
    grad_second,
    dlog_t,
    hidden_t,
    activated_t,
    final_rows,
    normed,
    grad_rows,
    grad_resid,
    grad_head,
    grad_gate,
    grad_up,
    grad_down,
    head_rows,
    gate_up_rows,
    down_rows,
    sems,
):
    def product(left, right):
        return jnp.dot(left, right, preferred_element_type=F32).astype(BF16)

    def store(src, dst, idx):
        copy = pltpu.make_async_copy(src, dst, sems.at[idx])
        copy.start()
        return copy

    grad_resid[...] = (grad_first[...] + grad_second[...]).astype(BF16)
    stores = []
    for k in range(4):
        columns = slice(k * SLICE, (k + 1) * SLICE)
        place = pl.ds(k * SLICE, SLICE)
        head_rows[:, columns] = product(dlog_t[...], final_rows[:, columns])
        stores.append(store(head_rows.at[:, place], grad_head.at[:, place], k))
    for k in range(4):
        columns = slice(k * SLICE, (k + 1) * SLICE)
        gate_up_rows[:, columns] = product(hidden_t[...], normed[:, columns])
    stores.append(store(gate_up_rows.at[pl.ds(0, 64)], grad_gate, 4))
    stores.append(store(gate_up_rows.at[pl.ds(64, 64)], grad_up, 5))
    for k in range(4):
        columns = slice(k * SLICE, (k + 1) * SLICE)
        down_rows[:, columns] = product(activated_t[...], grad_rows[:, columns])
    stores.append(store(down_rows, grad_down, 6))
    for copy in stores:
        copy.wait()


def shape(dims, dtype):
    return jax.ShapeDtypeStruct(dims, dtype)


def per_device(
    layer_out,
    resid_mid,
    final_gain,
    mlp_gain,
    head_weight,
    w_gate,
    w_up,
    w_down,
    teacher_logits,
    assign,
    lengths,
    token_ids,
):
    final_gain = final_gain.reshape(8, 1, BLOCK)
    mlp_gain = mlp_gain.reshape(8, 1, BLOCK)
    vmem = pl.BlockSpec(memory_space=pltpu.VMEM)
    smem = pl.BlockSpec(memory_space=pltpu.SMEM)
    hbm = pl.BlockSpec(memory_space=pl.ANY)
    full = pltpu.VMEM((4, 16, 16, SLICE), BF16)
    rows = pltpu.VMEM((256, D), BF16)
    dma = pltpu.SemaphoreType.DMA
    shared = pl.pallas_call(
        program,
        out_shape=[
            pltpu.VMEM((8, BLOCK), F32),
            pltpu.VMEM((8, BLOCK), F32),
            rows,
            rows,
            rows,
            pltpu.VMEM((384, 256), BF16),
            pltpu.VMEM((128, 256), BF16),
            pltpu.VMEM((64, 256), BF16),
        ],
        in_specs=[vmem] * 5 + [smem] * 3 + [hbm] * 4,
        out_specs=[vmem] * 8,
        scratch_shapes=[
            pltpu.VMEM((384, D), BF16),
            pltpu.VMEM((128, D), BF16),
            pltpu.VMEM((64, D), BF16),
            pltpu.VMEM((256, 384), BF16),
            pltpu.VMEM((4, 256, 384), BF16),
            pltpu.VMEM((4, 256, 128), BF16),
            pltpu.VMEM((16, 8, BLOCK), BF16),
            pltpu.VMEM((16, 8, BLOCK), BF16),
            full,
            full,
            full,
            pltpu.VMEM((32, 8, 512), BF16),
            pltpu.VMEM((32, 8, 512), BF16),
            pltpu.VMEM((256, 384), F32),
            pltpu.VMEM((128, 256), F32),
            pltpu.VMEM((64, 256), F32),
            pltpu.VMEM((16, 4, 256), F32),
            pltpu.VMEM((16, 4, 256), F32),
            pltpu.VMEM((128, 256), F32),
            pltpu.VMEM((8, BLOCK), BF16),
            pltpu.VMEM((8, 8, BLOCK), BF16),
            pltpu.VMEM((2, 2, 8, 128), F32),
            dma((4,)),
            dma((2, 4)),
            dma((2,)),
            dma((4,)),
            dma((2,)),
            dma((3, 2)),
            dma((3, 2, 8)),
            dma((3, 2)),
            dma((3, 2, 5)),
        ]
        + REDUCE_SCRATCH
        + REDUCE_SCRATCH,
        compiler_params=pltpu.CompilerParams(
            collective_id=0, has_side_effects=True, vmem_limit_bytes=VMEM_LIMIT
        ),
        name="backward",
    )(
        layer_out,
        resid_mid,
        final_gain,
        mlp_gain,
        teacher_logits,
        assign,
        lengths,
        token_ids,
        head_weight,
        w_gate,
        w_up,
        w_down,
    )
    return pl.pallas_call(
        weight_grads,
        out_shape=[
            shape((8, BLOCK), BF16),
            shape(head_weight.shape, BF16),
            shape(w_gate.shape, BF16),
            shape(w_up.shape, BF16),
            shape(w_down.shape, BF16),
        ],
        in_specs=[vmem] * 8,
        out_specs=[vmem] + [hbm] * 4,
        scratch_shapes=[
            pltpu.VMEM((384, D), BF16),
            pltpu.VMEM((128, D), BF16),
            pltpu.VMEM((64, D), BF16),
            dma((7,)),
        ],
        compiler_params=pltpu.CompilerParams(vmem_limit_bytes=GRADS_VMEM),
        cost_estimate=pl.CostEstimate(flops=2 * 256 * 576 * D, bytes_accessed=2 * 576 * D, transcendentals=0),
        name="weight_grads",
    )(shared[0], shared[1], shared[5], shared[6], shared[7], shared[2], shared[3], shared[4])


def solution(mesh):
    return jax.shard_map(
        per_device,
        mesh=mesh,
        in_specs=(
            P("dp", "tensor"),
            P("dp", "tensor"),
            P(),
            P(),
            P(("tensor", "dp"), None),
            P(("tensor", "dp"), None),
            P(("tensor", "dp"), None),
            P(("tensor", "dp"), None),
            P("dp", "tensor"),
            P("dp", None),
            P("dp", None),
            P("dp"),
        ),
        out_specs=(
            P("dp", "tensor"),
            P(("tensor", "dp"), None),
            P(("tensor", "dp"), None),
            P(("tensor", "dp"), None),
            P(("tensor", "dp"), None),
        ),
        check_vma=False,
    )
```

```python
import jax
import jax.numpy as jnp
from jax import lax
from jax.experimental import pallas as pl
from jax.experimental.pallas import tpu as pltpu
from jax.sharding import PartitionSpec as P

D = 5120
SLOT = 4
EPS = 1e-06
CE_WEIGHT = 0.5
LOSS_SCALE = 4096.0

BLOCK = 640
SLICE = 1280
CHIPS = 16
F32 = jnp.float32
BF16 = jnp.bfloat16
VMEM_LIMIT = 52 * 1024 * 1024
GRADS_VMEM = 20 * 1024 * 1024


def contract_cols(left, right):
    return lax.dot_general(left, right, (((1,), (1,)), ((), ())), preferred_element_type=F32)


def wrap(v, size):
    return jnp.where(v >= size, v - size, v)


def ring_bits(v):
    high = v // 2
    return v % 2 + high - 2 * (v % 2) * high, high


class Spot:
    def __init__(self):
        self.d = lax.axis_index("dp")
        self.z = lax.axis_index("tensor")
        self.chip = lax.div(self.d, 2)
        self.c = self.d - 2 * self.chip
        self.y = lax.div(self.chip, 4)
        self.x = self.chip - 4 * self.y
        c, other = self.c, 1 - self.c
        xv, yv = lax.div(self.x, 2), lax.div(self.y, 2)
        x_low, y_low = self.x - 2 * xv, self.y - 2 * yv
        xu, yu = x_low + xv - 2 * x_low * xv, y_low + yv - 2 * y_low * yv
        x_near, y_near = self.x + 1 - 2 * x_low, self.y + 1 - 2 * y_low
        x_far, y_far = 3 - self.x, 3 - self.y
        self.half = lax.div(self.z, 4)
        self.z_low = self.z - 4 * self.half
        bits = (xu, yu, xv, yv)
        moved = (x_near, y_near, x_far, y_far)
        self.own_bits = [bits[i] * other + bits[(i + 2) % 4] * c for i in range(4)]
        self.sib_bits = [bits[i] * c + bits[(i + 2) % 4] * other for i in range(4)]
        moved = [moved[i] * other + moved[(i + 2) % 4] * c for i in range(4)]
        self.chips = [self.y * 4 + moved[i] if i % 2 == 0 else moved[i] * 4 + self.x for i in range(4)]
        corner = []
        for i in range(4):
            j = (i + 1) % 4
            corner.append(moved[j] * 4 + moved[i] if i % 2 == 0 else moved[i] * 4 + moved[j])
        self.corners = corner

    def pick(self, values, kk, s):
        first, second = values[s % 4], values[(s + 1) % 4]
        return first + (second - first) * kk

    def bit(self, kk, s):
        return self.pick(self.own_bits, kk, s)

    def sib_bit(self, kk, s):
        return self.pick(self.sib_bits, kk, s)

    def base(self, kk, s):
        return sum((self.bit(kk, i) * (8 >> i) for i in range(s)), jnp.int32(0))

    def sib_base(self, kk, s):
        return sum((self.sib_bit(kk, i) * (8 >> i) for i in range(s)), jnp.int32(0))

    def place(self, kk):
        return self.base(kk, 4)

    def partner(self, kk, s):
        return (self.pick(self.chips, kk, s) * 2 + self.c, self.z)

    def diagonal(self, kk, s):
        return (self.pick(self.corners, kk, s) * 2 + self.c, self.z)

    def sibling(self):
        return (self.chip * 2 + 1 - self.c, self.z)

    def column_peer(self, up, flip=0):
        core = self.c if flip == 0 else 1 - self.c
        return (self.chip * 2 + core, wrap(self.z + up, 8))


def greet(spot):
    barrier = pltpu.get_barrier_semaphore()
    mesh = pl.DeviceIdType.MESH
    pl.semaphore_signal(barrier, inc=1, device_id=spot.sibling(), device_id_type=mesh)

    def column(up, carry):
        for flip in range(2):
            pl.semaphore_signal(barrier, inc=1, device_id=spot.column_peer(up, flip), device_id_type=mesh)
        return carry

    lax.fori_loop(1, 8, column, 0)

    def body(j, carry):
        chip = wrap(spot.chip + j, CHIPS)
        for core in range(2):
            pl.semaphore_signal(
                barrier, inc=1, device_id=(chip * 2 + core, spot.z), device_id_type=pl.DeviceIdType.MESH
            )
        return carry

    lax.fori_loop(1, CHIPS, body, 0)


def greeted():
    pl.semaphore_wait(pltpu.get_barrier_semaphore(), 45)


def remote(src, dst, send_sem, recv_sem, target):
    return pltpu.make_async_remote_copy(
        src_ref=src,
        dst_ref=dst,
        send_sem=send_sem,
        recv_sem=recv_sem,
        device_id=target,
        device_id_type=pl.DeviceIdType.MESH,
    )


def row_scale(raw, core):
    total = jnp.zeros((8, BLOCK), F32)
    for zb in range(8):
        part = raw[8 * core + zb].astype(F32)
        total = total + part * part
    return lax.rsqrt(jnp.sum(total, axis=1, keepdims=True) / D + EPS)


def loop(start, stop, body):
    def step(i, carry):
        body(i)
        return carry

    lax.fori_loop(start, stop, step, 0)


def wait_bytes(ref, sem):
    pltpu.make_async_copy(ref, ref, sem).wait()


class Gather:
    def __init__(self, spot, full, xy_send, xy_recv, sib_send, sib_recv):
        self.spot, self.full = spot, full
        self.xy_send, self.xy_recv, self.sib_send, self.sib_recv = xy_send, xy_recv, sib_send, sib_recv

    def view(self, kk, off, n, core=None):
        core = self.spot.c if core is None else core
        return self.full.at[2 * core + kk, pl.ds(off, n)]

    def send(self, kk, target, idx, off, n):
        view = self.view(kk, off, n)
        remote(view, view, self.xy_send.at[kk], self.xy_recv.at[kk, idx], target).start()

    def arrived(self, kk, idx, off, n):
        wait_bytes(self.view(kk, off, n), self.xy_recv.at[kk, idx])

    def pass_on(self, kk, idx, off, n):
        view = self.view(kk, off, n)
        remote(view, view, self.sib_send.at[kk], self.sib_recv.at[kk, idx], self.spot.sibling()).start()

    def step(self, stage, kk):
        spot = self.spot
        flip = [(8 >> s) * (1 - 2 * spot.bit(kk, s)) for s in range(4)]
        own, four = spot.place(kk), spot.base(kk, 2)
        if stage == 0:
            self.send(kk, spot.diagonal(kk, 2), 2, own, 1)
            self.send(kk, spot.partner(kk, 3), 0, own, 1)
            self.send(kk, spot.partner(kk, 2), 1, own, 1)
        elif stage == 1:
            self.arrived(kk, 0, own + flip[3], 1)
            self.arrived(kk, 1, own + flip[2], 1)
            self.arrived(kk, 2, own + flip[2] + flip[3], 1)
            self.send(kk, spot.partner(kk, 1), 3, four, 2)
            self.send(kk, spot.partner(kk, 1), 4, four + 2, 2)
            self.send(kk, spot.partner(kk, 0), 5, four, 4)
            self.pass_on(kk, 0, four, 4)
        elif stage == 2:
            new = four + flip[1]
            for i in range(2):
                self.arrived(kk, 3 + i, new + 2 * i, 2)
                self.send(kk, spot.partner(kk, 0), 6 + i, new + 2 * i, 2)
            self.pass_on(kk, 1, new, 4)
        elif stage == 3:
            new = four + flip[0]
            self.arrived(kk, 5, new, 4)
            self.pass_on(kk, 2, new, 4)
            new = new + flip[1]
            for i in range(2):
                self.arrived(kk, 6 + i, new + 2 * i, 2)
                self.pass_on(kk, 3 + i, new + 2 * i, 2)
        else:
            other = 1 - spot.c
            four = spot.sib_base(kk, 2)
            over_1 = four + 4 * (1 - 2 * spot.sib_bit(kk, 1))
            over_0 = 8 * (1 - 2 * spot.sib_bit(kk, 0))
            last = over_1 + over_0
            pieces = ((four, 4), (over_1, 4), (four + over_0, 4), (last, 2), (last + 2, 2))
            for idx, (off, n) in enumerate(pieces):
                wait_bytes(self.view(kk, off, n, other), self.sib_recv.at[kk, idx])

    def finish(self):
        for kk in range(2):
            wait_bytes(self.full.at[kk, pl.ds(0, 15)], self.xy_send.at[kk])
            wait_bytes(self.full.at[kk], self.sib_send.at[kk])


def block_place(k, chip):
    xu, xv = ring_bits(chip % 4)
    yu, yv = ring_bits(chip // 4)
    bits = (xu, yu, xv, yv)
    return sum(bits[(k + s) % 4] * (8 >> s) for s in range(4))


def slice_columns(kk, core):
    return pl.ds(pl.multiple_of((2 * core + kk) * SLICE, SLICE), SLICE)


def lay_out(full, out, kk, core):
    along_x = []
    for x in range(4):
        low, high = block_place(kk, x), block_place(2 + kk, x)
        along_x.append(low + (high - low) * core)

    def row(y):
        yv = jnp.where(y >= 2, 1, 0)
        y_low = y - 2 * yv
        yu = y_low + yv - 2 * y_low * yv
        weights = [(8 >> ((1 - k) % 4), 8 >> ((3 - k) % 4)) for k in (kk, 2 + kk)]
        place_u = weights[0][0] + (weights[1][0] - weights[0][0]) * core
        place_v = weights[0][1] + (weights[1][1] - weights[0][1]) * core
        along_y = yu * place_u + yv * place_v
        for x in range(4):
            rows = pl.ds(pl.multiple_of(64 * y + 16 * x, 16), 16)
            out[rows, slice_columns(kk, core)] = full[2 * core + kk, along_y + along_x[x]]

    loop(0, 4, row)


REDUCE_SCRATCH = [
    pltpu.VMEM((4, 16, 16, SLICE), BF16),
    pltpu.VMEM((2, 16, 16, SLICE), BF16),
    pltpu.VMEM((2, 15, 16, SLICE), BF16),
    pltpu.VMEM((8, 8, BLOCK), BF16),
    pltpu.VMEM((8, 8, BLOCK), BF16),
    pltpu.VMEM((2, 1, 128), F32),
    pltpu.VMEM((9, 1, 128), F32),
    pltpu.SemaphoreType.DMA((2,)),
    pltpu.SemaphoreType.DMA((2, 2)),
    pltpu.SemaphoreType.DMA((2,)),
    pltpu.SemaphoreType.DMA((2, 7)),
    pltpu.SemaphoreType.DMA((6,)),
]


class Reduce:
    def __init__(self, spot, scratch):
        self.spot = spot
        (
            self.partial,
            self.from_sib,
            self.from_xy,
            self.to_col,
            self.from_col,
            self.inner_to,
            self.inner_from,
            self.sib_send,
            self.sib_recv,
            self.xy_send,
            self.xy_recv,
            self.col_sems,
        ) = scratch

    def sib_copy(self, kk, sub, core, bit):
        half = (1 - sub) * (1 - bit) + sub * bit
        return remote(
            self.partial.at[2 * core + kk, pl.ds(half * 8, 8)],
            self.from_sib.at[kk, pl.ds(half * 8, 8)],
            self.sib_send.at[kk],
            self.sib_recv.at[kk, sub],
            self.spot.sibling(),
        )

    def start(self, kk, sub):
        self.sib_copy(kk, sub, 1 - self.spot.c, self.spot.sib_bit(kk, 0)).start()

    def from_sibling(self, kk, sub):
        self.sib_copy(kk, sub, self.spot.c, self.spot.bit(kk, 0)).wait_recv()

    def add(self, kk, off, ref, ref_off, n):
        k = 2 * self.spot.c + kk

        def body(i, carry):
            self.partial[k, off + i] = self.partial[k, off + i] + ref[kk, ref_off + i]
            return carry

        if n == 1:
            body(0, 0)
        else:
            lax.fori_loop(0, n, body, 0)

    def plan(self, kk, s):
        n = 8 >> s
        landing = 16 - 2 * n
        bit = self.spot.bit(kk, s)
        gone = self.spot.base(kk, s) + (1 - bit) * n
        kept = self.spot.base(kk, s) + bit * n
        half = n // 2
        after = self.spot.bit(kk, s + 1)
        pieces = []
        for sub in range(2):
            shift = ((1 - after) if sub == 0 else after) * half
            pieces.append((gone + shift, kept + shift, landing + sub * half, half, 2 * s + sub))
        return pieces

    def xy_copy(self, kk, s, piece):
        gone, _, landing, n, idx = piece
        return remote(
            self.partial.at[2 * self.spot.c + kk, pl.ds(gone, n)],
            self.from_xy.at[kk, pl.ds(landing, n)],
            self.xy_send.at[kk],
            self.xy_recv.at[kk, idx],
            self.spot.partner(kk, s),
        )

    def xy_start(self, kk, s, piece):
        self.xy_copy(kk, s, piece).start()

    def plane(self, beside=None):
        beside = beside or {}
        spot = self.spot

        def first(kk):
            self.from_sibling(kk, 0)
            for piece in self.plan(kk, 0):
                self.add(kk, piece[0], self.from_sib, piece[0], piece[3])
                self.xy_start(kk, 0, piece)

        def kept(kk):
            self.from_sibling(kk, 1)
            self.add(kk, spot.bit(kk, 0) * 8, self.from_sib, spot.bit(kk, 0) * 8, 8)

        def arrive(kk, s, sub):
            piece = self.plan(kk, s)[sub]
            self.xy_copy(kk, s, piece).wait_recv()
            self.add(kk, piece[1], self.from_xy, piece[2], piece[3])

        def second(kk):
            arrive(kk, 0, 0)
            for follow in self.plan(kk, 1):
                self.xy_start(kk, 1, follow)

        def third(kk):
            arrive(kk, 1, 0)
            by_2 = spot.place(kk) + 2 * (1 - 2 * spot.bit(kk, 2))
            self.tail_copy(kk, by_2 + 1 - 2 * spot.bit(kk, 3), 2, spot.diagonal(kk, 2)).start()
            self.tail_copy(kk, by_2, 0, spot.partner(kk, 2)).start()

        def fourth(kk):
            arrive(kk, 1, 1)
            own = spot.place(kk)
            self.tail_copy(kk, own + 1 - 2 * spot.bit(kk, 3), 1, spot.partner(kk, 3)).start()

        loop(0, 2, first)
        loop(0, 2, kept)
        for work in beside.get(-1, ()):
            work()
        loop(0, 2, second)
        loop(0, 2, lambda kk: arrive(kk, 0, 1))
        for work in beside.get(0, ()):
            work()
        loop(0, 2, third)
        loop(0, 2, fourth)
        for work in beside.get(1, ()):
            work()
        places = [spot.place(kk) for kk in range(2)]
        sums = []
        for kk in range(2):
            total = self.partial[2 * spot.c + kk, places[kk]].astype(F32)
            for i in range(3):
                self.tail_copy(kk, places[kk], i, spot.sibling()).wait_recv()
                total = total + self.from_xy[kk, 12 + i].astype(F32)
            sums.append(total)
        return sums

    def tail_copy(self, kk, block, i, target):
        return remote(
            self.partial.at[2 * self.spot.c + kk, pl.ds(block, 1)],
            self.from_xy.at[kk, pl.ds(12 + i, 1)],
            self.xy_send.at[kk],
            self.xy_recv.at[kk, 4 + i],
            target,
        )

    def column(self, sums, raw, gain, scale, beside=()):
        spot = self.spot
        for kk in range(2):
            for j in range(2):
                for core in range(2):
                    part = sums[kk][8 * core : 8 * core + 8, j * BLOCK : (j + 1) * BLOCK]
                    self.to_col[2 * (2 * kk + j) + core] = part.astype(BF16)

        def to_column(zz):
            zdst = 4 * spot.c + zz
            for core in range(2):
                mine = jnp.logical_and(zdst == spot.z, spot.c == core)

                @pl.when(jnp.logical_not(mine))
                def _(core=core):
                    remote(
                        self.to_col.at[2 * zz + core],
                        self.from_col.at[spot.z],
                        self.col_sems.at[0],
                        self.col_sems.at[1],
                        (spot.chip * 2 + core, zdst),
                    ).start()

                @pl.when(mine)
                def _(core=core):
                    self.from_col[spot.z] = self.to_col[2 * zz + core]

        loop(0, 4, to_column)
        row = lax.broadcasted_iota(jnp.int32, (8, 128), 0)
        diagonal = row == lax.broadcasted_iota(jnp.int32, (8, 128), 1)
        for core in range(2):
            total = jnp.zeros((8, BLOCK), F32)
            for kk in range(2):
                for j in range(2):
                    zb = 4 * spot.c + 2 * kk + j
                    part = sums[kk][8 * core : 8 * core + 8, j * BLOCK : (j + 1) * BLOCK]
                    total = total + raw[8 * core + zb].astype(F32) * gain[zb] * part
            inner = jnp.where(diagonal, jnp.sum(total, axis=1, keepdims=True), 0.0)
            self.inner_to[core] = jnp.sum(inner, axis=0, keepdims=True)
        to_sibling = remote(
            self.inner_to.at[1 - spot.c],
            self.inner_from.at[8],
            self.col_sems.at[4],
            self.col_sems.at[5],
            spot.sibling(),
        )
        to_sibling.start()
        to_sibling.wait_recv()
        self.inner_from[0] = self.inner_to[spot.c] + self.inner_from[8]
        loop(
            1,
            8,
            lambda up: remote(
                self.inner_from.at[0],
                self.inner_from.at[up],
                self.col_sems.at[2],
                self.col_sems.at[3],
                spot.column_peer(up),
            ).start(),
        )
        for work in beside:
            work()
        own = raw[8 * spot.c + spot.z].astype(F32)
        own_gain = gain[spot.z]
        wait_column(spot, self.from_col, self.col_sems.at[1])
        grad = jnp.zeros((8, BLOCK), F32)
        for zsrc in range(8):
            grad = grad + self.from_col[zsrc].astype(F32)
        wait_bytes(self.inner_from.at[pl.ds(1, 7)], self.col_sems.at[3])
        inner = jnp.zeros((1, 128), F32)
        for i in range(8):
            inner = inner + self.inner_from[i]
        inner = jnp.sum(jnp.where(diagonal, inner, 0.0), axis=1, keepdims=True) / D
        return scale * own_gain * grad - own * (scale * scale * scale) * inner

    def finish(self):
        for kk in range(2):
            wait_bytes(self.partial.at[kk], self.sib_send.at[kk])
            wait_bytes(self.partial.at[kk, pl.ds(0, 15)], self.xy_send.at[kk])
        wait_column(self.spot, self.to_col, self.col_sems.at[0])
        wait_bytes(self.inner_from.at[pl.ds(1, 7)], self.col_sems.at[2])
        wait_bytes(self.inner_from.at[pl.ds(8, 1)], self.col_sems.at[4])


def wait_column(spot, ref, sem):
    own = spot.half == spot.c

    @pl.when(own)
    def _():
        wait_bytes(ref.at[pl.ds(0, 7)], sem)

    @pl.when(jnp.logical_not(own))
    def _():
        wait_bytes(ref, sem)


def program(
    layer_out,
    resid_mid,
    final_gain,
    mlp_gain,
    teacher_in,
    assign,
    lengths,
    token_ids,
    head_hbm,
    gate_hbm,
    up_hbm,
    down_hbm,
    grad_first,
    grad_second,
    final_rows,
    normed,
    grad_rows,
    dlog_t,
    hidden_t,
    activated_t,
    head,
    w_gate_up,
    w_down,
    dlog,
    dlog_turned,
    hidden_turned,
    raw_out,
    raw_mid,
    full_out,
    full_mid,
    full_grad,
    packed,
    got,
    logits_ref,
    diff_ref,
    gate_up_pre,
    act_grad,
    first,
    second,
    stats_pad,
    own_b,
    own_from,
    scale_ref,
    load_sem,
    raw_sems,
    plane_sems,
    stat_sems,
    own_sems,
    xy_send,
    xy_recv,
    sib_send,
    sib_recv,
    *scratch,
):
    spot = Spot()
    c, other = spot.c, 1 - spot.c
    loads = [
        pltpu.make_async_copy(src, dst, load_sem.at[i])
        for i, (src, dst) in enumerate(
            (
                (head_hbm, head),
                (gate_hbm, w_gate_up.at[pl.ds(0, 64)]),
                (up_hbm, w_gate_up.at[pl.ds(64, 64)]),
                (down_hbm, w_down),
            )
        )
    ]
    for load in loads:
        load.start()
    reduces = [Reduce(spot, scratch[: len(REDUCE_SCRATCH)]), Reduce(spot, scratch[len(REDUCE_SCRATCH) :])]
    gathers = [
        Gather(spot, full, xy_send.at[a], xy_recv.at[a], sib_send.at[a], sib_recv.at[a])
        for a, full in enumerate((full_out, full_mid, full_grad))
    ]
    gather_out, gather_mid, gather_grad = gathers

    greet(spot)
    mine = 8 * c + spot.z
    raw_out[mine] = layer_out[...]
    raw_mid[mine] = resid_mid[...]

    row = lax.broadcasted_iota(jnp.int32, (8, 1), 0)
    order = jnp.zeros((8, 1), jnp.int32)
    for r in range(8):
        order = jnp.where(row == r, assign[0, r], order)

    def pack(peer):
        rows = teacher_in[:, pl.ds(pl.multiple_of(peer * 384, 384), 384)].astype(F32)
        picked = jnp.zeros((8, 384), F32)
        for r in range(8):
            picked = picked + jnp.where(order == r, rows[r : r + 1, :], 0.0)
        packed[peer] = picked.astype(BF16)

    loop(0, 32, pack)
    got[spot.d] = packed[spot.d]

    token = lax.broadcasted_iota(jnp.int32, (1, 256), 1)
    own_ids = jnp.full((1, 256), -1, jnp.int32)
    own_lengths = jnp.zeros((1, 256), jnp.int32)
    for r in range(8):
        here = token == 8 * spot.d + r
        own_ids = jnp.where(here, token_ids[r], own_ids)
        own_lengths = jnp.where(here, lengths[0, r // SLOT], own_lengths)
    live = (lax.rem(token, SLOT) < own_lengths).astype(jnp.int32)
    codes = jnp.where(own_ids >= 0, 2 * own_ids + live, 0).astype(F32)
    greeted()

    def send_raw(a, own, raw):
        loop(
            1,
            8,
            lambda up: remote(
                own, raw.at[mine], raw_sems.at[a, 0], raw_sems.at[a, 1], spot.column_peer(up)
            ).start(),
        )

    def pass_raw(a, raw):
        wait_bytes(raw.at[pl.ds(0, 7)], raw_sems.at[a, 1])
        rows = raw.at[pl.ds(8 * c, 8)]
        remote(rows, rows, raw_sems.at[a, 2], raw_sems.at[a, 3], spot.sibling()).start()

    def plane_start(i, carry):
        peer = wrap(spot.d + i, 32)
        remote(packed.at[peer], got.at[spot.d], plane_sems.at[0], plane_sems.at[1], (peer, spot.z)).start()
        return carry

    def normalise(a, raw, full, gain):
        wait_bytes(raw.at[pl.ds(0, 8)], raw_sems.at[a, 3])
        scales = [row_scale(raw, core) for core in range(2)]
        for kk in range(2):
            place = spot.place(kk)
            for j in range(2):
                zb = 4 * c + 2 * kk + j
                rows = jnp.concatenate(
                    [raw[8 * core + zb].astype(F32) * scales[core] * gain[zb] for core in range(2)], axis=0
                )
                full[2 * c + kk, place, :, j * BLOCK : (j + 1) * BLOCK] = rows.astype(BF16)
        for core in range(2):
            scale_ref[a, core] = jnp.broadcast_to(scales[core], (8, 128))

    def both(gather, stage):
        loop(0, 2, lambda kk: gather.step(stage, kk))

    send_raw(0, layer_out, raw_out)
    lax.fori_loop(1, 32, plane_start, 0)
    send_raw(1, resid_mid, raw_mid)
    pass_raw(0, raw_out)
    normalise(0, raw_out, full_out, final_gain)
    both(gather_out, 0)
    pass_raw(1, raw_mid)
    both(gather_out, 1)
    normalise(1, raw_mid, full_mid, mlp_gain)
    both(gather_out, 2)
    both(gather_out, 3)
    both(gather_mid, 0)

    def products(left, right, out, core):
        def body(kk):
            columns = slice_columns(kk, core)
            out[...] += contract_cols(left[:, columns], right[:, columns])

        loop(0, 2, body)

    for kk in range(2):
        lay_out(full_out, final_rows, kk, c)
    loads[0].wait()
    logits_ref[...] = jnp.zeros_like(logits_ref)
    products(final_rows, head, logits_ref, c)
    both(gather_mid, 1)
    both(gather_out, 4)
    for kk in range(2):
        lay_out(full_out, final_rows, kk, other)
    products(final_rows, head, logits_ref, other)
    both(gather_mid, 2)

    wait_bytes(got.at[pl.ds(0, 31)], plane_sems.at[1])
    logits = logits_ref[...]
    diff = logits - got[...].astype(F32).reshape(256, 384)
    local_max = jnp.max(logits, axis=1, keepdims=True)
    expd = jnp.exp(logits - local_max)
    total = jnp.sum(expd, axis=1, keepdims=True)
    moment = jnp.sum(expd * diff, axis=1, keepdims=True)
    logits_ref[...] = expd
    diff_ref[...] = diff
    lanes = lax.broadcasted_iota(jnp.int32, (256, 128), 1)
    columns = jnp.where(lanes == 0, local_max, jnp.where(lanes == 1, total, moment))
    first[0] = jnp.transpose(columns)[0:4]
    first[0, 3:4] = codes
    remote(first.at[0], first.at[1], stat_sems.at[0], stat_sems.at[1], spot.sibling()).start()

    def to_column(up):
        for flip in range(2):
            target = spot.column_peer(up, flip)
            remote(first.at[0], first.at[2 * up + flip], stat_sems.at[0], stat_sems.at[1], target).start()

    loop(1, 8, to_column)
    both(gather_mid, 3)

    def combine(ref, groups):
        top = ref[0, 0:1]
        for i in range(1, 16):
            top = jnp.maximum(top, ref[i, 0:1])
        total = jnp.zeros_like(top)
        moment = jnp.zeros_like(top)
        for i in range(16):
            weight = jnp.exp(ref[i, 0:1] - top)
            total = total + ref[i, 1:2] * weight
            moment = moment + ref[i, 2:3] * weight
        return jnp.concatenate([top, total, moment, sum(ref[i, 3:4] for i in range(groups))], axis=0)

    wait_bytes(first.at[pl.ds(1, 15)], stat_sems.at[1])
    second[0] = combine(first, 2)

    def to_plane(i):
        target = (wrap(spot.chip + i, CHIPS) * 2 + c, spot.z)
        remote(second.at[0], second.at[i], stat_sems.at[2], stat_sems.at[3], target).start()

    loop(1, CHIPS, to_plane)
    vocab = lax.broadcasted_iota(jnp.int32, (256, 384), 1) + (spot.z * 32 + spot.d) * 384
    stats_pad[...] = jnp.zeros_like(stats_pad)
    wait_bytes(second.at[pl.ds(1, 15)], stat_sems.at[3])
    stats_pad[0:4] = combine(second, 16)
    columns = jnp.transpose(stats_pad[...])
    global_max, totals, moments = columns[:, 0:1], columns[:, 1:2], columns[:, 2:3]
    code = columns[:, 3:4].astype(jnp.int32)
    ids_all = code >> 1
    live_mask = (code - 2 * ids_all).astype(F32)
    token_weight = live_mask * (LOSS_SCALE / jnp.sum(live_mask, axis=0, keepdims=True))
    share = token_weight * (jnp.exp(local_max - global_max) / totals)
    shift = CE_WEIGHT - moments / totals
    dlogits = share * logits_ref[...] * (diff_ref[...] + shift)
    dlogits = dlogits - jnp.where(ids_all == vocab, CE_WEIGHT * token_weight, 0.0)

    def turn(rows, out):
        for k in range(4):
            for chip in range(CHIPS):
                place = 16 * block_place(k, chip)
                out[k, place : place + 16, :] = rows[16 * chip : 16 * chip + 16]

    def spread(reduce, kk, core, half, left, right):
        k = 2 * core + kk
        rows = left[k, pl.ds(pl.multiple_of(half * 128, 128), 128)]
        part = jnp.dot(rows, right[:, slice_columns(kk, core)], preferred_element_type=F32).astype(BF16)
        reduce.partial[k, pl.ds(half * 8, 8)] = part.reshape(8, 16, SLICE)

    def send_partial(reduce, left, right):

        def to_sibling(i):
            sub = jnp.where(i >= 2, 1, 0)
            kk = i - 2 * sub
            bit = spot.sib_bit(kk, 0)
            spread(reduce, kk, other, (1 - sub) * (1 - bit) + sub * bit, left, right)
            reduce.start(kk, sub)

        def to_self(i):
            sub = jnp.where(i >= 2, 1, 0)
            kk = i - 2 * sub
            bit = spot.bit(kk, 0)
            spread(reduce, kk, c, (1 - sub) * (1 - bit) + sub * bit, left, right)

        loop(0, 4, to_sibling)
        loop(0, 4, to_self)

    dlog_b = dlogits.astype(BF16)
    turn(dlog_b, dlog_turned)
    dlog[...] = dlog_b

    def mid_rows(core):
        for kk in range(2):
            lay_out(full_mid, normed, kk, core)

    def mid_first():
        for load in loads[1:]:
            load.wait()
        gate_up_pre[...] = jnp.zeros_like(gate_up_pre)
        act_grad[...] = jnp.zeros_like(act_grad)
        mid_rows(c)
        products(w_gate_up, normed, gate_up_pre, c)

    def mid_second():
        both(gather_mid, 4)
        mid_rows(other)
        products(w_gate_up, normed, gate_up_pre, other)

    def activate():
        gate = gate_up_pre[0:64]
        activated_t[...] = (gate * jax.nn.sigmoid(gate) * gate_up_pre[64:128]).astype(BF16)

    def turn_dlog():
        dlog_t[...] = jnp.transpose(dlog[...].astype(F32)).astype(BF16)

    send_partial(reduces[0], dlog_turned, head)
    sums = reduces[0].plane({-1: [mid_first], 0: [mid_second], 1: [activate]})
    grad_out = reduces[0].column(sums, raw_out, final_gain, scale_ref[0, c][:, 0:1])
    own_b[...] = grad_out.astype(BF16)
    grad_first[...] = grad_out

    target_core = spot.half
    own_place = spot.z_low * 2 + c

    def own_to_column(zdst):
        mine = jnp.logical_and(spot.z == zdst, target_core == c)

        @pl.when(jnp.logical_not(mine))
        def _():
            target = (spot.chip * 2 + target_core, zdst)
            remote(own_b, own_from.at[own_place], own_sems.at[0], own_sems.at[1], target).start()

        @pl.when(mine)
        def _():
            own_from[own_place] = own_b[...]

    loop(0, 8, own_to_column)
    turn_dlog()
    wait_column(spot, own_from, own_sems.at[1])
    for kk in range(2):
        for j in range(2):
            zz = 2 * kk + j
            rows = jnp.concatenate([own_from[2 * zz + core].astype(F32) for core in range(2)], axis=0)
            full_grad[2 * c + kk, spot.place(kk), :, j * BLOCK : (j + 1) * BLOCK] = rows.astype(BF16)
    both(gather_grad, 0)
    for stage in range(1, 4):
        both(gather_grad, stage)
    for kk in range(2):
        lay_out(full_grad, grad_rows, kk, c)
    products(w_down, grad_rows, act_grad, c)
    both(gather_grad, 4)
    for kk in range(2):
        lay_out(full_grad, grad_rows, kk, other)
    products(w_down, grad_rows, act_grad, other)

    gate, up, act = gate_up_pre[0:64], gate_up_pre[64:128], act_grad[...]
    gate_sigmoid = jax.nn.sigmoid(gate)
    gate_grad = act * up * gate_sigmoid * (1.0 + gate * (1.0 - gate_sigmoid))
    both_grads = jnp.concatenate([gate_grad, act * gate * gate_sigmoid], axis=0)
    turn(jnp.transpose(both_grads).astype(BF16), hidden_turned)
    hidden_t[...] = both_grads.astype(BF16)
    send_partial(reduces[1], hidden_turned, w_gate_up)

    for a in range(2):
        wait_bytes(raw_out.at[pl.ds(0, 7)], raw_sems.at[a, 0])
        wait_bytes(raw_out.at[pl.ds(0, 8)], raw_sems.at[a, 2])
    wait_bytes(got.at[pl.ds(0, 31)], plane_sems.at[0])
    wait_bytes(first.at[pl.ds(1, 15)], stat_sems.at[0])
    wait_bytes(second.at[pl.ds(1, 15)], stat_sems.at[2])
    for gather in gathers:
        gather.finish()
    reduces[0].finish()
    wait_column(spot, own_from, own_sems.at[0])

    sums = reduces[1].plane()
    grad_second[...] = reduces[1].column(sums, raw_mid, mlp_gain, scale_ref[1, c][:, 0:1])
    reduces[1].finish()


def weight_grads(
    grad_first,
    grad_second,
    dlog_t,
    hidden_t,
    activated_t,
    final_rows,
    normed,
    grad_rows,
    grad_resid,
    grad_head,
    grad_gate,
    grad_up,
    grad_down,
    head_rows,
    gate_up_rows,
    down_rows,
    sems,
):
    def product(left, right):
        return jnp.dot(left, right, preferred_element_type=F32).astype(BF16)

    grad_resid[...] = (grad_first[...] + grad_second[...]).astype(BF16)

    def copies(k):
        place = pl.ds(pl.multiple_of(k * SLICE, SLICE), SLICE)
        return [
            pltpu.make_async_copy(head_rows.at[:, place], grad_head.at[:, place], sems.at[0, k]),
            pltpu.make_async_copy(gate_up_rows.at[pl.ds(0, 64), place], grad_gate.at[:, place], sems.at[1, k]),
            pltpu.make_async_copy(gate_up_rows.at[pl.ds(64, 64), place], grad_up.at[:, place], sems.at[2, k]),
            pltpu.make_async_copy(down_rows.at[:, place], grad_down.at[:, place], sems.at[3, k]),
        ]

    def chunk(k):
        place = pl.ds(pl.multiple_of(k * SLICE, SLICE), SLICE)
        to_head, to_gate, to_up, to_down = copies(k)
        head_rows[:, place] = product(dlog_t[...], final_rows[:, place])
        to_head.start()
        gate_up_rows[:, place] = product(hidden_t[...], normed[:, place])
        to_gate.start()
        to_up.start()
        down_rows[:, place] = product(activated_t[...], grad_rows[:, place])
        to_down.start()

    def done(k):
        for copy in copies(k):
            copy.wait()

    loop(0, 4, chunk)
    loop(0, 4, done)


def shape(dims, dtype):
    return jax.ShapeDtypeStruct(dims, dtype)


def per_device(
    layer_out,
    resid_mid,
    final_gain,
    mlp_gain,
    head_weight,
    w_gate,
    w_up,
    w_down,
    teacher_logits,
    assign,
    lengths,
    token_ids,
):
    final_gain = final_gain.reshape(8, 1, BLOCK)
    mlp_gain = mlp_gain.reshape(8, 1, BLOCK)
    vmem = pl.BlockSpec(memory_space=pltpu.VMEM)
    smem = pl.BlockSpec(memory_space=pltpu.SMEM)
    hbm = pl.BlockSpec(memory_space=pl.ANY)
    full = pltpu.VMEM((4, 16, 16, SLICE), BF16)
    rows = pltpu.VMEM((256, D), BF16)
    dma = pltpu.SemaphoreType.DMA
    shared = pl.pallas_call(
        program,
        out_shape=[
            pltpu.VMEM((8, BLOCK), F32),
            pltpu.VMEM((8, BLOCK), F32),
            rows,
            rows,
            rows,
            pltpu.VMEM((384, 256), BF16),
            pltpu.VMEM((128, 256), BF16),
            pltpu.VMEM((64, 256), BF16),
        ],
        in_specs=[vmem] * 5 + [smem] * 3 + [hbm] * 4,
        out_specs=[vmem] * 8,
        scratch_shapes=[
            pltpu.VMEM((384, D), BF16),
            pltpu.VMEM((128, D), BF16),
            pltpu.VMEM((64, D), BF16),
            pltpu.VMEM((256, 384), BF16),
            pltpu.VMEM((4, 256, 384), BF16),
            pltpu.VMEM((4, 256, 128), BF16),
            pltpu.VMEM((16, 8, BLOCK), BF16),
            pltpu.VMEM((16, 8, BLOCK), BF16),
            full,
            full,
            full,
            pltpu.VMEM((32, 8, 384), BF16),
            pltpu.VMEM((32, 8, 384), BF16),
            pltpu.VMEM((256, 384), F32),
            pltpu.VMEM((256, 384), F32),
            pltpu.VMEM((128, 256), F32),
            pltpu.VMEM((64, 256), F32),
            pltpu.VMEM((16, 4, 256), F32),
            pltpu.VMEM((16, 4, 256), F32),
            pltpu.VMEM((128, 256), F32),
            pltpu.VMEM((8, BLOCK), BF16),
            pltpu.VMEM((8, 8, BLOCK), BF16),
            pltpu.VMEM((2, 2, 8, 128), F32),
            dma((4,)),
            dma((2, 4)),
            dma((2,)),
            dma((4,)),
            dma((2,)),
            dma((3, 2)),
            dma((3, 2, 8)),
            dma((3, 2)),
            dma((3, 2, 5)),
        ]
        + REDUCE_SCRATCH
        + REDUCE_SCRATCH,
        compiler_params=pltpu.CompilerParams(
            collective_id=0, has_side_effects=True, vmem_limit_bytes=VMEM_LIMIT
        ),
        name="backward",
    )(
        layer_out,
        resid_mid,
        final_gain,
        mlp_gain,
        teacher_logits,
        assign,
        lengths,
        token_ids,
        head_weight,
        w_gate,
        w_up,
        w_down,
    )
    return pl.pallas_call(
        weight_grads,
        out_shape=[
            shape((8, BLOCK), BF16),
            shape(head_weight.shape, BF16),
            shape(w_gate.shape, BF16),
            shape(w_up.shape, BF16),
            shape(w_down.shape, BF16),
        ],
        in_specs=[vmem] * 8,
        out_specs=[vmem] + [hbm] * 4,
        scratch_shapes=[
            pltpu.VMEM((384, D), BF16),
            pltpu.VMEM((128, D), BF16),
            pltpu.VMEM((64, D), BF16),
            dma((4, 4)),
        ],
        compiler_params=pltpu.CompilerParams(vmem_limit_bytes=GRADS_VMEM),
        cost_estimate=pl.CostEstimate(flops=2 * 256 * 576 * D, bytes_accessed=2 * 576 * D, transcendentals=0),
        name="weight_grads",
    )(shared[0], shared[1], shared[5], shared[6], shared[7], shared[2], shared[3], shared[4])


def solution(mesh):
    return jax.shard_map(
        per_device,
        mesh=mesh,
        in_specs=(
            P("dp", "tensor"),
            P("dp", "tensor"),
            P(),
            P(),
            P(("tensor", "dp"), None),
            P(("tensor", "dp"), None),
            P(("tensor", "dp"), None),
            P(("tensor", "dp"), None),
            P("dp", "tensor"),
            P("dp", None),
            P("dp", None),
            P("dp"),
        ),
        out_specs=(
            P("dp", "tensor"),
            P(("tensor", "dp"), None),
            P(("tensor", "dp"), None),
            P(("tensor", "dp"), None),
            P(("tensor", "dp"), None),
        ),
        check_vma=False,
    )
```

```python
import jax
import jax.numpy as jnp
from jax import lax
from jax.experimental import pallas as pl
from jax.experimental.pallas import tpu as pltpu
from jax.sharding import PartitionSpec as P

D = 5120
SLOT = 4
EPS = 1e-06
CE_WEIGHT = 0.5
LOSS_SCALE = 4096.0

BLOCK = 640
SLICE = 1280
CHIPS = 16
F32 = jnp.float32
BF16 = jnp.bfloat16
VMEM_LIMIT = 52 * 1024 * 1024
GRADS_VMEM = 20 * 1024 * 1024


def contract_cols(left, right):
    return lax.dot_general(left, right, (((1,), (1,)), ((), ())), preferred_element_type=F32)


def wrap(v, size):
    return jnp.where(v >= size, v - size, v)


def ring_bits(v):
    high = v // 2
    return v % 2 + high - 2 * (v % 2) * high, high


class Spot:
    def __init__(self):
        self.d = lax.axis_index("dp")
        self.z = lax.axis_index("tensor")
        self.chip = lax.div(self.d, 2)
        self.c = self.d - 2 * self.chip
        self.y = lax.div(self.chip, 4)
        self.x = self.chip - 4 * self.y
        c, other = self.c, 1 - self.c
        xv, yv = lax.div(self.x, 2), lax.div(self.y, 2)
        x_low, y_low = self.x - 2 * xv, self.y - 2 * yv
        xu, yu = x_low + xv - 2 * x_low * xv, y_low + yv - 2 * y_low * yv
        x_near, y_near = self.x + 1 - 2 * x_low, self.y + 1 - 2 * y_low
        x_far, y_far = 3 - self.x, 3 - self.y
        self.half = lax.div(self.z, 4)
        self.z_low = self.z - 4 * self.half
        bits = (xu, yu, xv, yv)
        moved = (x_near, y_near, x_far, y_far)
        self.own_bits = [bits[i] * other + bits[(i + 2) % 4] * c for i in range(4)]
        self.sib_bits = [bits[i] * c + bits[(i + 2) % 4] * other for i in range(4)]
        moved = [moved[i] * other + moved[(i + 2) % 4] * c for i in range(4)]
        self.chips = [self.y * 4 + moved[i] if i % 2 == 0 else moved[i] * 4 + self.x for i in range(4)]
        corner = []
        for i in range(4):
            j = (i + 1) % 4
            corner.append(moved[j] * 4 + moved[i] if i % 2 == 0 else moved[i] * 4 + moved[j])
        self.corners = corner

    def pick(self, values, kk, s):
        if isinstance(kk, int):
            return values[(kk + s) % 4]
        first, second = values[s % 4], values[(s + 1) % 4]
        return first + (second - first) * kk

    def bit(self, kk, s):
        return self.pick(self.own_bits, kk, s)

    def sib_bit(self, kk, s):
        return self.pick(self.sib_bits, kk, s)

    def base(self, kk, s):
        return sum((self.bit(kk, i) * (8 >> i) for i in range(s)), jnp.int32(0))

    def sib_base(self, kk, s):
        return sum((self.sib_bit(kk, i) * (8 >> i) for i in range(s)), jnp.int32(0))

    def place(self, kk):
        return self.base(kk, 4)

    def partner(self, kk, s):
        return (self.pick(self.chips, kk, s) * 2 + self.c, self.z)

    def diagonal(self, kk, s):
        return (self.pick(self.corners, kk, s) * 2 + self.c, self.z)

    def sibling(self):
        return (self.chip * 2 + 1 - self.c, self.z)

    def column_peer(self, up, flip=0):
        core = self.c if flip == 0 else 1 - self.c
        return (self.chip * 2 + core, wrap(self.z + up, 8))


def greet(spot):
    barrier = pltpu.get_barrier_semaphore()
    mesh = pl.DeviceIdType.MESH
    pl.semaphore_signal(barrier, inc=1, device_id=spot.sibling(), device_id_type=mesh)

    def column(up, carry):
        for flip in range(2):
            pl.semaphore_signal(barrier, inc=1, device_id=spot.column_peer(up, flip), device_id_type=mesh)
        return carry

    lax.fori_loop(1, 8, column, 0)

    def body(j, carry):
        chip = wrap(spot.chip + j, CHIPS)
        for core in range(2):
            pl.semaphore_signal(
                barrier, inc=1, device_id=(chip * 2 + core, spot.z), device_id_type=pl.DeviceIdType.MESH
            )
        return carry

    lax.fori_loop(1, CHIPS, body, 0)


def greeted():
    pl.semaphore_wait(pltpu.get_barrier_semaphore(), 45)


def remote(src, dst, send_sem, recv_sem, target):
    return pltpu.make_async_remote_copy(
        src_ref=src,
        dst_ref=dst,
        send_sem=send_sem,
        recv_sem=recv_sem,
        device_id=target,
        device_id_type=pl.DeviceIdType.MESH,
    )


def row_scale(raw, core):
    total = jnp.zeros((8, BLOCK), F32)
    for zb in range(8):
        part = raw[8 * core + zb].astype(F32)
        total = total + part * part
    return lax.rsqrt(jnp.sum(total, axis=1, keepdims=True) / D + EPS)


def loop(start, stop, body):
    def step(i, carry):
        body(i)
        return carry

    lax.fori_loop(start, stop, step, 0)


def wait_bytes(ref, sem):
    pltpu.make_async_copy(ref, ref, sem).wait()


class Gather:
    def __init__(self, spot, full, xy_send, xy_recv, sib_send, sib_recv):
        self.spot, self.full = spot, full
        self.xy_send, self.xy_recv, self.sib_send, self.sib_recv = xy_send, xy_recv, sib_send, sib_recv

    def view(self, kk, off, n, core=None):
        core = self.spot.c if core is None else core
        return self.full.at[2 * core + kk, pl.ds(off, n)]

    def send(self, kk, target, idx, off, n):
        view = self.view(kk, off, n)
        remote(view, view, self.xy_send.at[kk], self.xy_recv.at[kk, idx], target).start()

    def arrived(self, kk, idx, off, n):
        wait_bytes(self.view(kk, off, n), self.xy_recv.at[kk, idx])

    def pass_on(self, kk, idx, off, n):
        view = self.view(kk, off, n)
        remote(view, view, self.sib_send.at[kk], self.sib_recv.at[kk, idx], self.spot.sibling()).start()

    def step(self, stage, kk):
        spot = self.spot
        flip = [(8 >> s) * (1 - 2 * spot.bit(kk, s)) for s in range(4)]
        own, four = spot.place(kk), spot.base(kk, 2)
        if stage == 0:
            self.send(kk, spot.diagonal(kk, 2), 2, own, 1)
            self.send(kk, spot.partner(kk, 3), 0, own, 1)
            self.send(kk, spot.partner(kk, 2), 1, own, 1)
        elif stage == 1:
            self.arrived(kk, 0, own + flip[3], 1)
            self.arrived(kk, 1, own + flip[2], 1)
            self.arrived(kk, 2, own + flip[2] + flip[3], 1)
            self.send(kk, spot.partner(kk, 1), 3, four, 2)
            self.send(kk, spot.partner(kk, 1), 4, four + 2, 2)
            self.send(kk, spot.partner(kk, 0), 5, four, 4)
            self.pass_on(kk, 0, four, 4)
        elif stage == 2:
            new = four + flip[1]
            for i in range(2):
                self.arrived(kk, 3 + i, new + 2 * i, 2)
                self.send(kk, spot.partner(kk, 0), 6 + i, new + 2 * i, 2)
            self.pass_on(kk, 1, new, 4)
        elif stage == 3:
            new = four + flip[0]
            self.arrived(kk, 5, new, 4)
            self.pass_on(kk, 2, new, 4)
            new = new + flip[1]
            for i in range(2):
                self.arrived(kk, 6 + i, new + 2 * i, 2)
                self.pass_on(kk, 3 + i, new + 2 * i, 2)
        else:
            other = 1 - spot.c
            four = spot.sib_base(kk, 2)
            over_1 = four + 4 * (1 - 2 * spot.sib_bit(kk, 1))
            over_0 = 8 * (1 - 2 * spot.sib_bit(kk, 0))
            last = over_1 + over_0
            pieces = ((four, 4), (over_1, 4), (four + over_0, 4), (last, 2), (last + 2, 2))
            for idx, (off, n) in enumerate(pieces):
                wait_bytes(self.view(kk, off, n, other), self.sib_recv.at[kk, idx])

    def finish(self):
        for kk in range(2):
            wait_bytes(self.full.at[kk, pl.ds(0, 15)], self.xy_send.at[kk])
            wait_bytes(self.full.at[kk], self.sib_send.at[kk])


def block_place(k, chip):
    xu, xv = ring_bits(chip % 4)
    yu, yv = ring_bits(chip // 4)
    bits = (xu, yu, xv, yv)
    return sum(bits[(k + s) % 4] * (8 >> s) for s in range(4))


def slice_columns(kk, core):
    return pl.ds(pl.multiple_of((2 * core + kk) * SLICE, SLICE), SLICE)


def lay_out(full, out, kk, core):
    for chip in range(CHIPS):
        low, high = block_place(kk, chip), block_place(2 + kk, chip)
        out[16 * chip : 16 * chip + 16, slice_columns(kk, core)] = full[2 * core + kk, low + (high - low) * core]


REDUCE_SCRATCH = [
    pltpu.VMEM((4, 16, 16, SLICE), BF16),
    pltpu.VMEM((2, 16, 16, SLICE), BF16),
    pltpu.VMEM((2, 15, 16, SLICE), BF16),
    pltpu.VMEM((8, 8, BLOCK), BF16),
    pltpu.VMEM((8, 8, BLOCK), BF16),
    pltpu.VMEM((2, 1, 128), F32),
    pltpu.VMEM((9, 1, 128), F32),
    pltpu.SemaphoreType.DMA((2,)),
    pltpu.SemaphoreType.DMA((2, 2)),
    pltpu.SemaphoreType.DMA((2,)),
    pltpu.SemaphoreType.DMA((2, 7)),
    pltpu.SemaphoreType.DMA((6,)),
]


class Reduce:
    def __init__(self, spot, scratch):
        self.spot = spot
        (
            self.partial,
            self.from_sib,
            self.from_xy,
            self.to_col,
            self.from_col,
            self.inner_to,
            self.inner_from,
            self.sib_send,
            self.sib_recv,
            self.xy_send,
            self.xy_recv,
            self.col_sems,
        ) = scratch

    def sib_copy(self, kk, sub, core, bit):
        half = (1 - sub) * (1 - bit) + sub * bit
        return remote(
            self.partial.at[2 * core + kk, pl.ds(half * 8, 8)],
            self.from_sib.at[kk, pl.ds(half * 8, 8)],
            self.sib_send.at[kk],
            self.sib_recv.at[kk, sub],
            self.spot.sibling(),
        )

    def start(self, kk, sub):
        self.sib_copy(kk, sub, 1 - self.spot.c, self.spot.sib_bit(kk, 0)).start()

    def from_sibling(self, kk, sub):
        self.sib_copy(kk, sub, self.spot.c, self.spot.bit(kk, 0)).wait_recv()

    def add(self, kk, off, ref, ref_off, n):
        k = 2 * self.spot.c + kk

        def body(i, carry):
            self.partial[k, off + i] = self.partial[k, off + i] + ref[kk, ref_off + i]
            return carry

        if n == 1:
            body(0, 0)
        else:
            lax.fori_loop(0, n, body, 0)

    def plan(self, kk, s):
        n = 8 >> s
        landing = 16 - 2 * n
        bit = self.spot.bit(kk, s)
        gone = self.spot.base(kk, s) + (1 - bit) * n
        kept = self.spot.base(kk, s) + bit * n
        half = n // 2
        after = self.spot.bit(kk, s + 1)
        pieces = []
        for sub in range(2):
            shift = ((1 - after) if sub == 0 else after) * half
            pieces.append((gone + shift, kept + shift, landing + sub * half, half, 2 * s + sub))
        return pieces

    def xy_copy(self, kk, s, piece):
        gone, _, landing, n, idx = piece
        return remote(
            self.partial.at[2 * self.spot.c + kk, pl.ds(gone, n)],
            self.from_xy.at[kk, pl.ds(landing, n)],
            self.xy_send.at[kk],
            self.xy_recv.at[kk, idx],
            self.spot.partner(kk, s),
        )

    def xy_start(self, kk, s, piece):
        self.xy_copy(kk, s, piece).start()

    def plane(self, own_part, beside):
        spot = self.spot

        def first(kk):
            self.from_sibling(kk, 0)
            for piece in self.plan(kk, 0):
                self.add(kk, piece[0], self.from_sib, piece[0], piece[3])
                self.xy_start(kk, 0, piece)

        def kept(kk):
            self.from_sibling(kk, 1)
            self.add(kk, spot.bit(kk, 0) * 8, self.from_sib, spot.bit(kk, 0) * 8, 8)

        def arrive(kk, s, sub):
            piece = self.plan(kk, s)[sub]
            self.xy_copy(kk, s, piece).wait_recv()
            self.add(kk, piece[1], self.from_xy, piece[2], piece[3])

        def second(kk):
            arrive(kk, 0, 0)
            for follow in self.plan(kk, 1):
                self.xy_start(kk, 1, follow)

        def third(kk):
            arrive(kk, 1, 0)
            by_2 = spot.place(kk) + 2 * (1 - 2 * spot.bit(kk, 2))
            self.tail_copy(kk, by_2 + 1 - 2 * spot.bit(kk, 3), 2, spot.diagonal(kk, 2)).start()
            self.tail_copy(kk, by_2, 0, spot.partner(kk, 2)).start()

        def fourth(kk):
            arrive(kk, 1, 1)
            own = spot.place(kk)
            self.tail_copy(kk, own + 1 - 2 * spot.bit(kk, 3), 1, spot.partner(kk, 3)).start()

        for kk in range(2):
            own_part(kk, 0)
            first(kk)
        for kk in range(2):
            own_part(kk, 1)
        for kk in range(2):
            kept(kk)
        for work in beside.get(-1, ()):
            work()
        for kk in range(2):
            second(kk)
        for kk in range(2):
            arrive(kk, 0, 1)
        for work in beside.get(0, ()):
            work()
        for kk in range(2):
            third(kk)
        for kk in range(2):
            fourth(kk)
        for work in beside.get(1, ()):
            work()
        places = [spot.place(kk) for kk in range(2)]
        sums = []
        for kk in range(2):
            total = self.partial[2 * spot.c + kk, places[kk]].astype(F32)
            for i in range(3):
                self.tail_copy(kk, places[kk], i, spot.sibling()).wait_recv()
                total = total + self.from_xy[kk, 12 + i].astype(F32)
            sums.append(total)
        return sums

    def tail_copy(self, kk, block, i, target):
        return remote(
            self.partial.at[2 * self.spot.c + kk, pl.ds(block, 1)],
            self.from_xy.at[kk, pl.ds(12 + i, 1)],
            self.xy_send.at[kk],
            self.xy_recv.at[kk, 4 + i],
            target,
        )

    def column(self, sums, raw, gain, scale, beside=()):
        spot = self.spot
        for kk in range(2):
            for j in range(2):
                for core in range(2):
                    part = sums[kk][8 * core : 8 * core + 8, j * BLOCK : (j + 1) * BLOCK]
                    self.to_col[2 * (2 * kk + j) + core] = part.astype(BF16)

        def to_column(zz):
            zdst = 4 * spot.c + zz
            for core in range(2):
                mine = jnp.logical_and(zdst == spot.z, spot.c == core)

                @pl.when(jnp.logical_not(mine))
                def _(core=core):
                    remote(
                        self.to_col.at[2 * zz + core],
                        self.from_col.at[spot.z],
                        self.col_sems.at[0],
                        self.col_sems.at[1],
                        (spot.chip * 2 + core, zdst),
                    ).start()

                @pl.when(mine)
                def _(core=core):
                    self.from_col[spot.z] = self.to_col[2 * zz + core]

        loop(0, 4, to_column)
        row = lax.broadcasted_iota(jnp.int32, (8, 128), 0)
        diagonal = row == lax.broadcasted_iota(jnp.int32, (8, 128), 1)
        for core in range(2):
            total = jnp.zeros((8, BLOCK), F32)
            for kk in range(2):
                for j in range(2):
                    zb = 4 * spot.c + 2 * kk + j
                    part = sums[kk][8 * core : 8 * core + 8, j * BLOCK : (j + 1) * BLOCK]
                    total = total + raw[8 * core + zb].astype(F32) * gain[zb] * part
            inner = jnp.where(diagonal, jnp.sum(total, axis=1, keepdims=True), 0.0)
            self.inner_to[core] = jnp.sum(inner, axis=0, keepdims=True)
        to_sibling = remote(
            self.inner_to.at[1 - spot.c],
            self.inner_from.at[8],
            self.col_sems.at[4],
            self.col_sems.at[5],
            spot.sibling(),
        )
        to_sibling.start()
        to_sibling.wait_recv()
        self.inner_from[0] = self.inner_to[spot.c] + self.inner_from[8]
        loop(
            1,
            8,
            lambda up: remote(
                self.inner_from.at[0],
                self.inner_from.at[up],
                self.col_sems.at[2],
                self.col_sems.at[3],
                spot.column_peer(up),
            ).start(),
        )
        for work in beside:
            work()
        own = raw[8 * spot.c + spot.z].astype(F32)
        own_gain = gain[spot.z]
        wait_column(spot, self.from_col, self.col_sems.at[1])
        grad = jnp.zeros((8, BLOCK), F32)
        for zsrc in range(8):
            grad = grad + self.from_col[zsrc].astype(F32)
        wait_bytes(self.inner_from.at[pl.ds(1, 7)], self.col_sems.at[3])
        inner = jnp.zeros((1, 128), F32)
        for i in range(8):
            inner = inner + self.inner_from[i]
        inner = jnp.sum(jnp.where(diagonal, inner, 0.0), axis=1, keepdims=True) / D
        return scale * own_gain * grad - own * (scale * scale * scale) * inner

    def finish(self):
        for kk in range(2):
            wait_bytes(self.partial.at[kk], self.sib_send.at[kk])
            wait_bytes(self.partial.at[kk, pl.ds(0, 15)], self.xy_send.at[kk])
        wait_column(self.spot, self.to_col, self.col_sems.at[0])
        wait_bytes(self.inner_from.at[pl.ds(1, 7)], self.col_sems.at[2])
        wait_bytes(self.inner_from.at[pl.ds(8, 1)], self.col_sems.at[4])


def wait_column(spot, ref, sem):
    own = spot.half == spot.c

    @pl.when(own)
    def _():
        wait_bytes(ref.at[pl.ds(0, 7)], sem)

    @pl.when(jnp.logical_not(own))
    def _():
        wait_bytes(ref, sem)


def program(
    layer_out,
    resid_mid,
    final_gain,
    mlp_gain,
    teacher_in,
    assign,
    lengths,
    token_ids,
    head_hbm,
    gate_hbm,
    up_hbm,
    down_hbm,
    grad_first,
    grad_second,
    final_rows,
    normed,
    grad_rows,
    dlog_t,
    hidden_t,
    activated_t,
    head,
    w_gate_up,
    w_down,
    dlog,
    dlog_turned,
    hidden_turned,
    raw_out,
    raw_mid,
    full_out,
    full_mid,
    full_grad,
    packed,
    got,
    logits_ref,
    diff_ref,
    gate_up_pre,
    act_grad,
    first,
    second,
    stats_pad,
    own_b,
    own_from,
    scale_ref,
    load_sem,
    raw_sems,
    plane_sems,
    stat_sems,
    own_sems,
    xy_send,
    xy_recv,
    sib_send,
    sib_recv,
    *scratch,
):
    spot = Spot()
    c, other = spot.c, 1 - spot.c
    loads = [
        pltpu.make_async_copy(src, dst, load_sem.at[i])
        for i, (src, dst) in enumerate(
            (
                (head_hbm, head),
                (gate_hbm, w_gate_up.at[pl.ds(0, 64)]),
                (up_hbm, w_gate_up.at[pl.ds(64, 64)]),
                (down_hbm, w_down),
            )
        )
    ]
    for load in loads:
        load.start()
    reduces = [Reduce(spot, scratch[: len(REDUCE_SCRATCH)]), Reduce(spot, scratch[len(REDUCE_SCRATCH) :])]
    gathers = [
        Gather(spot, full, xy_send.at[a], xy_recv.at[a], sib_send.at[a], sib_recv.at[a])
        for a, full in enumerate((full_out, full_mid, full_grad))
    ]
    gather_out, gather_mid, gather_grad = gathers

    greet(spot)
    mine = 8 * c + spot.z
    raw_out[mine] = layer_out[...]
    raw_mid[mine] = resid_mid[...]

    row = lax.broadcasted_iota(jnp.int32, (8, 1), 0)
    order = jnp.zeros((8, 1), jnp.int32)
    for r in range(8):
        order = jnp.where(row == r, assign[0, r], order)

    def pack(peer):
        rows = teacher_in[:, pl.ds(pl.multiple_of(peer * 384, 384), 384)].astype(F32)
        picked = jnp.zeros((8, 384), F32)
        for r in range(8):
            picked = picked + jnp.where(order == r, rows[r : r + 1, :], 0.0)
        packed[peer] = picked.astype(BF16)

    loop(0, 32, pack)
    got[spot.d] = packed[spot.d]

    token = lax.broadcasted_iota(jnp.int32, (1, 256), 1)
    own_ids = jnp.full((1, 256), -1, jnp.int32)
    own_lengths = jnp.zeros((1, 256), jnp.int32)
    for r in range(8):
        here = token == 8 * spot.d + r
        own_ids = jnp.where(here, token_ids[r], own_ids)
        own_lengths = jnp.where(here, lengths[0, r // SLOT], own_lengths)
    live = (lax.rem(token, SLOT) < own_lengths).astype(jnp.int32)
    codes = jnp.where(own_ids >= 0, 2 * own_ids + live, 0).astype(F32)
    greeted()

    def send_raw(a, own, raw):
        loop(
            1,
            8,
            lambda up: remote(
                own, raw.at[mine], raw_sems.at[a, 0], raw_sems.at[a, 1], spot.column_peer(up)
            ).start(),
        )

    def pass_raw(a, raw):
        wait_bytes(raw.at[pl.ds(0, 7)], raw_sems.at[a, 1])
        rows = raw.at[pl.ds(8 * c, 8)]
        remote(rows, rows, raw_sems.at[a, 2], raw_sems.at[a, 3], spot.sibling()).start()

    def plane_start(i, carry):
        peer = wrap(spot.d + i, 32)
        remote(packed.at[peer], got.at[spot.d], plane_sems.at[0], plane_sems.at[1], (peer, spot.z)).start()
        return carry

    def normalise(a, raw, full, gain):
        wait_bytes(raw.at[pl.ds(0, 8)], raw_sems.at[a, 3])
        scales = [row_scale(raw, core) for core in range(2)]
        for kk in range(2):
            place = spot.place(kk)
            for j in range(2):
                zb = 4 * c + 2 * kk + j
                rows = jnp.concatenate(
                    [raw[8 * core + zb].astype(F32) * scales[core] * gain[zb] for core in range(2)], axis=0
                )
                full[2 * c + kk, place, :, j * BLOCK : (j + 1) * BLOCK] = rows.astype(BF16)
        for core in range(2):
            scale_ref[a, core] = jnp.broadcast_to(scales[core], (8, 128))

    def both(gather, stage):
        for kk in range(2):
            gather.step(stage, kk)

    send_raw(0, layer_out, raw_out)
    lax.fori_loop(1, 32, plane_start, 0)
    send_raw(1, resid_mid, raw_mid)
    pass_raw(0, raw_out)
    normalise(0, raw_out, full_out, final_gain)
    both(gather_out, 0)
    both(gather_out, 1)
    pass_raw(1, raw_mid)
    both(gather_out, 2)
    normalise(1, raw_mid, full_mid, mlp_gain)
    both(gather_out, 3)
    both(gather_mid, 0)

    def products(left, right, out, core):
        def body(kk):
            columns = slice_columns(kk, core)
            out[...] += contract_cols(left[:, columns], right[:, columns])

        loop(0, 2, body)

    for kk in range(2):
        lay_out(full_out, final_rows, kk, c)
    loads[0].wait()
    logits_ref[...] = jnp.zeros_like(logits_ref)
    products(final_rows, head, logits_ref, c)
    both(gather_mid, 1)
    both(gather_out, 4)
    for kk in range(2):
        lay_out(full_out, final_rows, kk, other)
    products(final_rows, head, logits_ref, other)

    wait_bytes(got.at[pl.ds(0, 31)], plane_sems.at[1])
    logits = logits_ref[...]
    diff = logits - got[...].astype(F32).reshape(256, 384)
    local_max = jnp.max(logits, axis=1, keepdims=True)
    expd = jnp.exp(logits - local_max)
    total = jnp.sum(expd, axis=1, keepdims=True)
    moment = jnp.sum(expd * diff, axis=1, keepdims=True)
    logits_ref[...] = expd
    diff_ref[...] = diff
    lanes = lax.broadcasted_iota(jnp.int32, (256, 128), 1)
    columns = jnp.where(lanes == 0, local_max, jnp.where(lanes == 1, total, moment))
    first[0] = jnp.transpose(columns)[0:4]
    first[0, 3:4] = codes
    remote(first.at[0], first.at[1], stat_sems.at[0], stat_sems.at[1], spot.sibling()).start()

    def to_column(up):
        for flip in range(2):
            target = spot.column_peer(up, flip)
            remote(first.at[0], first.at[2 * up + flip], stat_sems.at[0], stat_sems.at[1], target).start()

    loop(1, 8, to_column)
    both(gather_mid, 2)

    def combine(ref, groups):
        top = ref[0, 0:1]
        for i in range(1, 16):
            top = jnp.maximum(top, ref[i, 0:1])
        total = jnp.zeros_like(top)
        moment = jnp.zeros_like(top)
        for i in range(16):
            weight = jnp.exp(ref[i, 0:1] - top)
            total = total + ref[i, 1:2] * weight
            moment = moment + ref[i, 2:3] * weight
        return jnp.concatenate([top, total, moment, sum(ref[i, 3:4] for i in range(groups))], axis=0)

    wait_bytes(first.at[pl.ds(1, 15)], stat_sems.at[1])
    second[0] = combine(first, 2)

    def to_plane(i):
        target = (wrap(spot.chip + i, CHIPS) * 2 + c, spot.z)
        remote(second.at[0], second.at[i], stat_sems.at[2], stat_sems.at[3], target).start()

    loop(1, CHIPS, to_plane)
    both(gather_mid, 3)
    vocab = lax.broadcasted_iota(jnp.int32, (256, 384), 1) + (spot.z * 32 + spot.d) * 384
    stats_pad[...] = jnp.zeros_like(stats_pad)
    wait_bytes(second.at[pl.ds(1, 15)], stat_sems.at[3])
    stats_pad[0:4] = combine(second, 16)
    columns = jnp.transpose(stats_pad[...])
    global_max, totals, moments = columns[:, 0:1], columns[:, 1:2], columns[:, 2:3]
    code = columns[:, 3:4].astype(jnp.int32)
    ids_all = code >> 1
    live_mask = (code - 2 * ids_all).astype(F32)
    token_weight = live_mask * (LOSS_SCALE / jnp.sum(live_mask, axis=0, keepdims=True))
    share = token_weight * (jnp.exp(local_max - global_max) / totals)
    shift = CE_WEIGHT - moments / totals
    dlogits = share * logits_ref[...] * (diff_ref[...] + shift)
    dlogits = dlogits - jnp.where(ids_all == vocab, CE_WEIGHT * token_weight, 0.0)

    def turn(rows, out):
        for k in range(4):
            for chip in range(CHIPS):
                place = 16 * block_place(k, chip)
                out[k, place : place + 16, :] = rows[16 * chip : 16 * chip + 16]

    def spread(reduce, kk, core, half, left, right):
        k = 2 * core + kk
        rows = left[k, pl.ds(pl.multiple_of(half * 128, 128), 128)]
        part = jnp.dot(rows, right[:, slice_columns(kk, core)], preferred_element_type=F32).astype(BF16)
        reduce.partial[k, pl.ds(half * 8, 8)] = part.reshape(8, 16, SLICE)

    def send_partial(reduce, left, right):

        def to_sibling(i):
            sub = jnp.where(i >= 2, 1, 0)
            kk = i - 2 * sub
            bit = spot.sib_bit(kk, 0)
            spread(reduce, kk, other, (1 - sub) * (1 - bit) + sub * bit, left, right)
            reduce.start(kk, sub)

        loop(0, 4, to_sibling)

        def own_part(kk, sub):
            bit = spot.bit(kk, 0)
            spread(reduce, kk, c, (1 - bit) if sub == 0 else bit, left, right)

        return own_part

    dlog_b = dlogits.astype(BF16)
    turn(dlog_b, dlog_turned)
    dlog[...] = dlog_b

    def mid_rows(core):
        for kk in range(2):
            lay_out(full_mid, normed, kk, core)

    def mid_first():
        for load in loads[1:]:
            load.wait()
        gate_up_pre[...] = jnp.zeros_like(gate_up_pre)
        act_grad[...] = jnp.zeros_like(act_grad)
        mid_rows(c)
        products(w_gate_up, normed, gate_up_pre, c)

    def mid_second():
        both(gather_mid, 4)
        mid_rows(other)
        products(w_gate_up, normed, gate_up_pre, other)

    def activate():
        gate = gate_up_pre[0:64]
        activated_t[...] = (gate * jax.nn.sigmoid(gate) * gate_up_pre[64:128]).astype(BF16)

    def turn_dlog():
        dlog_t[...] = jnp.transpose(dlog[...].astype(F32)).astype(BF16)

    own_part = send_partial(reduces[0], dlog_turned, head)
    sums = reduces[0].plane(own_part, {-1: [mid_first], 0: [mid_second], 1: [activate]})
    grad_out = reduces[0].column(sums, raw_out, final_gain, scale_ref[0, c][:, 0:1])
    own_b[...] = grad_out.astype(BF16)
    grad_first[...] = grad_out

    target_core = spot.half
    own_place = spot.z_low * 2 + c

    def own_to_column(zdst):
        mine = jnp.logical_and(spot.z == zdst, target_core == c)

        @pl.when(jnp.logical_not(mine))
        def _():
            target = (spot.chip * 2 + target_core, zdst)
            remote(own_b, own_from.at[own_place], own_sems.at[0], own_sems.at[1], target).start()

        @pl.when(mine)
        def _():
            own_from[own_place] = own_b[...]

    loop(0, 8, own_to_column)
    turn_dlog()
    wait_column(spot, own_from, own_sems.at[1])
    for kk in range(2):
        for j in range(2):
            zz = 2 * kk + j
            rows = jnp.concatenate([own_from[2 * zz + core].astype(F32) for core in range(2)], axis=0)
            full_grad[2 * c + kk, spot.place(kk), :, j * BLOCK : (j + 1) * BLOCK] = rows.astype(BF16)
    both(gather_grad, 0)
    for stage in range(1, 4):
        both(gather_grad, stage)
    for kk in range(2):
        lay_out(full_grad, grad_rows, kk, c)
    products(w_down, grad_rows, act_grad, c)
    both(gather_grad, 4)
    for kk in range(2):
        lay_out(full_grad, grad_rows, kk, other)
    products(w_down, grad_rows, act_grad, other)

    gate, up, act = gate_up_pre[0:64], gate_up_pre[64:128], act_grad[...]
    gate_sigmoid = jax.nn.sigmoid(gate)
    gate_grad = act * up * gate_sigmoid * (1.0 + gate * (1.0 - gate_sigmoid))
    both_grads = jnp.concatenate([gate_grad, act * gate * gate_sigmoid], axis=0)
    turn(jnp.transpose(both_grads).astype(BF16), hidden_turned)
    hidden_t[...] = both_grads.astype(BF16)
    own_part = send_partial(reduces[1], hidden_turned, w_gate_up)

    def left_earlier():
        for a in range(2):
            wait_bytes(raw_out.at[pl.ds(0, 7)], raw_sems.at[a, 0])
            wait_bytes(raw_out.at[pl.ds(0, 8)], raw_sems.at[a, 2])
        wait_bytes(got.at[pl.ds(0, 31)], plane_sems.at[0])
        wait_bytes(first.at[pl.ds(1, 15)], stat_sems.at[0])
        wait_bytes(second.at[pl.ds(1, 15)], stat_sems.at[2])
        for gather in gathers:
            gather.finish()
        reduces[0].finish()
        wait_column(spot, own_from, own_sems.at[0])

    sums = reduces[1].plane(own_part, {-1: [left_earlier]})
    grad_second[...] = reduces[1].column(sums, raw_mid, mlp_gain, scale_ref[1, c][:, 0:1])
    reduces[1].finish()


def weight_grads(
    grad_first,
    grad_second,
    dlog_t,
    hidden_t,
    activated_t,
    final_rows,
    normed,
    grad_rows,
    grad_resid,
    grad_head,
    grad_gate,
    grad_up,
    grad_down,
    head_rows,
    gate_up_rows,
    down_rows,
    sems,
):
    def product(left, right):
        return jnp.dot(left, right, preferred_element_type=F32).astype(BF16)

    grad_resid[...] = (grad_first[...] + grad_second[...]).astype(BF16)

    def copies(k):
        place = pl.ds(pl.multiple_of(k * SLICE, SLICE), SLICE)
        return [
            pltpu.make_async_copy(head_rows.at[:, place], grad_head.at[:, place], sems.at[0, k]),
            pltpu.make_async_copy(gate_up_rows.at[pl.ds(0, 64), place], grad_gate.at[:, place], sems.at[1, k]),
            pltpu.make_async_copy(gate_up_rows.at[pl.ds(64, 64), place], grad_up.at[:, place], sems.at[2, k]),
            pltpu.make_async_copy(down_rows.at[:, place], grad_down.at[:, place], sems.at[3, k]),
        ]

    def chunk(k):
        place = pl.ds(pl.multiple_of(k * SLICE, SLICE), SLICE)
        to_head, to_gate, to_up, to_down = copies(k)
        head_rows[:, place] = product(dlog_t[...], final_rows[:, place])
        to_head.start()
        gate_up_rows[:, place] = product(hidden_t[...], normed[:, place])
        to_gate.start()
        to_up.start()
        down_rows[:, place] = product(activated_t[...], grad_rows[:, place])
        to_down.start()

    def done(k):
        for copy in copies(k):
            copy.wait()

    loop(0, 4, chunk)
    loop(0, 4, done)


def shape(dims, dtype):
    return jax.ShapeDtypeStruct(dims, dtype)


def per_device(
    layer_out,
    resid_mid,
    final_gain,
    mlp_gain,
    head_weight,
    w_gate,
    w_up,
    w_down,
    teacher_logits,
    assign,
    lengths,
    token_ids,
):
    final_gain = final_gain.reshape(8, 1, BLOCK)
    mlp_gain = mlp_gain.reshape(8, 1, BLOCK)
    vmem = pl.BlockSpec(memory_space=pltpu.VMEM)
    smem = pl.BlockSpec(memory_space=pltpu.SMEM)
    hbm = pl.BlockSpec(memory_space=pl.ANY)
    full = pltpu.VMEM((4, 16, 16, SLICE), BF16)
    rows = pltpu.VMEM((256, D), BF16)
    dma = pltpu.SemaphoreType.DMA
    shared = pl.pallas_call(
        program,
        out_shape=[
            pltpu.VMEM((8, BLOCK), F32),
            pltpu.VMEM((8, BLOCK), F32),
            rows,
            rows,
            rows,
            pltpu.VMEM((384, 256), BF16),
            pltpu.VMEM((128, 256), BF16),
            pltpu.VMEM((64, 256), BF16),
        ],
        in_specs=[vmem] * 5 + [smem] * 3 + [hbm] * 4,
        out_specs=[vmem] * 8,
        scratch_shapes=[
            pltpu.VMEM((384, D), BF16),
            pltpu.VMEM((128, D), BF16),
            pltpu.VMEM((64, D), BF16),
            pltpu.VMEM((256, 384), BF16),
            pltpu.VMEM((4, 256, 384), BF16),
            pltpu.VMEM((4, 256, 128), BF16),
            pltpu.VMEM((16, 8, BLOCK), BF16),
            pltpu.VMEM((16, 8, BLOCK), BF16),
            full,
            full,
            full,
            pltpu.VMEM((32, 8, 384), BF16),
            pltpu.VMEM((32, 8, 384), BF16),
            pltpu.VMEM((256, 384), F32),
            pltpu.VMEM((256, 384), F32),
            pltpu.VMEM((128, 256), F32),
            pltpu.VMEM((64, 256), F32),
            pltpu.VMEM((16, 4, 256), F32),
            pltpu.VMEM((16, 4, 256), F32),
            pltpu.VMEM((128, 256), F32),
            pltpu.VMEM((8, BLOCK), BF16),
            pltpu.VMEM((8, 8, BLOCK), BF16),
            pltpu.VMEM((2, 2, 8, 128), F32),
            dma((4,)),
            dma((2, 4)),
            dma((2,)),
            dma((4,)),
            dma((2,)),
            dma((3, 2)),
            dma((3, 2, 8)),
            dma((3, 2)),
            dma((3, 2, 5)),
        ]
        + REDUCE_SCRATCH
        + REDUCE_SCRATCH,
        compiler_params=pltpu.CompilerParams(
            collective_id=0, has_side_effects=True, vmem_limit_bytes=VMEM_LIMIT
        ),
        name="backward",
    )(
        layer_out,
        resid_mid,
        final_gain,
        mlp_gain,
        teacher_logits,
        assign,
        lengths,
        token_ids,
        head_weight,
        w_gate,
        w_up,
        w_down,
    )
    return pl.pallas_call(
        weight_grads,
        out_shape=[
            shape((8, BLOCK), BF16),
            shape(head_weight.shape, BF16),
            shape(w_gate.shape, BF16),
            shape(w_up.shape, BF16),
            shape(w_down.shape, BF16),
        ],
        in_specs=[vmem] * 8,
        out_specs=[vmem] + [hbm] * 4,
        scratch_shapes=[
            pltpu.VMEM((384, D), BF16),
            pltpu.VMEM((128, D), BF16),
            pltpu.VMEM((64, D), BF16),
            dma((4, 4)),
        ],
        compiler_params=pltpu.CompilerParams(vmem_limit_bytes=GRADS_VMEM),
        cost_estimate=pl.CostEstimate(flops=2 * 256 * 576 * D, bytes_accessed=2 * 576 * D, transcendentals=0),
        name="weight_grads",
    )(shared[0], shared[1], shared[5], shared[6], shared[7], shared[2], shared[3], shared[4])


def solution(mesh):
    return jax.shard_map(
        per_device,
        mesh=mesh,
        in_specs=(
            P("dp", "tensor"),
            P("dp", "tensor"),
            P(),
            P(),
            P(("tensor", "dp"), None),
            P(("tensor", "dp"), None),
            P(("tensor", "dp"), None),
            P(("tensor", "dp"), None),
            P("dp", "tensor"),
            P("dp", None),
            P("dp", None),
            P("dp"),
        ),
        out_specs=(
            P("dp", "tensor"),
            P(("tensor", "dp"), None),
            P(("tensor", "dp"), None),
            P(("tensor", "dp"), None),
            P(("tensor", "dp"), None),
        ),
        check_vma=False,
    )
```

```python
import jax
import jax.numpy as jnp
from jax import lax
from jax.experimental import pallas as pl
from jax.experimental.pallas import tpu as pltpu
from jax.sharding import PartitionSpec as P

D = 5120
SLOT = 4
EPS = 1e-06
CE_WEIGHT = 0.5
LOSS_SCALE = 4096.0

BLOCK = 640
SLICE = 1280
CHIPS = 16
F32 = jnp.float32
BF16 = jnp.bfloat16
VMEM_LIMIT = 52 * 1024 * 1024
GRADS_VMEM = 20 * 1024 * 1024


def contract_cols(left, right):
    return lax.dot_general(left, right, (((1,), (1,)), ((), ())), preferred_element_type=F32)


def wrap(v, size):
    return jnp.where(v >= size, v - size, v)


def ring_bits(v):
    high = v // 2
    return v % 2 + high - 2 * (v % 2) * high, high


class Spot:
    def __init__(self):
        self.d = lax.axis_index("dp")
        self.z = lax.axis_index("tensor")
        self.chip = lax.div(self.d, 2)
        self.c = self.d - 2 * self.chip
        self.y = lax.div(self.chip, 4)
        self.x = self.chip - 4 * self.y
        c, other = self.c, 1 - self.c
        xv, yv = lax.div(self.x, 2), lax.div(self.y, 2)
        x_low, y_low = self.x - 2 * xv, self.y - 2 * yv
        xu, yu = x_low + xv - 2 * x_low * xv, y_low + yv - 2 * y_low * yv
        x_near, y_near = self.x + 1 - 2 * x_low, self.y + 1 - 2 * y_low
        x_far, y_far = 3 - self.x, 3 - self.y
        self.half = lax.div(self.z, 4)
        self.z_low = self.z - 4 * self.half
        bits = (xu, yu, xv, yv)
        moved = (x_near, y_near, x_far, y_far)
        self.own_bits = [bits[i] * other + bits[(i + 2) % 4] * c for i in range(4)]
        self.sib_bits = [bits[i] * c + bits[(i + 2) % 4] * other for i in range(4)]
        moved = [moved[i] * other + moved[(i + 2) % 4] * c for i in range(4)]
        self.chips = [self.y * 4 + moved[i] if i % 2 == 0 else moved[i] * 4 + self.x for i in range(4)]
        corner = []
        for i in range(4):
            j = (i + 1) % 4
            corner.append(moved[j] * 4 + moved[i] if i % 2 == 0 else moved[i] * 4 + moved[j])
        self.corners = corner

    def pick(self, values, kk, s):
        if isinstance(kk, int):
            return values[(kk + s) % 4]
        first, second = values[s % 4], values[(s + 1) % 4]
        return first + (second - first) * kk

    def bit(self, kk, s):
        return self.pick(self.own_bits, kk, s)

    def sib_bit(self, kk, s):
        return self.pick(self.sib_bits, kk, s)

    def base(self, kk, s):
        return sum((self.bit(kk, i) * (8 >> i) for i in range(s)), jnp.int32(0))

    def sib_base(self, kk, s):
        return sum((self.sib_bit(kk, i) * (8 >> i) for i in range(s)), jnp.int32(0))

    def place(self, kk):
        return self.base(kk, 4)

    def partner(self, kk, s):
        return (self.pick(self.chips, kk, s) * 2 + self.c, self.z)

    def diagonal(self, kk, s):
        return (self.pick(self.corners, kk, s) * 2 + self.c, self.z)

    def sibling(self):
        return (self.chip * 2 + 1 - self.c, self.z)

    def column_peer(self, up, flip=0):
        core = self.c if flip == 0 else 1 - self.c
        return (self.chip * 2 + core, wrap(self.z + up, 8))


def greet(spot):
    barrier = pltpu.get_barrier_semaphore()
    mesh = pl.DeviceIdType.MESH
    pl.semaphore_signal(barrier, inc=1, device_id=spot.sibling(), device_id_type=mesh)

    def column(up, carry):
        for flip in range(2):
            pl.semaphore_signal(barrier, inc=1, device_id=spot.column_peer(up, flip), device_id_type=mesh)
        return carry

    lax.fori_loop(1, 8, column, 0)

    def body(j, carry):
        chip = wrap(spot.chip + j, CHIPS)
        for core in range(2):
            pl.semaphore_signal(
                barrier, inc=1, device_id=(chip * 2 + core, spot.z), device_id_type=pl.DeviceIdType.MESH
            )
        return carry

    lax.fori_loop(1, CHIPS, body, 0)


def greeted():
    pl.semaphore_wait(pltpu.get_barrier_semaphore(), 45)


def remote(src, dst, send_sem, recv_sem, target):
    return pltpu.make_async_remote_copy(
        src_ref=src,
        dst_ref=dst,
        send_sem=send_sem,
        recv_sem=recv_sem,
        device_id=target,
        device_id_type=pl.DeviceIdType.MESH,
    )


def row_scale(raw, core):
    total = jnp.zeros((8, BLOCK), F32)
    for zb in range(8):
        part = raw[8 * core + zb].astype(F32)
        total = total + part * part
    return lax.rsqrt(jnp.sum(total, axis=1, keepdims=True) / D + EPS)


def loop(start, stop, body):
    def step(i, carry):
        body(i)
        return carry

    lax.fori_loop(start, stop, step, 0)


def wait_bytes(ref, sem):
    pltpu.make_async_copy(ref, ref, sem).wait()


class Gather:
    def __init__(self, spot, full, xy_send, xy_recv, sib_send, sib_recv):
        self.spot, self.full = spot, full
        self.xy_send, self.xy_recv, self.sib_send, self.sib_recv = xy_send, xy_recv, sib_send, sib_recv

    def view(self, kk, off, n, core=None):
        core = self.spot.c if core is None else core
        return self.full.at[2 * core + kk, pl.ds(off, n)]

    def send(self, kk, target, idx, off, n):
        view = self.view(kk, off, n)
        remote(view, view, self.xy_send.at[kk], self.xy_recv.at[kk, idx], target).start()

    def arrived(self, kk, idx, off, n):
        wait_bytes(self.view(kk, off, n), self.xy_recv.at[kk, idx])

    def pass_on(self, kk, idx, off, n):
        view = self.view(kk, off, n)
        remote(view, view, self.sib_send.at[kk], self.sib_recv.at[kk, idx], self.spot.sibling()).start()

    def step(self, stage, kk):
        spot = self.spot
        flip = [(8 >> s) * (1 - 2 * spot.bit(kk, s)) for s in range(4)]
        own, four = spot.place(kk), spot.base(kk, 2)
        if stage == 0:
            self.send(kk, spot.diagonal(kk, 2), 2, own, 1)
            self.send(kk, spot.partner(kk, 3), 0, own, 1)
            self.send(kk, spot.partner(kk, 2), 1, own, 1)
        elif stage == 1:
            self.arrived(kk, 0, own + flip[3], 1)
            self.arrived(kk, 1, own + flip[2], 1)
            self.arrived(kk, 2, own + flip[2] + flip[3], 1)
            self.send(kk, spot.partner(kk, 1), 3, four, 2)
            self.send(kk, spot.partner(kk, 1), 4, four + 2, 2)
            self.send(kk, spot.partner(kk, 0), 5, four, 4)
            self.pass_on(kk, 0, four, 4)
        elif stage == 2:
            new = four + flip[1]
            for i in range(2):
                self.arrived(kk, 3 + i, new + 2 * i, 2)
                self.send(kk, spot.partner(kk, 0), 6 + i, new + 2 * i, 2)
            self.pass_on(kk, 1, new, 4)
        elif stage == 3:
            new = four + flip[0]
            self.arrived(kk, 5, new, 4)
            self.pass_on(kk, 2, new, 4)
            new = new + flip[1]
            for i in range(2):
                self.arrived(kk, 6 + i, new + 2 * i, 2)
                self.pass_on(kk, 3 + i, new + 2 * i, 2)
        else:
            other = 1 - spot.c
            four = spot.sib_base(kk, 2)
            over_1 = four + 4 * (1 - 2 * spot.sib_bit(kk, 1))
            over_0 = 8 * (1 - 2 * spot.sib_bit(kk, 0))
            last = over_1 + over_0
            pieces = ((four, 4), (over_1, 4), (four + over_0, 4), (last, 2), (last + 2, 2))
            for idx, (off, n) in enumerate(pieces):
                wait_bytes(self.view(kk, off, n, other), self.sib_recv.at[kk, idx])

    def finish(self):
        for kk in range(2):
            wait_bytes(self.full.at[kk, pl.ds(0, 15)], self.xy_send.at[kk])
            wait_bytes(self.full.at[kk], self.sib_send.at[kk])


def block_place(k, chip):
    xu, xv = ring_bits(chip % 4)
    yu, yv = ring_bits(chip // 4)
    bits = (xu, yu, xv, yv)
    return sum(bits[(k + s) % 4] * (8 >> s) for s in range(4))


def slice_columns(kk, core):
    return pl.ds(pl.multiple_of((2 * core + kk) * SLICE, SLICE), SLICE)


def lay_out(full, out, kk, core):
    for chip in range(CHIPS):
        low, high = block_place(kk, chip), block_place(2 + kk, chip)
        out[16 * chip : 16 * chip + 16, slice_columns(kk, core)] = full[2 * core + kk, low + (high - low) * core]


REDUCE_SCRATCH = [
    pltpu.VMEM((4, 16, 16, SLICE), BF16),
    pltpu.VMEM((2, 16, 16, SLICE), BF16),
    pltpu.VMEM((2, 15, 16, SLICE), BF16),
    pltpu.VMEM((8, 8, BLOCK), BF16),
    pltpu.VMEM((8, 8, BLOCK), BF16),
    pltpu.VMEM((2, 1, 128), F32),
    pltpu.VMEM((9, 1, 128), F32),
    pltpu.SemaphoreType.DMA((2,)),
    pltpu.SemaphoreType.DMA((2, 2)),
    pltpu.SemaphoreType.DMA((2,)),
    pltpu.SemaphoreType.DMA((2, 7)),
    pltpu.SemaphoreType.DMA((6,)),
]


class Reduce:
    def __init__(self, spot, scratch):
        self.spot = spot
        (
            self.partial,
            self.from_sib,
            self.from_xy,
            self.to_col,
            self.from_col,
            self.inner_to,
            self.inner_from,
            self.sib_send,
            self.sib_recv,
            self.xy_send,
            self.xy_recv,
            self.col_sems,
        ) = scratch

    def sib_copy(self, kk, sub, core, bit):
        half = (1 - sub) * (1 - bit) + sub * bit
        return remote(
            self.partial.at[2 * core + kk, pl.ds(half * 8, 8)],
            self.from_sib.at[kk, pl.ds(half * 8, 8)],
            self.sib_send.at[kk],
            self.sib_recv.at[kk, sub],
            self.spot.sibling(),
        )

    def start(self, kk, sub):
        self.sib_copy(kk, sub, 1 - self.spot.c, self.spot.sib_bit(kk, 0)).start()

    def from_sibling(self, kk, sub):
        self.sib_copy(kk, sub, self.spot.c, self.spot.bit(kk, 0)).wait_recv()

    def add(self, kk, off, ref, ref_off, n):
        k = 2 * self.spot.c + kk

        def body(i, carry):
            self.partial[k, off + i] = self.partial[k, off + i] + ref[kk, ref_off + i]
            return carry

        if n == 1:
            body(0, 0)
        else:
            lax.fori_loop(0, n, body, 0)

    def plan(self, kk, s):
        n = 8 >> s
        landing = 16 - 2 * n
        bit = self.spot.bit(kk, s)
        gone = self.spot.base(kk, s) + (1 - bit) * n
        kept = self.spot.base(kk, s) + bit * n
        half = n // 2
        after = self.spot.bit(kk, s + 1)
        pieces = []
        for sub in range(2):
            shift = ((1 - after) if sub == 0 else after) * half
            pieces.append((gone + shift, kept + shift, landing + sub * half, half, 2 * s + sub))
        return pieces

    def xy_copy(self, kk, s, piece):
        gone, _, landing, n, idx = piece
        return remote(
            self.partial.at[2 * self.spot.c + kk, pl.ds(gone, n)],
            self.from_xy.at[kk, pl.ds(landing, n)],
            self.xy_send.at[kk],
            self.xy_recv.at[kk, idx],
            self.spot.partner(kk, s),
        )

    def xy_start(self, kk, s, piece):
        self.xy_copy(kk, s, piece).start()

    def plane(self, own_part, beside):
        spot = self.spot

        def first(kk):
            self.from_sibling(kk, 0)
            for piece in self.plan(kk, 0):
                self.add(kk, piece[0], self.from_sib, piece[0], piece[3])
                self.xy_start(kk, 0, piece)

        def kept(kk):
            self.from_sibling(kk, 1)
            self.add(kk, spot.bit(kk, 0) * 8, self.from_sib, spot.bit(kk, 0) * 8, 8)

        def arrive(kk, s, sub):
            piece = self.plan(kk, s)[sub]
            self.xy_copy(kk, s, piece).wait_recv()
            self.add(kk, piece[1], self.from_xy, piece[2], piece[3])

        def second(kk):
            arrive(kk, 0, 0)
            for follow in self.plan(kk, 1):
                self.xy_start(kk, 1, follow)

        def third(kk):
            arrive(kk, 1, 0)
            by_2 = spot.place(kk) + 2 * (1 - 2 * spot.bit(kk, 2))
            self.tail_copy(kk, by_2 + 1 - 2 * spot.bit(kk, 3), 2, spot.diagonal(kk, 2)).start()
            self.tail_copy(kk, by_2, 0, spot.partner(kk, 2)).start()

        def fourth(kk):
            arrive(kk, 1, 1)
            own = spot.place(kk)
            self.tail_copy(kk, own + 1 - 2 * spot.bit(kk, 3), 1, spot.partner(kk, 3)).start()

        for kk in range(2):
            own_part(kk, 0)
            first(kk)
        for kk in range(2):
            own_part(kk, 1)
        for kk in range(2):
            kept(kk)
        for work in beside.get(-1, ()):
            work()
        for kk in range(2):
            second(kk)
        for kk in range(2):
            arrive(kk, 0, 1)
        for work in beside.get(0, ()):
            work()
        for kk in range(2):
            third(kk)
        for kk in range(2):
            fourth(kk)
        for work in beside.get(1, ()):
            work()
        places = [spot.place(kk) for kk in range(2)]
        sums = []
        for kk in range(2):
            total = self.partial[2 * spot.c + kk, places[kk]].astype(F32)
            for i in range(3):
                self.tail_copy(kk, places[kk], i, spot.sibling()).wait_recv()
                total = total + self.from_xy[kk, 12 + i].astype(F32)
            sums.append(total)
        return sums

    def tail_copy(self, kk, block, i, target):
        return remote(
            self.partial.at[2 * self.spot.c + kk, pl.ds(block, 1)],
            self.from_xy.at[kk, pl.ds(12 + i, 1)],
            self.xy_send.at[kk],
            self.xy_recv.at[kk, 4 + i],
            target,
        )

    def column(self, sums, raw, gain, scale, beside=()):
        spot = self.spot
        for kk in range(2):
            for j in range(2):
                for core in range(2):
                    part = sums[kk][8 * core : 8 * core + 8, j * BLOCK : (j + 1) * BLOCK]
                    self.to_col[2 * (2 * kk + j) + core] = part.astype(BF16)

        def to_column(zz):
            zdst = 4 * spot.c + zz
            for core in range(2):
                mine = jnp.logical_and(zdst == spot.z, spot.c == core)

                @pl.when(jnp.logical_not(mine))
                def _(core=core):
                    remote(
                        self.to_col.at[2 * zz + core],
                        self.from_col.at[spot.z],
                        self.col_sems.at[0],
                        self.col_sems.at[1],
                        (spot.chip * 2 + core, zdst),
                    ).start()

                @pl.when(mine)
                def _(core=core):
                    self.from_col[spot.z] = self.to_col[2 * zz + core]

        loop(0, 4, to_column)
        row = lax.broadcasted_iota(jnp.int32, (8, 128), 0)
        diagonal = row == lax.broadcasted_iota(jnp.int32, (8, 128), 1)
        for core in range(2):
            total = jnp.zeros((8, BLOCK), F32)
            for kk in range(2):
                for j in range(2):
                    zb = 4 * spot.c + 2 * kk + j
                    part = sums[kk][8 * core : 8 * core + 8, j * BLOCK : (j + 1) * BLOCK]
                    total = total + raw[8 * core + zb].astype(F32) * gain[zb] * part
            inner = jnp.where(diagonal, jnp.sum(total, axis=1, keepdims=True), 0.0)
            self.inner_to[core] = jnp.sum(inner, axis=0, keepdims=True)
        to_sibling = remote(
            self.inner_to.at[1 - spot.c],
            self.inner_from.at[8],
            self.col_sems.at[4],
            self.col_sems.at[5],
            spot.sibling(),
        )
        to_sibling.start()
        to_sibling.wait_recv()
        self.inner_from[0] = self.inner_to[spot.c] + self.inner_from[8]
        loop(
            1,
            8,
            lambda up: remote(
                self.inner_from.at[0],
                self.inner_from.at[up],
                self.col_sems.at[2],
                self.col_sems.at[3],
                spot.column_peer(up),
            ).start(),
        )
        for work in beside:
            work()
        own = raw[8 * spot.c + spot.z].astype(F32)
        own_gain = gain[spot.z]
        wait_column(spot, self.from_col, self.col_sems.at[1])
        grad = jnp.zeros((8, BLOCK), F32)
        for zsrc in range(8):
            grad = grad + self.from_col[zsrc].astype(F32)
        wait_bytes(self.inner_from.at[pl.ds(1, 7)], self.col_sems.at[3])
        inner = jnp.zeros((1, 128), F32)
        for i in range(8):
            inner = inner + self.inner_from[i]
        inner = jnp.sum(jnp.where(diagonal, inner, 0.0), axis=1, keepdims=True) / D
        return scale * own_gain * grad - own * (scale * scale * scale) * inner

    def finish(self):
        for kk in range(2):
            wait_bytes(self.partial.at[kk], self.sib_send.at[kk])
            wait_bytes(self.partial.at[kk, pl.ds(0, 15)], self.xy_send.at[kk])
        wait_column(self.spot, self.to_col, self.col_sems.at[0])
        wait_bytes(self.inner_from.at[pl.ds(1, 7)], self.col_sems.at[2])
        wait_bytes(self.inner_from.at[pl.ds(8, 1)], self.col_sems.at[4])


def wait_column(spot, ref, sem):
    own = spot.half == spot.c

    @pl.when(own)
    def _():
        wait_bytes(ref.at[pl.ds(0, 7)], sem)

    @pl.when(jnp.logical_not(own))
    def _():
        wait_bytes(ref, sem)


def program(
    layer_out,
    resid_mid,
    final_gain,
    mlp_gain,
    teacher_in,
    assign,
    lengths,
    token_ids,
    head_hbm,
    gate_hbm,
    up_hbm,
    down_hbm,
    grad_first,
    grad_second,
    final_rows,
    normed,
    grad_rows,
    dlog_t,
    hidden_t,
    activated_t,
    head,
    w_gate_up,
    w_down,
    dlog,
    dlog_turned,
    hidden_turned,
    raw_out,
    raw_mid,
    full_out,
    full_mid,
    full_grad,
    packed,
    got,
    logits_ref,
    diff_ref,
    gate_up_pre,
    act_grad,
    first,
    second,
    stats_pad,
    own_b,
    own_from,
    scale_ref,
    load_sem,
    raw_sems,
    plane_sems,
    stat_sems,
    own_sems,
    xy_send,
    xy_recv,
    sib_send,
    sib_recv,
    *scratch,
):
    spot = Spot()
    c, other = spot.c, 1 - spot.c
    loads = [
        pltpu.make_async_copy(src, dst, load_sem.at[i])
        for i, (src, dst) in enumerate(
            (
                (head_hbm, head),
                (gate_hbm, w_gate_up.at[pl.ds(0, 64)]),
                (up_hbm, w_gate_up.at[pl.ds(64, 64)]),
                (down_hbm, w_down),
            )
        )
    ]
    for load in loads:
        load.start()
    reduces = [Reduce(spot, scratch[: len(REDUCE_SCRATCH)]), Reduce(spot, scratch[len(REDUCE_SCRATCH) :])]
    gathers = [
        Gather(spot, full, xy_send.at[a], xy_recv.at[a], sib_send.at[a], sib_recv.at[a])
        for a, full in enumerate((full_out, full_mid, full_grad))
    ]
    gather_out, gather_mid, gather_grad = gathers

    greet(spot)
    mine = 8 * c + spot.z
    raw_out[mine] = layer_out[...]
    raw_mid[mine] = resid_mid[...]

    greeted()

    def send_raw(a, own, raw):
        loop(
            1,
            8,
            lambda up: remote(
                own, raw.at[mine], raw_sems.at[a, 0], raw_sems.at[a, 1], spot.column_peer(up)
            ).start(),
        )

    def pass_raw(a, raw):
        wait_bytes(raw.at[pl.ds(0, 7)], raw_sems.at[a, 1])
        rows = raw.at[pl.ds(8 * c, 8)]
        remote(rows, rows, raw_sems.at[a, 2], raw_sems.at[a, 3], spot.sibling()).start()

    def plane_start(i, carry):
        peer = wrap(spot.d + i, 32)
        remote(packed.at[peer], got.at[spot.d], plane_sems.at[0], plane_sems.at[1], (peer, spot.z)).start()
        return carry

    def normalise(a, raw, full, gain):
        wait_bytes(raw.at[pl.ds(0, 8)], raw_sems.at[a, 3])
        scales = [row_scale(raw, core) for core in range(2)]
        for kk in range(2):
            place = spot.place(kk)
            for j in range(2):
                zb = 4 * c + 2 * kk + j
                rows = jnp.concatenate(
                    [raw[8 * core + zb].astype(F32) * scales[core] * gain[zb] for core in range(2)], axis=0
                )
                full[2 * c + kk, place, :, j * BLOCK : (j + 1) * BLOCK] = rows.astype(BF16)
        for core in range(2):
            scale_ref[a, core] = jnp.broadcast_to(scales[core], (8, 128))

    def both(gather, stage):
        for kk in range(2):
            gather.step(stage, kk)

    send_raw(0, layer_out, raw_out)

    row = lax.broadcasted_iota(jnp.int32, (8, 1), 0)
    order = jnp.zeros((8, 1), jnp.int32)
    for r in range(8):
        order = jnp.where(row == r, assign[0, r], order)

    def pack(peer):
        rows = teacher_in[:, pl.ds(pl.multiple_of(peer * 384, 384), 384)].astype(F32)
        picked = jnp.zeros((8, 384), F32)
        for r in range(8):
            picked = picked + jnp.where(order == r, rows[r : r + 1, :], 0.0)
        packed[peer] = picked.astype(BF16)

    loop(0, 32, pack)
    got[spot.d] = packed[spot.d]

    token = lax.broadcasted_iota(jnp.int32, (1, 256), 1)
    own_ids = jnp.full((1, 256), -1, jnp.int32)
    own_lengths = jnp.zeros((1, 256), jnp.int32)
    for r in range(8):
        here = token == 8 * spot.d + r
        own_ids = jnp.where(here, token_ids[r], own_ids)
        own_lengths = jnp.where(here, lengths[0, r // SLOT], own_lengths)
    live = (lax.rem(token, SLOT) < own_lengths).astype(jnp.int32)
    codes = jnp.where(own_ids >= 0, 2 * own_ids + live, 0).astype(F32)

    lax.fori_loop(1, 14, plane_start, 0)
    send_raw(1, resid_mid, raw_mid)
    pass_raw(0, raw_out)
    normalise(0, raw_out, full_out, final_gain)
    both(gather_out, 0)
    lax.fori_loop(14, 32, plane_start, 0)
    both(gather_out, 1)
    pass_raw(1, raw_mid)
    both(gather_out, 2)
    normalise(1, raw_mid, full_mid, mlp_gain)
    both(gather_out, 3)
    both(gather_mid, 0)

    def products(left, right, out, core):
        def body(kk):
            columns = slice_columns(kk, core)
            out[...] += contract_cols(left[:, columns], right[:, columns])

        loop(0, 2, body)

    for kk in range(2):
        lay_out(full_out, final_rows, kk, c)
    loads[0].wait()
    logits_ref[...] = jnp.zeros_like(logits_ref)
    products(final_rows, head, logits_ref, c)
    both(gather_mid, 1)
    both(gather_out, 4)
    for kk in range(2):
        lay_out(full_out, final_rows, kk, other)
    products(final_rows, head, logits_ref, other)

    wait_bytes(got.at[pl.ds(0, 31)], plane_sems.at[1])
    logits = logits_ref[...]
    diff = logits - got[...].astype(F32).reshape(256, 384)
    local_max = jnp.max(logits, axis=1, keepdims=True)
    expd = jnp.exp(logits - local_max)
    total = jnp.sum(expd, axis=1, keepdims=True)
    moment = jnp.sum(expd * diff, axis=1, keepdims=True)
    logits_ref[...] = expd
    diff_ref[...] = diff
    lanes = lax.broadcasted_iota(jnp.int32, (256, 128), 1)
    columns = jnp.where(lanes == 0, local_max, jnp.where(lanes == 1, total, moment))
    first[0] = jnp.transpose(columns)[0:4]
    first[0, 3:4] = codes
    remote(first.at[0], first.at[1], stat_sems.at[0], stat_sems.at[1], spot.sibling()).start()

    def to_column(up):
        for flip in range(2):
            target = spot.column_peer(up, flip)
            remote(first.at[0], first.at[2 * up + flip], stat_sems.at[0], stat_sems.at[1], target).start()

    loop(1, 8, to_column)
    both(gather_mid, 2)

    def combine(ref, groups):
        top = ref[0, 0:1]
        for i in range(1, 16):
            top = jnp.maximum(top, ref[i, 0:1])
        total = jnp.zeros_like(top)
        moment = jnp.zeros_like(top)
        for i in range(16):
            weight = jnp.exp(ref[i, 0:1] - top)
            total = total + ref[i, 1:2] * weight
            moment = moment + ref[i, 2:3] * weight
        return jnp.concatenate([top, total, moment, sum(ref[i, 3:4] for i in range(groups))], axis=0)

    wait_bytes(first.at[pl.ds(1, 15)], stat_sems.at[1])
    second[0] = combine(first, 2)

    def to_plane(i):
        target = (wrap(spot.chip + i, CHIPS) * 2 + c, spot.z)
        remote(second.at[0], second.at[i], stat_sems.at[2], stat_sems.at[3], target).start()

    loop(1, CHIPS, to_plane)
    both(gather_mid, 3)
    vocab = lax.broadcasted_iota(jnp.int32, (256, 384), 1) + (spot.z * 32 + spot.d) * 384
    stats_pad[...] = jnp.zeros_like(stats_pad)
    wait_bytes(second.at[pl.ds(1, 15)], stat_sems.at[3])
    stats_pad[0:4] = combine(second, 16)
    columns = jnp.transpose(stats_pad[...])
    global_max, totals, moments = columns[:, 0:1], columns[:, 1:2], columns[:, 2:3]
    code = columns[:, 3:4].astype(jnp.int32)
    ids_all = code >> 1
    live_mask = (code - 2 * ids_all).astype(F32)
    token_weight = live_mask * (LOSS_SCALE / jnp.sum(live_mask, axis=0, keepdims=True))
    share = token_weight * (jnp.exp(local_max - global_max) / totals)
    shift = CE_WEIGHT - moments / totals
    dlogits = share * logits_ref[...] * (diff_ref[...] + shift)
    dlogits = dlogits - jnp.where(ids_all == vocab, CE_WEIGHT * token_weight, 0.0)

    def turn(rows, out):
        for k in range(4):
            for chip in range(CHIPS):
                place = 16 * block_place(k, chip)
                out[k, place : place + 16, :] = rows[16 * chip : 16 * chip + 16]

    def spread(reduce, kk, core, half, left, right):
        k = 2 * core + kk
        rows = left[k, pl.ds(pl.multiple_of(half * 128, 128), 128)]
        part = jnp.dot(rows, right[:, slice_columns(kk, core)], preferred_element_type=F32).astype(BF16)
        reduce.partial[k, pl.ds(half * 8, 8)] = part.reshape(8, 16, SLICE)

    def send_partial(reduce, left, right):

        def to_sibling(i):
            sub = jnp.where(i >= 2, 1, 0)
            kk = i - 2 * sub
            bit = spot.sib_bit(kk, 0)
            spread(reduce, kk, other, (1 - sub) * (1 - bit) + sub * bit, left, right)
            reduce.start(kk, sub)

        loop(0, 4, to_sibling)

        def own_part(kk, sub):
            bit = spot.bit(kk, 0)
            spread(reduce, kk, c, (1 - bit) if sub == 0 else bit, left, right)

        return own_part

    dlog_b = dlogits.astype(BF16)
    turn(dlog_b, dlog_turned)
    dlog[...] = dlog_b

    def mid_rows(core):
        for kk in range(2):
            lay_out(full_mid, normed, kk, core)

    def mid_first():
        for load in loads[1:]:
            load.wait()
        gate_up_pre[...] = jnp.zeros_like(gate_up_pre)
        act_grad[...] = jnp.zeros_like(act_grad)
        mid_rows(c)
        products(w_gate_up, normed, gate_up_pre, c)

    def mid_second():
        both(gather_mid, 4)
        mid_rows(other)
        products(w_gate_up, normed, gate_up_pre, other)

    def activate():
        gate, up = gate_up_pre[0:64], gate_up_pre[64:128]
        gate_sigmoid = jax.nn.sigmoid(gate)
        activated_t[...] = (gate * gate_sigmoid * up).astype(BF16)
        gate_up_pre[0:64] = up * gate_sigmoid * (1.0 + gate * (1.0 - gate_sigmoid))
        gate_up_pre[64:128] = gate * gate_sigmoid

    def turn_dlog():
        dlog_t[...] = jnp.transpose(dlog[...].astype(F32)).astype(BF16)

    own_part = send_partial(reduces[0], dlog_turned, head)
    sums = reduces[0].plane(own_part, {-1: [turn_dlog]})
    grad_out = reduces[0].column(sums, raw_out, final_gain, scale_ref[0, c][:, 0:1], [mid_first])
    own_b[...] = grad_out.astype(BF16)
    grad_first[...] = grad_out

    target_core = spot.half
    own_place = spot.z_low * 2 + c

    def own_to_column(zdst):
        mine = jnp.logical_and(spot.z == zdst, target_core == c)

        @pl.when(jnp.logical_not(mine))
        def _():
            target = (spot.chip * 2 + target_core, zdst)
            remote(own_b, own_from.at[own_place], own_sems.at[0], own_sems.at[1], target).start()

        @pl.when(mine)
        def _():
            own_from[own_place] = own_b[...]

    loop(0, 8, own_to_column)
    mid_second()
    activate()
    wait_column(spot, own_from, own_sems.at[1])
    for kk in range(2):
        for j in range(2):
            zz = 2 * kk + j
            rows = jnp.concatenate([own_from[2 * zz + core].astype(F32) for core in range(2)], axis=0)
            full_grad[2 * c + kk, spot.place(kk), :, j * BLOCK : (j + 1) * BLOCK] = rows.astype(BF16)
    both(gather_grad, 0)
    for stage in range(1, 4):
        both(gather_grad, stage)
    for kk in range(2):
        lay_out(full_grad, grad_rows, kk, c)
    products(w_down, grad_rows, act_grad, c)
    both(gather_grad, 4)
    for kk in range(2):
        lay_out(full_grad, grad_rows, kk, other)
    products(w_down, grad_rows, act_grad, other)

    act = act_grad[...]
    both_grads = jnp.concatenate([act * gate_up_pre[0:64], act * gate_up_pre[64:128]], axis=0)
    turn(jnp.transpose(both_grads).astype(BF16), hidden_turned)
    hidden_t[...] = both_grads.astype(BF16)
    own_part = send_partial(reduces[1], hidden_turned, w_gate_up)

    def left_earlier():
        for a in range(2):
            wait_bytes(raw_out.at[pl.ds(0, 7)], raw_sems.at[a, 0])
            wait_bytes(raw_out.at[pl.ds(0, 8)], raw_sems.at[a, 2])
        wait_bytes(got.at[pl.ds(0, 31)], plane_sems.at[0])
        wait_bytes(first.at[pl.ds(1, 15)], stat_sems.at[0])
        wait_bytes(second.at[pl.ds(1, 15)], stat_sems.at[2])
        for gather in gathers:
            gather.finish()
        reduces[0].finish()
        wait_column(spot, own_from, own_sems.at[0])

    sums = reduces[1].plane(own_part, {})
    grad_second[...] = reduces[1].column(sums, raw_mid, mlp_gain, scale_ref[1, c][:, 0:1], [left_earlier])
    reduces[1].finish()


def weight_grads(
    grad_first,
    grad_second,
    dlog_t,
    hidden_t,
    activated_t,
    final_rows,
    normed,
    grad_rows,
    grad_resid,
    grad_head,
    grad_gate,
    grad_up,
    grad_down,
    head_rows,
    gate_up_rows,
    down_rows,
    sems,
):
    def product(left, right):
        return jnp.dot(left, right, preferred_element_type=F32).astype(BF16)

    grad_resid[...] = (grad_first[...] + grad_second[...]).astype(BF16)

    def copies(k):
        place = pl.ds(pl.multiple_of(k * SLICE, SLICE), SLICE)
        return [
            pltpu.make_async_copy(head_rows.at[:, place], grad_head.at[:, place], sems.at[0, k]),
            pltpu.make_async_copy(gate_up_rows.at[pl.ds(0, 64), place], grad_gate.at[:, place], sems.at[1, k]),
            pltpu.make_async_copy(gate_up_rows.at[pl.ds(64, 64), place], grad_up.at[:, place], sems.at[2, k]),
            pltpu.make_async_copy(down_rows.at[:, place], grad_down.at[:, place], sems.at[3, k]),
        ]

    def chunk(k):
        place = pl.ds(pl.multiple_of(k * SLICE, SLICE), SLICE)
        to_head, to_gate, to_up, to_down = copies(k)
        head_rows[:, place] = product(dlog_t[...], final_rows[:, place])
        to_head.start()
        gate_up_rows[:, place] = product(hidden_t[...], normed[:, place])
        to_gate.start()
        to_up.start()
        down_rows[:, place] = product(activated_t[...], grad_rows[:, place])
        to_down.start()

    def done(k):
        for copy in copies(k):
            copy.wait()

    loop(0, 4, chunk)
    loop(0, 4, done)


def shape(dims, dtype):
    return jax.ShapeDtypeStruct(dims, dtype)


def per_device(
    layer_out,
    resid_mid,
    final_gain,
    mlp_gain,
    head_weight,
    w_gate,
    w_up,
    w_down,
    teacher_logits,
    assign,
    lengths,
    token_ids,
):
    final_gain = final_gain.reshape(8, 1, BLOCK)
    mlp_gain = mlp_gain.reshape(8, 1, BLOCK)
    vmem = pl.BlockSpec(memory_space=pltpu.VMEM)
    smem = pl.BlockSpec(memory_space=pltpu.SMEM)
    hbm = pl.BlockSpec(memory_space=pl.ANY)
    full = pltpu.VMEM((4, 16, 16, SLICE), BF16)
    rows = pltpu.VMEM((256, D), BF16)
    dma = pltpu.SemaphoreType.DMA
    shared = pl.pallas_call(
        program,
        out_shape=[
            pltpu.VMEM((8, BLOCK), F32),
            pltpu.VMEM((8, BLOCK), F32),
            rows,
            rows,
            rows,
            pltpu.VMEM((384, 256), BF16),
            pltpu.VMEM((128, 256), BF16),
            pltpu.VMEM((64, 256), BF16),
        ],
        in_specs=[vmem] * 5 + [smem] * 3 + [hbm] * 4,
        out_specs=[vmem] * 8,
        scratch_shapes=[
            pltpu.VMEM((384, D), BF16),
            pltpu.VMEM((128, D), BF16),
            pltpu.VMEM((64, D), BF16),
            pltpu.VMEM((256, 384), BF16),
            pltpu.VMEM((4, 256, 384), BF16),
            pltpu.VMEM((4, 256, 128), BF16),
            pltpu.VMEM((16, 8, BLOCK), BF16),
            pltpu.VMEM((16, 8, BLOCK), BF16),
            full,
            full,
            full,
            pltpu.VMEM((32, 8, 384), BF16),
            pltpu.VMEM((32, 8, 384), BF16),
            pltpu.VMEM((256, 384), F32),
            pltpu.VMEM((256, 384), F32),
            pltpu.VMEM((128, 256), F32),
            pltpu.VMEM((64, 256), F32),
            pltpu.VMEM((16, 4, 256), F32),
            pltpu.VMEM((16, 4, 256), F32),
            pltpu.VMEM((128, 256), F32),
            pltpu.VMEM((8, BLOCK), BF16),
            pltpu.VMEM((8, 8, BLOCK), BF16),
            pltpu.VMEM((2, 2, 8, 128), F32),
            dma((4,)),
            dma((2, 4)),
            dma((2,)),
            dma((4,)),
            dma((2,)),
            dma((3, 2)),
            dma((3, 2, 8)),
            dma((3, 2)),
            dma((3, 2, 5)),
        ]
        + REDUCE_SCRATCH
        + REDUCE_SCRATCH,
        compiler_params=pltpu.CompilerParams(
            collective_id=0, has_side_effects=True, vmem_limit_bytes=VMEM_LIMIT
        ),
        name="backward",
    )(
        layer_out,
        resid_mid,
        final_gain,
        mlp_gain,
        teacher_logits,
        assign,
        lengths,
        token_ids,
        head_weight,
        w_gate,
        w_up,
        w_down,
    )
    return pl.pallas_call(
        weight_grads,
        out_shape=[
            shape((8, BLOCK), BF16),
            shape(head_weight.shape, BF16),
            shape(w_gate.shape, BF16),
            shape(w_up.shape, BF16),
            shape(w_down.shape, BF16),
        ],
        in_specs=[vmem] * 8,
        out_specs=[vmem] + [hbm] * 4,
        scratch_shapes=[
            pltpu.VMEM((384, D), BF16),
            pltpu.VMEM((128, D), BF16),
            pltpu.VMEM((64, D), BF16),
            dma((4, 4)),
        ],
        compiler_params=pltpu.CompilerParams(vmem_limit_bytes=GRADS_VMEM),
        cost_estimate=pl.CostEstimate(flops=2 * 256 * 576 * D, bytes_accessed=2 * 576 * D, transcendentals=0),
        name="weight_grads",
    )(shared[0], shared[1], shared[5], shared[6], shared[7], shared[2], shared[3], shared[4])


def solution(mesh):
    return jax.shard_map(
        per_device,
        mesh=mesh,
        in_specs=(
            P("dp", "tensor"),
            P("dp", "tensor"),
            P(),
            P(),
            P(("tensor", "dp"), None),
            P(("tensor", "dp"), None),
            P(("tensor", "dp"), None),
            P(("tensor", "dp"), None),
            P("dp", "tensor"),
            P("dp", None),
            P("dp", None),
            P("dp"),
        ),
        out_specs=(
            P("dp", "tensor"),
            P(("tensor", "dp"), None),
            P(("tensor", "dp"), None),
            P(("tensor", "dp"), None),
            P(("tensor", "dp"), None),
        ),
        check_vma=False,
    )
```

```python
import jax
import jax.numpy as jnp
from jax import lax
from jax.experimental import pallas as pl
from jax.experimental.pallas import tpu as pltpu
from jax.sharding import PartitionSpec as P

D = 5120
SLOT = 4
EPS = 1e-06
CE_WEIGHT = 0.5
LOSS_SCALE = 4096.0

BLOCK = 640
SLICE = 1280
CHIPS = 16
F32 = jnp.float32
BF16 = jnp.bfloat16
VMEM_LIMIT = 52 * 1024 * 1024
GRADS_VMEM = 20 * 1024 * 1024


def contract_cols(left, right):
    return lax.dot_general(left, right, (((1,), (1,)), ((), ())), preferred_element_type=F32)


def wrap(v, size):
    return jnp.where(v >= size, v - size, v)


def ring_bits(v):
    high = v // 2
    return v % 2 + high - 2 * (v % 2) * high, high


class Spot:
    def __init__(self):
        self.d = lax.axis_index("dp")
        self.z = lax.axis_index("tensor")
        self.chip = lax.div(self.d, 2)
        self.c = self.d - 2 * self.chip
        self.y = lax.div(self.chip, 4)
        self.x = self.chip - 4 * self.y
        c, other = self.c, 1 - self.c
        xv, yv = lax.div(self.x, 2), lax.div(self.y, 2)
        x_low, y_low = self.x - 2 * xv, self.y - 2 * yv
        xu, yu = x_low + xv - 2 * x_low * xv, y_low + yv - 2 * y_low * yv
        x_near, y_near = self.x + 1 - 2 * x_low, self.y + 1 - 2 * y_low
        x_far, y_far = 3 - self.x, 3 - self.y
        self.half = lax.div(self.z, 4)
        self.z_low = self.z - 4 * self.half
        bits = (xu, yu, xv, yv)
        moved = (x_near, y_near, x_far, y_far)
        self.own_bits = [bits[i] * other + bits[(i + 2) % 4] * c for i in range(4)]
        self.sib_bits = [bits[i] * c + bits[(i + 2) % 4] * other for i in range(4)]
        moved = [moved[i] * other + moved[(i + 2) % 4] * c for i in range(4)]
        self.chips = [self.y * 4 + moved[i] if i % 2 == 0 else moved[i] * 4 + self.x for i in range(4)]
        corner = []
        for i in range(4):
            j = (i + 1) % 4
            corner.append(moved[j] * 4 + moved[i] if i % 2 == 0 else moved[i] * 4 + moved[j])
        self.corners = corner

    def pick(self, values, kk, s):
        if isinstance(kk, int):
            return values[(kk + s) % 4]
        first, second = values[s % 4], values[(s + 1) % 4]
        return first + (second - first) * kk

    def bit(self, kk, s):
        return self.pick(self.own_bits, kk, s)

    def sib_bit(self, kk, s):
        return self.pick(self.sib_bits, kk, s)

    def base(self, kk, s):
        return sum((self.bit(kk, i) * (8 >> i) for i in range(s)), jnp.int32(0))

    def sib_base(self, kk, s):
        return sum((self.sib_bit(kk, i) * (8 >> i) for i in range(s)), jnp.int32(0))

    def place(self, kk):
        return self.base(kk, 4)

    def partner(self, kk, s):
        return (self.pick(self.chips, kk, s) * 2 + self.c, self.z)

    def diagonal(self, kk, s):
        return (self.pick(self.corners, kk, s) * 2 + self.c, self.z)

    def sibling(self):
        return (self.chip * 2 + 1 - self.c, self.z)

    def column_peer(self, up, flip=0):
        core = self.c if flip == 0 else 1 - self.c
        return (self.chip * 2 + core, wrap(self.z + up, 8))


def greet(spot):
    barrier = pltpu.get_barrier_semaphore()
    mesh = pl.DeviceIdType.MESH
    pl.semaphore_signal(barrier, inc=1, device_id=spot.sibling(), device_id_type=mesh)

    def column(up, carry):
        for flip in range(2):
            pl.semaphore_signal(barrier, inc=1, device_id=spot.column_peer(up, flip), device_id_type=mesh)
        return carry

    lax.fori_loop(1, 8, column, 0)

    def body(j, carry):
        chip = wrap(spot.chip + j, CHIPS)
        for core in range(2):
            pl.semaphore_signal(
                barrier, inc=1, device_id=(chip * 2 + core, spot.z), device_id_type=pl.DeviceIdType.MESH
            )
        return carry

    lax.fori_loop(1, CHIPS, body, 0)


def greeted():
    pl.semaphore_wait(pltpu.get_barrier_semaphore(), 45)


def remote(src, dst, send_sem, recv_sem, target):
    return pltpu.make_async_remote_copy(
        src_ref=src,
        dst_ref=dst,
        send_sem=send_sem,
        recv_sem=recv_sem,
        device_id=target,
        device_id_type=pl.DeviceIdType.MESH,
    )


def row_scale(raw, core):
    total = jnp.zeros((8, BLOCK), F32)
    for zb in range(8):
        part = raw[8 * core + zb].astype(F32)
        total = total + part * part
    return lax.rsqrt(jnp.sum(total, axis=1, keepdims=True) / D + EPS)


def loop(start, stop, body):
    def step(i, carry):
        body(i)
        return carry

    lax.fori_loop(start, stop, step, 0)


def wait_bytes(ref, sem):
    pltpu.make_async_copy(ref, ref, sem).wait()


class Gather:
    def __init__(self, spot, full, xy_send, xy_recv, sib_send, sib_recv):
        self.spot, self.full = spot, full
        self.xy_send, self.xy_recv, self.sib_send, self.sib_recv = xy_send, xy_recv, sib_send, sib_recv

    def view(self, kk, off, n, core=None):
        core = self.spot.c if core is None else core
        return self.full.at[2 * core + kk, pl.ds(off, n)]

    def send(self, kk, target, idx, off, n):
        view = self.view(kk, off, n)
        remote(view, view, self.xy_send.at[kk], self.xy_recv.at[kk, idx], target).start()

    def arrived(self, kk, idx, off, n):
        wait_bytes(self.view(kk, off, n), self.xy_recv.at[kk, idx])

    def pass_on(self, kk, idx, off, n):
        view = self.view(kk, off, n)
        remote(view, view, self.sib_send.at[kk], self.sib_recv.at[kk, idx], self.spot.sibling()).start()

    def step(self, stage, kk):
        spot = self.spot
        flip = [(8 >> s) * (1 - 2 * spot.bit(kk, s)) for s in range(4)]
        own, four = spot.place(kk), spot.base(kk, 2)
        if stage == 0:
            self.send(kk, spot.diagonal(kk, 2), 2, own, 1)
            self.send(kk, spot.partner(kk, 3), 0, own, 1)
            self.send(kk, spot.partner(kk, 2), 1, own, 1)
        elif stage == 1:
            self.arrived(kk, 0, own + flip[3], 1)
            self.arrived(kk, 1, own + flip[2], 1)
            self.arrived(kk, 2, own + flip[2] + flip[3], 1)
            self.send(kk, spot.partner(kk, 1), 3, four, 2)
            self.send(kk, spot.partner(kk, 1), 4, four + 2, 2)
            self.send(kk, spot.partner(kk, 0), 5, four, 4)
            self.pass_on(kk, 0, four, 4)
        elif stage == 2:
            new = four + flip[1]
            for i in range(2):
                self.arrived(kk, 3 + i, new + 2 * i, 2)
                self.send(kk, spot.partner(kk, 0), 6 + i, new + 2 * i, 2)
            self.pass_on(kk, 1, new, 4)
        elif stage == 3:
            new = four + flip[0]
            self.arrived(kk, 5, new, 4)
            self.pass_on(kk, 2, new, 4)
            new = new + flip[1]
            for i in range(2):
                self.arrived(kk, 6 + i, new + 2 * i, 2)
                self.pass_on(kk, 3 + i, new + 2 * i, 2)
        else:
            other = 1 - spot.c
            four = spot.sib_base(kk, 2)
            over_1 = four + 4 * (1 - 2 * spot.sib_bit(kk, 1))
            over_0 = 8 * (1 - 2 * spot.sib_bit(kk, 0))
            last = over_1 + over_0
            pieces = ((four, 4), (over_1, 4), (four + over_0, 4), (last, 2), (last + 2, 2))
            for idx, (off, n) in enumerate(pieces):
                wait_bytes(self.view(kk, off, n, other), self.sib_recv.at[kk, idx])

    def finish(self):
        for kk in range(2):
            wait_bytes(self.full.at[kk, pl.ds(0, 15)], self.xy_send.at[kk])
            wait_bytes(self.full.at[kk], self.sib_send.at[kk])


def block_place(k, chip):
    xu, xv = ring_bits(chip % 4)
    yu, yv = ring_bits(chip // 4)
    bits = (xu, yu, xv, yv)
    return sum(bits[(k + s) % 4] * (8 >> s) for s in range(4))


def slice_columns(kk, core):
    return pl.ds(pl.multiple_of((2 * core + kk) * SLICE, SLICE), SLICE)


def lay_out(full, out, kk, core):
    for chip in range(CHIPS):
        low, high = block_place(kk, chip), block_place(2 + kk, chip)
        out[16 * chip : 16 * chip + 16, slice_columns(kk, core)] = full[2 * core + kk, low + (high - low) * core]


REDUCE_SCRATCH = [
    pltpu.VMEM((4, 16, 16, SLICE), BF16),
    pltpu.VMEM((2, 16, 16, SLICE), BF16),
    pltpu.VMEM((2, 15, 16, SLICE), BF16),
    pltpu.VMEM((8, 8, BLOCK), BF16),
    pltpu.VMEM((8, 8, BLOCK), BF16),
    pltpu.VMEM((2, 1, 128), F32),
    pltpu.VMEM((9, 1, 128), F32),
    pltpu.SemaphoreType.DMA((2,)),
    pltpu.SemaphoreType.DMA((2, 2)),
    pltpu.SemaphoreType.DMA((2,)),
    pltpu.SemaphoreType.DMA((2, 7)),
    pltpu.SemaphoreType.DMA((6,)),
]


class Reduce:
    def __init__(self, spot, scratch):
        self.spot = spot
        (
            self.partial,
            self.from_sib,
            self.from_xy,
            self.to_col,
            self.from_col,
            self.inner_to,
            self.inner_from,
            self.sib_send,
            self.sib_recv,
            self.xy_send,
            self.xy_recv,
            self.col_sems,
        ) = scratch

    def sib_copy(self, kk, sub, core, bit):
        half = (1 - sub) * (1 - bit) + sub * bit
        return remote(
            self.partial.at[2 * core + kk, pl.ds(half * 8, 8)],
            self.from_sib.at[kk, pl.ds(half * 8, 8)],
            self.sib_send.at[kk],
            self.sib_recv.at[kk, sub],
            self.spot.sibling(),
        )

    def start(self, kk, sub):
        self.sib_copy(kk, sub, 1 - self.spot.c, self.spot.sib_bit(kk, 0)).start()

    def from_sibling(self, kk, sub):
        self.sib_copy(kk, sub, self.spot.c, self.spot.bit(kk, 0)).wait_recv()

    def add(self, kk, off, ref, ref_off, n):
        k = 2 * self.spot.c + kk

        def body(i, carry):
            self.partial[k, off + i] = self.partial[k, off + i] + ref[kk, ref_off + i]
            return carry

        if n == 1:
            body(0, 0)
        else:
            lax.fori_loop(0, n, body, 0)

    def plan(self, kk, s):
        n = 8 >> s
        landing = 16 - 2 * n
        bit = self.spot.bit(kk, s)
        gone = self.spot.base(kk, s) + (1 - bit) * n
        kept = self.spot.base(kk, s) + bit * n
        half = n // 2
        after = self.spot.bit(kk, s + 1)
        pieces = []
        for sub in range(2):
            shift = ((1 - after) if sub == 0 else after) * half
            pieces.append((gone + shift, kept + shift, landing + sub * half, half, 2 * s + sub))
        return pieces

    def xy_copy(self, kk, s, piece):
        gone, _, landing, n, idx = piece
        return remote(
            self.partial.at[2 * self.spot.c + kk, pl.ds(gone, n)],
            self.from_xy.at[kk, pl.ds(landing, n)],
            self.xy_send.at[kk],
            self.xy_recv.at[kk, idx],
            self.spot.partner(kk, s),
        )

    def xy_start(self, kk, s, piece):
        self.xy_copy(kk, s, piece).start()

    def plane(self, parts, beside):
        sib_part, own_part = parts
        spot = self.spot

        def first(kk):
            self.from_sibling(kk, 0)
            for piece in self.plan(kk, 0):
                self.add(kk, piece[0], self.from_sib, piece[0], piece[3])
                self.xy_start(kk, 0, piece)

        def kept(kk):
            self.from_sibling(kk, 1)
            self.add(kk, spot.bit(kk, 0) * 8, self.from_sib, spot.bit(kk, 0) * 8, 8)

        def arrive(kk, s, sub):
            piece = self.plan(kk, s)[sub]
            self.xy_copy(kk, s, piece).wait_recv()
            self.add(kk, piece[1], self.from_xy, piece[2], piece[3])

        def second(kk):
            arrive(kk, 0, 0)
            for follow in self.plan(kk, 1):
                self.xy_start(kk, 1, follow)

        def third(kk):
            arrive(kk, 1, 0)
            by_2 = spot.place(kk) + 2 * (1 - 2 * spot.bit(kk, 2))
            self.tail_copy(kk, by_2 + 1 - 2 * spot.bit(kk, 3), 2, spot.diagonal(kk, 2)).start()
            self.tail_copy(kk, by_2, 0, spot.partner(kk, 2)).start()

        def fourth(kk):
            arrive(kk, 1, 1)
            own = spot.place(kk)
            self.tail_copy(kk, own + 1 - 2 * spot.bit(kk, 3), 1, spot.partner(kk, 3)).start()

        for kk in range(2):
            sib_part(kk, 0)
        for kk in range(2):
            own_part(kk, 0)
            first(kk)
        for kk in range(2):
            sib_part(kk, 1)
        for kk in range(2):
            own_part(kk, 1)
        for kk in range(2):
            kept(kk)
        for work in beside.get(-1, ()):
            work()
        for kk in range(2):
            second(kk)
        for kk in range(2):
            arrive(kk, 0, 1)
        for work in beside.get(0, ()):
            work()
        for kk in range(2):
            third(kk)
        for kk in range(2):
            fourth(kk)
        for work in beside.get(1, ()):
            work()
        places = [spot.place(kk) for kk in range(2)]
        sums = []
        for kk in range(2):
            total = self.partial[2 * spot.c + kk, places[kk]].astype(F32)
            for i in range(3):
                self.tail_copy(kk, places[kk], i, spot.sibling()).wait_recv()
                total = total + self.from_xy[kk, 12 + i].astype(F32)
            sums.append(total)
        return sums

    def tail_copy(self, kk, block, i, target):
        return remote(
            self.partial.at[2 * self.spot.c + kk, pl.ds(block, 1)],
            self.from_xy.at[kk, pl.ds(12 + i, 1)],
            self.xy_send.at[kk],
            self.xy_recv.at[kk, 4 + i],
            target,
        )

    def column(self, sums, raw, gain, scale, beside=()):
        spot = self.spot
        for kk in range(2):
            for j in range(2):
                for core in range(2):
                    part = sums[kk][8 * core : 8 * core + 8, j * BLOCK : (j + 1) * BLOCK]
                    self.to_col[2 * (2 * kk + j) + core] = part.astype(BF16)

        def to_column(zz):
            zdst = 4 * spot.c + zz
            for core in range(2):
                mine = jnp.logical_and(zdst == spot.z, spot.c == core)

                @pl.when(jnp.logical_not(mine))
                def _(core=core):
                    remote(
                        self.to_col.at[2 * zz + core],
                        self.from_col.at[spot.z],
                        self.col_sems.at[0],
                        self.col_sems.at[1],
                        (spot.chip * 2 + core, zdst),
                    ).start()

                @pl.when(mine)
                def _(core=core):
                    self.from_col[spot.z] = self.to_col[2 * zz + core]

        loop(0, 4, to_column)
        row = lax.broadcasted_iota(jnp.int32, (8, 128), 0)
        diagonal = row == lax.broadcasted_iota(jnp.int32, (8, 128), 1)
        for core in range(2):
            total = jnp.zeros((8, BLOCK), F32)
            for kk in range(2):
                for j in range(2):
                    zb = 4 * spot.c + 2 * kk + j
                    part = sums[kk][8 * core : 8 * core + 8, j * BLOCK : (j + 1) * BLOCK]
                    total = total + raw[8 * core + zb].astype(F32) * gain[zb] * part
            inner = jnp.where(diagonal, jnp.sum(total, axis=1, keepdims=True), 0.0)
            self.inner_to[core] = jnp.sum(inner, axis=0, keepdims=True)
        to_sibling = remote(
            self.inner_to.at[1 - spot.c],
            self.inner_from.at[8],
            self.col_sems.at[4],
            self.col_sems.at[5],
            spot.sibling(),
        )
        to_sibling.start()
        to_sibling.wait_recv()
        self.inner_from[0] = self.inner_to[spot.c] + self.inner_from[8]
        loop(
            1,
            8,
            lambda up: remote(
                self.inner_from.at[0],
                self.inner_from.at[up],
                self.col_sems.at[2],
                self.col_sems.at[3],
                spot.column_peer(up),
            ).start(),
        )
        for work in beside:
            work()
        own = raw[8 * spot.c + spot.z].astype(F32)
        own_gain = gain[spot.z]
        wait_column(spot, self.from_col, self.col_sems.at[1])
        grad = jnp.zeros((8, BLOCK), F32)
        for zsrc in range(8):
            grad = grad + self.from_col[zsrc].astype(F32)
        wait_bytes(self.inner_from.at[pl.ds(1, 7)], self.col_sems.at[3])
        inner = jnp.zeros((1, 128), F32)
        for i in range(8):
            inner = inner + self.inner_from[i]
        inner = jnp.sum(jnp.where(diagonal, inner, 0.0), axis=1, keepdims=True) / D
        return scale * own_gain * grad - own * (scale * scale * scale) * inner

    def finish(self):
        for kk in range(2):
            wait_bytes(self.partial.at[kk], self.sib_send.at[kk])
            wait_bytes(self.partial.at[kk, pl.ds(0, 15)], self.xy_send.at[kk])
        wait_column(self.spot, self.to_col, self.col_sems.at[0])
        wait_bytes(self.inner_from.at[pl.ds(1, 7)], self.col_sems.at[2])
        wait_bytes(self.inner_from.at[pl.ds(8, 1)], self.col_sems.at[4])


def wait_column(spot, ref, sem):
    own = spot.half == spot.c

    @pl.when(own)
    def _():
        wait_bytes(ref.at[pl.ds(0, 7)], sem)

    @pl.when(jnp.logical_not(own))
    def _():
        wait_bytes(ref, sem)


def program(
    layer_out,
    resid_mid,
    final_gain,
    mlp_gain,
    teacher_in,
    assign,
    lengths,
    token_ids,
    head_hbm,
    gate_hbm,
    up_hbm,
    down_hbm,
    grad_first,
    grad_second,
    final_rows,
    normed,
    grad_rows,
    dlog_t,
    hidden_t,
    activated_t,
    head,
    w_gate_up,
    w_down,
    dlog,
    dlog_turned,
    hidden_turned,
    raw_out,
    raw_mid,
    full_out,
    full_mid,
    full_grad,
    packed,
    got,
    logits_ref,
    diff_ref,
    gate_up_pre,
    act_grad,
    first,
    second,
    stats_pad,
    own_b,
    own_from,
    scale_ref,
    load_sem,
    raw_sems,
    plane_sems,
    stat_sems,
    own_sems,
    xy_send,
    xy_recv,
    sib_send,
    sib_recv,
    *scratch,
):
    spot = Spot()
    c, other = spot.c, 1 - spot.c
    loads = [
        pltpu.make_async_copy(src, dst, load_sem.at[i])
        for i, (src, dst) in enumerate(
            (
                (head_hbm, head),
                (gate_hbm, w_gate_up.at[pl.ds(0, 64)]),
                (up_hbm, w_gate_up.at[pl.ds(64, 64)]),
                (down_hbm, w_down),
            )
        )
    ]
    for load in loads:
        load.start()
    reduces = [Reduce(spot, scratch[: len(REDUCE_SCRATCH)]), Reduce(spot, scratch[len(REDUCE_SCRATCH) :])]
    gathers = [
        Gather(spot, full, xy_send.at[a], xy_recv.at[a], sib_send.at[a], sib_recv.at[a])
        for a, full in enumerate((full_out, full_mid, full_grad))
    ]
    gather_out, gather_mid, gather_grad = gathers

    greet(spot)
    mine = 8 * c + spot.z
    raw_out[mine] = layer_out[...]
    raw_mid[mine] = resid_mid[...]

    greeted()

    def send_raw(a, own, raw):
        loop(
            1,
            8,
            lambda up: remote(
                own, raw.at[mine], raw_sems.at[a, 0], raw_sems.at[a, 1], spot.column_peer(up)
            ).start(),
        )

    def pass_raw(a, raw):
        wait_bytes(raw.at[pl.ds(0, 7)], raw_sems.at[a, 1])
        rows = raw.at[pl.ds(8 * c, 8)]
        remote(rows, rows, raw_sems.at[a, 2], raw_sems.at[a, 3], spot.sibling()).start()

    def plane_start(i, carry):
        peer = wrap(spot.d + i, 32)
        remote(packed.at[peer], got.at[spot.d], plane_sems.at[0], plane_sems.at[1], (peer, spot.z)).start()
        return carry

    def normalise(a, raw, full, gain):
        wait_bytes(raw.at[pl.ds(0, 8)], raw_sems.at[a, 3])
        scales = [row_scale(raw, core) for core in range(2)]
        for kk in range(2):
            place = spot.place(kk)
            for j in range(2):
                zb = 4 * c + 2 * kk + j
                rows = jnp.concatenate(
                    [raw[8 * core + zb].astype(F32) * scales[core] * gain[zb] for core in range(2)], axis=0
                )
                full[2 * c + kk, place, :, j * BLOCK : (j + 1) * BLOCK] = rows.astype(BF16)
        for core in range(2):
            scale_ref[a, core] = jnp.broadcast_to(scales[core], (8, 128))

    def both(gather, stage):
        for kk in range(2):
            gather.step(stage, kk)

    send_raw(0, layer_out, raw_out)

    row = lax.broadcasted_iota(jnp.int32, (8, 1), 0)
    order = jnp.zeros((8, 1), jnp.int32)
    for r in range(8):
        order = jnp.where(row == r, assign[0, r], order)

    def pack(peer):
        rows = teacher_in[:, pl.ds(pl.multiple_of(peer * 384, 384), 384)].astype(F32)
        picked = jnp.zeros((8, 384), F32)
        for r in range(8):
            picked = picked + jnp.where(order == r, rows[r : r + 1, :], 0.0)
        packed[peer] = picked.astype(BF16)

    loop(0, 32, pack)
    got[spot.d] = packed[spot.d]

    token = lax.broadcasted_iota(jnp.int32, (1, 256), 1)
    own_ids = jnp.full((1, 256), -1, jnp.int32)
    own_lengths = jnp.zeros((1, 256), jnp.int32)
    for r in range(8):
        here = token == 8 * spot.d + r
        own_ids = jnp.where(here, token_ids[r], own_ids)
        own_lengths = jnp.where(here, lengths[0, r // SLOT], own_lengths)
    live = (lax.rem(token, SLOT) < own_lengths).astype(jnp.int32)
    codes = jnp.where(own_ids >= 0, 2 * own_ids + live, 0).astype(F32)

    lax.fori_loop(1, 14, plane_start, 0)
    send_raw(1, resid_mid, raw_mid)
    pass_raw(0, raw_out)
    normalise(0, raw_out, full_out, final_gain)
    both(gather_out, 0)
    lax.fori_loop(14, 32, plane_start, 0)
    both(gather_out, 1)
    pass_raw(1, raw_mid)
    both(gather_out, 2)
    normalise(1, raw_mid, full_mid, mlp_gain)
    both(gather_out, 3)
    both(gather_mid, 0)

    def products(left, right, out, core):
        def body(kk):
            columns = slice_columns(kk, core)
            out[...] += contract_cols(left[:, columns], right[:, columns])

        loop(0, 2, body)

    for kk in range(2):
        lay_out(full_out, final_rows, kk, c)
    loads[0].wait()
    logits_ref[...] = jnp.zeros_like(logits_ref)
    products(final_rows, head, logits_ref, c)
    both(gather_out, 4)
    for kk in range(2):
        lay_out(full_out, final_rows, kk, other)
    products(final_rows, head, logits_ref, other)
    both(gather_mid, 1)

    wait_bytes(got.at[pl.ds(0, 31)], plane_sems.at[1])
    logits = logits_ref[...]
    diff = logits - got[...].astype(F32).reshape(256, 384)
    local_max = jnp.max(logits, axis=1, keepdims=True)
    expd = jnp.exp(logits - local_max)
    total = jnp.sum(expd, axis=1, keepdims=True)
    moment = jnp.sum(expd * diff, axis=1, keepdims=True)
    logits_ref[...] = expd
    diff_ref[...] = diff
    lanes = lax.broadcasted_iota(jnp.int32, (256, 128), 1)
    columns = jnp.where(lanes == 0, local_max, jnp.where(lanes == 1, total, moment))
    first[0] = jnp.transpose(columns)[0:4]
    first[0, 3:4] = codes
    remote(first.at[0], first.at[1], stat_sems.at[0], stat_sems.at[1], spot.sibling()).start()

    def to_column(up):
        for flip in range(2):
            target = spot.column_peer(up, flip)
            remote(first.at[0], first.at[2 * up + flip], stat_sems.at[0], stat_sems.at[1], target).start()

    loop(1, 8, to_column)
    both(gather_mid, 2)

    def combine(ref, groups):
        top = ref[0, 0:1]
        for i in range(1, 16):
            top = jnp.maximum(top, ref[i, 0:1])
        total = jnp.zeros_like(top)
        moment = jnp.zeros_like(top)
        for i in range(16):
            weight = jnp.exp(ref[i, 0:1] - top)
            total = total + ref[i, 1:2] * weight
            moment = moment + ref[i, 2:3] * weight
        return jnp.concatenate([top, total, moment, sum(ref[i, 3:4] for i in range(groups))], axis=0)

    wait_bytes(first.at[pl.ds(1, 15)], stat_sems.at[1])
    second[0] = combine(first, 2)

    def to_plane(i):
        target = (wrap(spot.chip + i, CHIPS) * 2 + c, spot.z)
        remote(second.at[0], second.at[i], stat_sems.at[2], stat_sems.at[3], target).start()

    loop(1, CHIPS, to_plane)
    both(gather_mid, 3)
    vocab = lax.broadcasted_iota(jnp.int32, (256, 384), 1) + (spot.z * 32 + spot.d) * 384
    stats_pad[...] = jnp.zeros_like(stats_pad)
    wait_bytes(second.at[pl.ds(1, 15)], stat_sems.at[3])
    stats_pad[0:4] = combine(second, 16)
    columns = jnp.transpose(stats_pad[...])
    global_max, totals, moments = columns[:, 0:1], columns[:, 1:2], columns[:, 2:3]
    code = columns[:, 3:4].astype(jnp.int32)
    ids_all = code >> 1
    live_mask = (code - 2 * ids_all).astype(F32)
    token_weight = live_mask * (LOSS_SCALE / jnp.sum(live_mask, axis=0, keepdims=True))
    share = token_weight * (jnp.exp(local_max - global_max) / totals)
    shift = CE_WEIGHT - moments / totals
    dlogits = share * logits_ref[...] * (diff_ref[...] + shift)
    dlogits = dlogits - jnp.where(ids_all == vocab, CE_WEIGHT * token_weight, 0.0)

    def turn(rows, out):
        for k in range(4):
            for chip in range(CHIPS):
                place = 16 * block_place(k, chip)
                out[k, place : place + 16, :] = rows[16 * chip : 16 * chip + 16]

    def spread(reduce, kk, core, half, left, right):
        k = 2 * core + kk
        rows = left[k, pl.ds(pl.multiple_of(half * 128, 128), 128)]
        part = jnp.dot(rows, right[:, slice_columns(kk, core)], preferred_element_type=F32).astype(BF16)
        reduce.partial[k, pl.ds(half * 8, 8)] = part.reshape(8, 16, SLICE)

    def partials(reduce, left, right):

        def sib_part(kk, sub):
            bit = spot.sib_bit(kk, 0)
            spread(reduce, kk, other, (1 - bit) if sub == 0 else bit, left, right)
            reduce.start(kk, sub)

        def own_part(kk, sub):
            bit = spot.bit(kk, 0)
            spread(reduce, kk, c, (1 - bit) if sub == 0 else bit, left, right)

        return sib_part, own_part

    dlog_b = dlogits.astype(BF16)
    turn(dlog_b, dlog_turned)
    dlog[...] = dlog_b

    def mid_rows(core):
        for kk in range(2):
            lay_out(full_mid, normed, kk, core)

    def mid_first():
        for load in loads[1:]:
            load.wait()
        gate_up_pre[...] = jnp.zeros_like(gate_up_pre)
        act_grad[...] = jnp.zeros_like(act_grad)
        mid_rows(c)
        products(w_gate_up, normed, gate_up_pre, c)

    def mid_second():
        both(gather_mid, 4)
        mid_rows(other)
        products(w_gate_up, normed, gate_up_pre, other)

    def activate():
        gate, up = gate_up_pre[0:64], gate_up_pre[64:128]
        gate_sigmoid = jax.nn.sigmoid(gate)
        activated_t[...] = (gate * gate_sigmoid * up).astype(BF16)
        gate_up_pre[0:64] = up * gate_sigmoid * (1.0 + gate * (1.0 - gate_sigmoid))
        gate_up_pre[64:128] = gate * gate_sigmoid

    def turn_dlog():
        dlog_t[...] = jnp.transpose(dlog[...].astype(F32)).astype(BF16)

    sums = reduces[0].plane(partials(reduces[0], dlog_turned, head), {-1: [turn_dlog]})
    grad_out = reduces[0].column(sums, raw_out, final_gain, scale_ref[0, c][:, 0:1], [mid_first])
    own_b[...] = grad_out.astype(BF16)
    grad_first[...] = grad_out

    target_core = spot.half
    own_place = spot.z_low * 2 + c

    def own_to_column(zdst):
        mine = jnp.logical_and(spot.z == zdst, target_core == c)

        @pl.when(jnp.logical_not(mine))
        def _():
            target = (spot.chip * 2 + target_core, zdst)
            remote(own_b, own_from.at[own_place], own_sems.at[0], own_sems.at[1], target).start()

        @pl.when(mine)
        def _():
            own_from[own_place] = own_b[...]

    loop(0, 8, own_to_column)
    mid_second()
    activate()
    wait_column(spot, own_from, own_sems.at[1])
    for kk in range(2):
        for j in range(2):
            zz = 2 * kk + j
            rows = jnp.concatenate([own_from[2 * zz + core].astype(F32) for core in range(2)], axis=0)
            full_grad[2 * c + kk, spot.place(kk), :, j * BLOCK : (j + 1) * BLOCK] = rows.astype(BF16)
    both(gather_grad, 0)
    for stage in range(1, 4):
        both(gather_grad, stage)
    for kk in range(2):
        lay_out(full_grad, grad_rows, kk, c)
    products(w_down, grad_rows, act_grad, c)
    both(gather_grad, 4)
    for kk in range(2):
        lay_out(full_grad, grad_rows, kk, other)
    products(w_down, grad_rows, act_grad, other)

    act = act_grad[...]
    both_grads = jnp.concatenate([act * gate_up_pre[0:64], act * gate_up_pre[64:128]], axis=0)
    turn(jnp.transpose(both_grads).astype(BF16), hidden_turned)
    hidden_t[...] = both_grads.astype(BF16)

    def left_earlier():
        for a in range(2):
            wait_bytes(raw_out.at[pl.ds(0, 7)], raw_sems.at[a, 0])
            wait_bytes(raw_out.at[pl.ds(0, 8)], raw_sems.at[a, 2])
        wait_bytes(got.at[pl.ds(0, 31)], plane_sems.at[0])
        wait_bytes(first.at[pl.ds(1, 15)], stat_sems.at[0])
        wait_bytes(second.at[pl.ds(1, 15)], stat_sems.at[2])
        for gather in gathers:
            gather.finish()
        reduces[0].finish()
        wait_column(spot, own_from, own_sems.at[0])

    sums = reduces[1].plane(partials(reduces[1], hidden_turned, w_gate_up), {})
    grad_second[...] = reduces[1].column(sums, raw_mid, mlp_gain, scale_ref[1, c][:, 0:1], [left_earlier])
    reduces[1].finish()


def weight_grads(
    grad_first,
    grad_second,
    dlog_t,
    hidden_t,
    activated_t,
    final_rows,
    normed,
    grad_rows,
    grad_resid,
    grad_head,
    grad_gate,
    grad_up,
    grad_down,
    head_rows,
    gate_up_rows,
    down_rows,
    sems,
):
    def product(left, right):
        return jnp.dot(left, right, preferred_element_type=F32).astype(BF16)

    grad_resid[...] = (grad_first[...] + grad_second[...]).astype(BF16)

    def copies(k):
        place = pl.ds(pl.multiple_of(k * SLICE, SLICE), SLICE)
        return [
            pltpu.make_async_copy(head_rows.at[:, place], grad_head.at[:, place], sems.at[0, k]),
            pltpu.make_async_copy(gate_up_rows.at[pl.ds(0, 64), place], grad_gate.at[:, place], sems.at[1, k]),
            pltpu.make_async_copy(gate_up_rows.at[pl.ds(64, 64), place], grad_up.at[:, place], sems.at[2, k]),
            pltpu.make_async_copy(down_rows.at[:, place], grad_down.at[:, place], sems.at[3, k]),
        ]

    def chunk(k):
        place = pl.ds(pl.multiple_of(k * SLICE, SLICE), SLICE)
        to_head, to_gate, to_up, to_down = copies(k)
        head_rows[:, place] = product(dlog_t[...], final_rows[:, place])
        to_head.start()
        gate_up_rows[:, place] = product(hidden_t[...], normed[:, place])
        to_gate.start()
        to_up.start()
        down_rows[:, place] = product(activated_t[...], grad_rows[:, place])
        to_down.start()

    def done(k):
        for copy in copies(k):
            copy.wait()

    loop(0, 4, chunk)
    loop(0, 4, done)


def shape(dims, dtype):
    return jax.ShapeDtypeStruct(dims, dtype)


def per_device(
    layer_out,
    resid_mid,
    final_gain,
    mlp_gain,
    head_weight,
    w_gate,
    w_up,
    w_down,
    teacher_logits,
    assign,
    lengths,
    token_ids,
):
    final_gain = final_gain.reshape(8, 1, BLOCK)
    mlp_gain = mlp_gain.reshape(8, 1, BLOCK)
    vmem = pl.BlockSpec(memory_space=pltpu.VMEM)
    smem = pl.BlockSpec(memory_space=pltpu.SMEM)
    hbm = pl.BlockSpec(memory_space=pl.ANY)
    full = pltpu.VMEM((4, 16, 16, SLICE), BF16)
    rows = pltpu.VMEM((256, D), BF16)
    dma = pltpu.SemaphoreType.DMA
    shared = pl.pallas_call(
        program,
        out_shape=[
            pltpu.VMEM((8, BLOCK), F32),
            pltpu.VMEM((8, BLOCK), F32),
            rows,
            rows,
            rows,
            pltpu.VMEM((384, 256), BF16),
            pltpu.VMEM((128, 256), BF16),
            pltpu.VMEM((64, 256), BF16),
        ],
        in_specs=[vmem] * 5 + [smem] * 3 + [hbm] * 4,
        out_specs=[vmem] * 8,
        scratch_shapes=[
            pltpu.VMEM((384, D), BF16),
            pltpu.VMEM((128, D), BF16),
            pltpu.VMEM((64, D), BF16),
            pltpu.VMEM((256, 384), BF16),
            pltpu.VMEM((4, 256, 384), BF16),
            pltpu.VMEM((4, 256, 128), BF16),
            pltpu.VMEM((16, 8, BLOCK), BF16),
            pltpu.VMEM((16, 8, BLOCK), BF16),
            full,
            full,
            full,
            pltpu.VMEM((32, 8, 384), BF16),
            pltpu.VMEM((32, 8, 384), BF16),
            pltpu.VMEM((256, 384), F32),
            pltpu.VMEM((256, 384), F32),
            pltpu.VMEM((128, 256), F32),
            pltpu.VMEM((64, 256), F32),
            pltpu.VMEM((16, 4, 256), F32),
            pltpu.VMEM((16, 4, 256), F32),
            pltpu.VMEM((128, 256), F32),
            pltpu.VMEM((8, BLOCK), BF16),
            pltpu.VMEM((8, 8, BLOCK), BF16),
            pltpu.VMEM((2, 2, 8, 128), F32),
            dma((4,)),
            dma((2, 4)),
            dma((2,)),
            dma((4,)),
            dma((2,)),
            dma((3, 2)),
            dma((3, 2, 8)),
            dma((3, 2)),
            dma((3, 2, 5)),
        ]
        + REDUCE_SCRATCH
        + REDUCE_SCRATCH,
        compiler_params=pltpu.CompilerParams(
            collective_id=0, has_side_effects=True, vmem_limit_bytes=VMEM_LIMIT
        ),
        name="backward",
    )(
        layer_out,
        resid_mid,
        final_gain,
        mlp_gain,
        teacher_logits,
        assign,
        lengths,
        token_ids,
        head_weight,
        w_gate,
        w_up,
        w_down,
    )
    return pl.pallas_call(
        weight_grads,
        out_shape=[
            shape((8, BLOCK), BF16),
            shape(head_weight.shape, BF16),
            shape(w_gate.shape, BF16),
            shape(w_up.shape, BF16),
            shape(w_down.shape, BF16),
        ],
        in_specs=[vmem] * 8,
        out_specs=[vmem] + [hbm] * 4,
        scratch_shapes=[
            pltpu.VMEM((384, D), BF16),
            pltpu.VMEM((128, D), BF16),
            pltpu.VMEM((64, D), BF16),
            dma((4, 4)),
        ],
        compiler_params=pltpu.CompilerParams(vmem_limit_bytes=GRADS_VMEM),
        cost_estimate=pl.CostEstimate(flops=2 * 256 * 576 * D, bytes_accessed=2 * 576 * D, transcendentals=0),
        name="weight_grads",
    )(shared[0], shared[1], shared[5], shared[6], shared[7], shared[2], shared[3], shared[4])


def solution(mesh):
    return jax.shard_map(
        per_device,
        mesh=mesh,
        in_specs=(
            P("dp", "tensor"),
            P("dp", "tensor"),
            P(),
            P(),
            P(("tensor", "dp"), None),
            P(("tensor", "dp"), None),
            P(("tensor", "dp"), None),
            P(("tensor", "dp"), None),
            P("dp", "tensor"),
            P("dp", None),
            P("dp", None),
            P("dp"),
        ),
        out_specs=(
            P("dp", "tensor"),
            P(("tensor", "dp"), None),
            P(("tensor", "dp"), None),
            P(("tensor", "dp"), None),
            P(("tensor", "dp"), None),
        ),
        check_vma=False,
    )
```

```python
import jax
import jax.numpy as jnp
from jax import lax
from jax.experimental import pallas as pl
from jax.experimental.pallas import tpu as pltpu
from jax.sharding import PartitionSpec as P

D = 5120
SLOT = 4
EPS = 1e-06
CE_WEIGHT = 0.5
LOSS_SCALE = 4096.0

BLOCK = 640
SLICE = 1280
CHIPS = 16
F32 = jnp.float32
BF16 = jnp.bfloat16
VMEM_LIMIT = 52 * 1024 * 1024
GRADS_VMEM = 20 * 1024 * 1024


def contract_cols(left, right):
    return lax.dot_general(left, right, (((1,), (1,)), ((), ())), preferred_element_type=F32)


def wrap(v, size):
    return jnp.where(v >= size, v - size, v)


def ring_bits(v):
    high = v // 2
    return v % 2 + high - 2 * (v % 2) * high, high


class Spot:
    def __init__(self):
        self.d = lax.axis_index("dp")
        self.z = lax.axis_index("tensor")
        self.chip = lax.div(self.d, 2)
        self.c = self.d - 2 * self.chip
        self.y = lax.div(self.chip, 4)
        self.x = self.chip - 4 * self.y
        c, other = self.c, 1 - self.c
        xv, yv = lax.div(self.x, 2), lax.div(self.y, 2)
        x_low, y_low = self.x - 2 * xv, self.y - 2 * yv
        xu, yu = x_low + xv - 2 * x_low * xv, y_low + yv - 2 * y_low * yv
        x_near, y_near = self.x + 1 - 2 * x_low, self.y + 1 - 2 * y_low
        x_far, y_far = 3 - self.x, 3 - self.y
        self.half = lax.div(self.z, 4)
        self.z_low = self.z - 4 * self.half
        bits = (xu, yu, xv, yv)
        moved = (x_near, y_near, x_far, y_far)
        self.own_bits = [bits[i] * other + bits[(i + 2) % 4] * c for i in range(4)]
        self.sib_bits = [bits[i] * c + bits[(i + 2) % 4] * other for i in range(4)]
        moved = [moved[i] * other + moved[(i + 2) % 4] * c for i in range(4)]
        self.chips = [self.y * 4 + moved[i] if i % 2 == 0 else moved[i] * 4 + self.x for i in range(4)]
        corner = []
        for i in range(4):
            j = (i + 1) % 4
            corner.append(moved[j] * 4 + moved[i] if i % 2 == 0 else moved[i] * 4 + moved[j])
        self.corners = corner

    def pick(self, values, kk, s):
        if isinstance(kk, int):
            return values[(kk + s) % 4]
        first, second = values[s % 4], values[(s + 1) % 4]
        return first + (second - first) * kk

    def bit(self, kk, s):
        return self.pick(self.own_bits, kk, s)

    def sib_bit(self, kk, s):
        return self.pick(self.sib_bits, kk, s)

    def base(self, kk, s):
        return sum((self.bit(kk, i) * (8 >> i) for i in range(s)), jnp.int32(0))

    def sib_base(self, kk, s):
        return sum((self.sib_bit(kk, i) * (8 >> i) for i in range(s)), jnp.int32(0))

    def place(self, kk):
        return self.base(kk, 4)

    def partner(self, kk, s):
        return (self.pick(self.chips, kk, s) * 2 + self.c, self.z)

    def diagonal(self, kk, s):
        return (self.pick(self.corners, kk, s) * 2 + self.c, self.z)

    def sibling(self):
        return (self.chip * 2 + 1 - self.c, self.z)

    def column_peer(self, up, flip=0):
        core = self.c if flip == 0 else 1 - self.c
        return (self.chip * 2 + core, wrap(self.z + up, 8))


def greet(spot):
    barrier = pltpu.get_barrier_semaphore()
    mesh = pl.DeviceIdType.MESH
    pl.semaphore_signal(barrier, inc=1, device_id=spot.sibling(), device_id_type=mesh)

    def column(up, carry):
        for flip in range(2):
            pl.semaphore_signal(barrier, inc=1, device_id=spot.column_peer(up, flip), device_id_type=mesh)
        return carry

    lax.fori_loop(1, 8, column, 0)

    def body(j, carry):
        chip = wrap(spot.chip + j, CHIPS)
        for core in range(2):
            pl.semaphore_signal(
                barrier, inc=1, device_id=(chip * 2 + core, spot.z), device_id_type=pl.DeviceIdType.MESH
            )
        return carry

    lax.fori_loop(1, CHIPS, body, 0)


def greeted():
    pl.semaphore_wait(pltpu.get_barrier_semaphore(), 45)


def remote(src, dst, send_sem, recv_sem, target):
    return pltpu.make_async_remote_copy(
        src_ref=src,
        dst_ref=dst,
        send_sem=send_sem,
        recv_sem=recv_sem,
        device_id=target,
        device_id_type=pl.DeviceIdType.MESH,
    )


def row_scale(raw, core):
    total = jnp.zeros((8, BLOCK), F32)
    for zb in range(8):
        part = raw[8 * core + zb].astype(F32)
        total = total + part * part
    return lax.rsqrt(jnp.sum(total, axis=1, keepdims=True) / D + EPS)


def loop(start, stop, body):
    def step(i, carry):
        body(i)
        return carry

    lax.fori_loop(start, stop, step, 0)


def wait_bytes(ref, sem):
    pltpu.make_async_copy(ref, ref, sem).wait()


class Gather:
    def __init__(self, spot, full, xy_send, xy_recv, sib_send, sib_recv):
        self.spot, self.full = spot, full
        self.xy_send, self.xy_recv, self.sib_send, self.sib_recv = xy_send, xy_recv, sib_send, sib_recv

    def view(self, kk, off, n, core=None):
        core = self.spot.c if core is None else core
        return self.full.at[2 * core + kk, pl.ds(off, n)]

    def send(self, kk, target, idx, off, n):
        view = self.view(kk, off, n)
        remote(view, view, self.xy_send.at[kk], self.xy_recv.at[kk, idx], target).start()

    def arrived(self, kk, idx, off, n):
        wait_bytes(self.view(kk, off, n), self.xy_recv.at[kk, idx])

    def pass_on(self, kk, idx, off, n):
        view = self.view(kk, off, n)
        remote(view, view, self.sib_send.at[kk], self.sib_recv.at[kk, idx], self.spot.sibling()).start()

    def step(self, stage, kk):
        spot = self.spot
        flip = [(8 >> s) * (1 - 2 * spot.bit(kk, s)) for s in range(4)]
        own, four = spot.place(kk), spot.base(kk, 2)
        if stage == 0:
            self.send(kk, spot.diagonal(kk, 2), 2, own, 1)
            self.send(kk, spot.partner(kk, 3), 0, own, 1)
            self.send(kk, spot.partner(kk, 2), 1, own, 1)
        elif stage == 1:
            self.arrived(kk, 0, own + flip[3], 1)
            self.arrived(kk, 1, own + flip[2], 1)
            self.arrived(kk, 2, own + flip[2] + flip[3], 1)
            self.send(kk, spot.partner(kk, 1), 3, four, 2)
            self.send(kk, spot.partner(kk, 1), 4, four + 2, 2)
            self.send(kk, spot.partner(kk, 0), 5, four, 4)
            self.pass_on(kk, 0, four, 4)
        elif stage == 2:
            new = four + flip[1]
            for i in range(2):
                self.arrived(kk, 3 + i, new + 2 * i, 2)
                self.send(kk, spot.partner(kk, 0), 6 + i, new + 2 * i, 2)
            self.pass_on(kk, 1, new, 4)
        elif stage == 3:
            new = four + flip[0]
            self.arrived(kk, 5, new, 4)
            self.pass_on(kk, 2, new, 4)
            new = new + flip[1]
            for i in range(2):
                self.arrived(kk, 6 + i, new + 2 * i, 2)
                self.pass_on(kk, 3 + i, new + 2 * i, 2)
        else:
            other = 1 - spot.c
            four = spot.sib_base(kk, 2)
            over_1 = four + 4 * (1 - 2 * spot.sib_bit(kk, 1))
            over_0 = 8 * (1 - 2 * spot.sib_bit(kk, 0))
            last = over_1 + over_0
            pieces = ((four, 4), (over_1, 4), (four + over_0, 4), (last, 2), (last + 2, 2))
            for idx, (off, n) in enumerate(pieces):
                wait_bytes(self.view(kk, off, n, other), self.sib_recv.at[kk, idx])

    def finish(self):
        for kk in range(2):
            wait_bytes(self.full.at[kk, pl.ds(0, 15)], self.xy_send.at[kk])
            wait_bytes(self.full.at[kk], self.sib_send.at[kk])


def block_place(k, chip):
    xu, xv = ring_bits(chip % 4)
    yu, yv = ring_bits(chip // 4)
    bits = (xu, yu, xv, yv)
    return sum(bits[(k + s) % 4] * (8 >> s) for s in range(4))


def slice_columns(kk, core):
    return pl.ds(pl.multiple_of((2 * core + kk) * SLICE, SLICE), SLICE)


def lay_out(full, out, kk, core):
    for chip in range(CHIPS):
        low, high = block_place(kk, chip), block_place(2 + kk, chip)
        out[16 * chip : 16 * chip + 16, slice_columns(kk, core)] = full[2 * core + kk, low + (high - low) * core]


REDUCE_SCRATCH = [
    pltpu.VMEM((4, 16, 16, SLICE), BF16),
    pltpu.VMEM((2, 16, 16, SLICE), BF16),
    pltpu.VMEM((2, 15, 16, SLICE), BF16),
    pltpu.VMEM((8, 8, BLOCK), BF16),
    pltpu.VMEM((8, 8, BLOCK), BF16),
    pltpu.VMEM((2, 1, 128), F32),
    pltpu.VMEM((9, 1, 128), F32),
    pltpu.SemaphoreType.DMA((2,)),
    pltpu.SemaphoreType.DMA((2, 2)),
    pltpu.SemaphoreType.DMA((2,)),
    pltpu.SemaphoreType.DMA((2, 7)),
    pltpu.SemaphoreType.DMA((6,)),
]


class Reduce:
    def __init__(self, spot, scratch):
        self.spot = spot
        (
            self.partial,
            self.from_sib,
            self.from_xy,
            self.to_col,
            self.from_col,
            self.inner_to,
            self.inner_from,
            self.sib_send,
            self.sib_recv,
            self.xy_send,
            self.xy_recv,
            self.col_sems,
        ) = scratch

    def sib_copy(self, kk, sub, core, bit):
        half = (1 - sub) * (1 - bit) + sub * bit
        return remote(
            self.partial.at[2 * core + kk, pl.ds(half * 8, 8)],
            self.from_sib.at[kk, pl.ds(half * 8, 8)],
            self.sib_send.at[kk],
            self.sib_recv.at[kk, sub],
            self.spot.sibling(),
        )

    def start(self, kk, sub):
        self.sib_copy(kk, sub, 1 - self.spot.c, self.spot.sib_bit(kk, 0)).start()

    def from_sibling(self, kk, sub):
        self.sib_copy(kk, sub, self.spot.c, self.spot.bit(kk, 0)).wait_recv()

    def add(self, kk, off, ref, ref_off, n):
        k = 2 * self.spot.c + kk

        def body(i, carry):
            self.partial[k, off + i] = self.partial[k, off + i] + ref[kk, ref_off + i]
            return carry

        if n == 1:
            body(0, 0)
        else:
            lax.fori_loop(0, n, body, 0)

    def plan(self, kk, s):
        n = 8 >> s
        landing = 16 - 2 * n
        bit = self.spot.bit(kk, s)
        gone = self.spot.base(kk, s) + (1 - bit) * n
        kept = self.spot.base(kk, s) + bit * n
        half = n // 2
        after = self.spot.bit(kk, s + 1)
        pieces = []
        for sub in range(2):
            shift = ((1 - after) if sub == 0 else after) * half
            pieces.append((gone + shift, kept + shift, landing + sub * half, half, 2 * s + sub))
        return pieces

    def xy_copy(self, kk, s, piece):
        gone, _, landing, n, idx = piece
        return remote(
            self.partial.at[2 * self.spot.c + kk, pl.ds(gone, n)],
            self.from_xy.at[kk, pl.ds(landing, n)],
            self.xy_send.at[kk],
            self.xy_recv.at[kk, idx],
            self.spot.partner(kk, s),
        )

    def xy_start(self, kk, s, piece):
        self.xy_copy(kk, s, piece).start()

    def plane(self, parts, beside):
        sib_part, own_part = parts
        spot = self.spot

        def first(kk):
            self.from_sibling(kk, 0)
            for piece in self.plan(kk, 0):
                self.add(kk, piece[0], self.from_sib, piece[0], piece[3])
                self.xy_start(kk, 0, piece)

        def kept(kk):
            self.from_sibling(kk, 1)
            self.add(kk, spot.bit(kk, 0) * 8, self.from_sib, spot.bit(kk, 0) * 8, 8)

        def arrive(kk, s, sub):
            piece = self.plan(kk, s)[sub]
            self.xy_copy(kk, s, piece).wait_recv()
            self.add(kk, piece[1], self.from_xy, piece[2], piece[3])

        def second(kk):
            arrive(kk, 0, 0)
            for follow in self.plan(kk, 1):
                self.xy_start(kk, 1, follow)

        def third(kk):
            arrive(kk, 1, 0)
            by_2 = spot.place(kk) + 2 * (1 - 2 * spot.bit(kk, 2))
            self.tail_copy(kk, by_2 + 1 - 2 * spot.bit(kk, 3), 2, spot.diagonal(kk, 2)).start()
            self.tail_copy(kk, by_2, 0, spot.partner(kk, 2)).start()

        def fourth(kk):
            arrive(kk, 1, 1)
            own = spot.place(kk)
            self.tail_copy(kk, own + 1 - 2 * spot.bit(kk, 3), 1, spot.partner(kk, 3)).start()

        for kk in range(2):
            sib_part(kk, 0)
        for kk in range(2):
            own_part(kk, 0)
            first(kk)
        for kk in range(2):
            sib_part(kk, 1)
        for kk in range(2):
            own_part(kk, 1)
        for kk in range(2):
            kept(kk)
        for work in beside.get(-1, ()):
            work()
        for kk in range(2):
            second(kk)
        for kk in range(2):
            arrive(kk, 0, 1)
        for work in beside.get(0, ()):
            work()
        for kk in range(2):
            third(kk)
        for kk in range(2):
            fourth(kk)
        for work in beside.get(1, ()):
            work()
        places = [spot.place(kk) for kk in range(2)]
        sums = []
        for kk in range(2):
            total = self.partial[2 * spot.c + kk, places[kk]].astype(F32)
            for i in range(3):
                self.tail_copy(kk, places[kk], i, spot.sibling()).wait_recv()
                total = total + self.from_xy[kk, 12 + i].astype(F32)
            sums.append(total)
        return sums

    def tail_copy(self, kk, block, i, target):
        return remote(
            self.partial.at[2 * self.spot.c + kk, pl.ds(block, 1)],
            self.from_xy.at[kk, pl.ds(12 + i, 1)],
            self.xy_send.at[kk],
            self.xy_recv.at[kk, 4 + i],
            target,
        )

    def column(self, sums, raw, gain, scale, beside=()):
        spot = self.spot
        for kk in range(2):
            for j in range(2):
                for core in range(2):
                    part = sums[kk][8 * core : 8 * core + 8, j * BLOCK : (j + 1) * BLOCK]
                    self.to_col[2 * (2 * kk + j) + core] = part.astype(BF16)

        def to_column(zz):
            zdst = 4 * spot.c + zz
            for core in range(2):
                mine = jnp.logical_and(zdst == spot.z, spot.c == core)

                @pl.when(jnp.logical_not(mine))
                def _(core=core):
                    remote(
                        self.to_col.at[2 * zz + core],
                        self.from_col.at[spot.z],
                        self.col_sems.at[0],
                        self.col_sems.at[1],
                        (spot.chip * 2 + core, zdst),
                    ).start()

                @pl.when(mine)
                def _(core=core):
                    self.from_col[spot.z] = self.to_col[2 * zz + core]

        loop(0, 4, to_column)
        row = lax.broadcasted_iota(jnp.int32, (8, 128), 0)
        diagonal = row == lax.broadcasted_iota(jnp.int32, (8, 128), 1)
        for core in range(2):
            total = jnp.zeros((8, BLOCK), F32)
            for kk in range(2):
                for j in range(2):
                    zb = 4 * spot.c + 2 * kk + j
                    part = sums[kk][8 * core : 8 * core + 8, j * BLOCK : (j + 1) * BLOCK]
                    total = total + raw[8 * core + zb].astype(F32) * gain[zb] * part
            inner = jnp.where(diagonal, jnp.sum(total, axis=1, keepdims=True), 0.0)
            self.inner_to[core] = jnp.sum(inner, axis=0, keepdims=True)
        to_sibling = remote(
            self.inner_to.at[1 - spot.c],
            self.inner_from.at[8],
            self.col_sems.at[4],
            self.col_sems.at[5],
            spot.sibling(),
        )
        to_sibling.start()
        to_sibling.wait_recv()
        self.inner_from[0] = self.inner_to[spot.c] + self.inner_from[8]
        loop(
            1,
            8,
            lambda up: remote(
                self.inner_from.at[0],
                self.inner_from.at[up],
                self.col_sems.at[2],
                self.col_sems.at[3],
                spot.column_peer(up),
            ).start(),
        )
        for work in beside:
            work()
        own = raw[8 * spot.c + spot.z].astype(F32)
        own_gain = gain[spot.z]
        wait_column(spot, self.from_col, self.col_sems.at[1])
        grad = jnp.zeros((8, BLOCK), F32)
        for zsrc in range(8):
            grad = grad + self.from_col[zsrc].astype(F32)
        wait_bytes(self.inner_from.at[pl.ds(1, 7)], self.col_sems.at[3])
        inner = jnp.zeros((1, 128), F32)
        for i in range(8):
            inner = inner + self.inner_from[i]
        inner = jnp.sum(jnp.where(diagonal, inner, 0.0), axis=1, keepdims=True) / D
        return scale * own_gain * grad - own * (scale * scale * scale) * inner

    def finish(self):
        for kk in range(2):
            wait_bytes(self.partial.at[kk], self.sib_send.at[kk])
            wait_bytes(self.partial.at[kk, pl.ds(0, 15)], self.xy_send.at[kk])
        wait_column(self.spot, self.to_col, self.col_sems.at[0])
        wait_bytes(self.inner_from.at[pl.ds(1, 7)], self.col_sems.at[2])
        wait_bytes(self.inner_from.at[pl.ds(8, 1)], self.col_sems.at[4])


def wait_column(spot, ref, sem):
    own = spot.half == spot.c

    @pl.when(own)
    def _():
        wait_bytes(ref.at[pl.ds(0, 7)], sem)

    @pl.when(jnp.logical_not(own))
    def _():
        wait_bytes(ref, sem)


def program(
    layer_out,
    resid_mid,
    final_gain,
    mlp_gain,
    teacher_in,
    assign,
    lengths,
    token_ids,
    head_hbm,
    gate_hbm,
    up_hbm,
    down_hbm,
    grad_first,
    grad_second,
    final_rows,
    normed,
    grad_rows,
    dlog_t,
    hidden_t,
    activated_t,
    head,
    w_gate_up,
    w_down,
    dlog,
    dlog_turned,
    hidden_turned,
    raw_out,
    raw_mid,
    full_out,
    full_mid,
    full_grad,
    packed,
    got,
    logits_ref,
    diff_ref,
    gate_up_pre,
    act_grad,
    first,
    second,
    stats_pad,
    own_b,
    own_from,
    scale_ref,
    load_sem,
    raw_sems,
    plane_sems,
    stat_sems,
    own_sems,
    xy_send,
    xy_recv,
    sib_send,
    sib_recv,
    *scratch,
):
    spot = Spot()
    c, other = spot.c, 1 - spot.c
    loads = [
        pltpu.make_async_copy(src, dst, load_sem.at[i])
        for i, (src, dst) in enumerate(
            (
                (head_hbm, head),
                (gate_hbm, w_gate_up.at[pl.ds(0, 64)]),
                (up_hbm, w_gate_up.at[pl.ds(64, 64)]),
                (down_hbm, w_down),
            )
        )
    ]
    for load in loads:
        load.start()
    reduces = [Reduce(spot, scratch[: len(REDUCE_SCRATCH)]), Reduce(spot, scratch[len(REDUCE_SCRATCH) :])]
    gathers = [
        Gather(spot, full, xy_send.at[a], xy_recv.at[a], sib_send.at[a], sib_recv.at[a])
        for a, full in enumerate((full_out, full_mid, full_grad))
    ]
    gather_out, gather_mid, gather_grad = gathers

    greet(spot)
    mine = 8 * c + spot.z
    raw_out[mine] = layer_out[...]
    raw_mid[mine] = resid_mid[...]

    greeted()

    def send_raw(a, own, raw):
        loop(
            1,
            8,
            lambda up: remote(
                own, raw.at[mine], raw_sems.at[a, 0], raw_sems.at[a, 1], spot.column_peer(up)
            ).start(),
        )

    def pass_raw(a, raw):
        wait_bytes(raw.at[pl.ds(0, 7)], raw_sems.at[a, 1])
        rows = raw.at[pl.ds(8 * c, 8)]
        remote(rows, rows, raw_sems.at[a, 2], raw_sems.at[a, 3], spot.sibling()).start()

    def plane_start(i, carry):
        peer = wrap(spot.d + i, 32)
        remote(packed.at[peer], got.at[spot.d], plane_sems.at[0], plane_sems.at[1], (peer, spot.z)).start()
        return carry

    def normalise(a, raw, full, gain):
        wait_bytes(raw.at[pl.ds(0, 8)], raw_sems.at[a, 3])
        scales = [row_scale(raw, core) for core in range(2)]
        for kk in range(2):
            place = spot.place(kk)
            for j in range(2):
                zb = 4 * c + 2 * kk + j
                rows = jnp.concatenate(
                    [raw[8 * core + zb].astype(F32) * scales[core] * gain[zb] for core in range(2)], axis=0
                )
                full[2 * c + kk, place, :, j * BLOCK : (j + 1) * BLOCK] = rows.astype(BF16)
        for core in range(2):
            scale_ref[a, core] = jnp.broadcast_to(scales[core], (8, 128))

    def both(gather, stage):
        for kk in range(2):
            gather.step(stage, kk)

    send_raw(0, layer_out, raw_out)

    row = lax.broadcasted_iota(jnp.int32, (8, 1), 0)
    order = jnp.zeros((8, 1), jnp.int32)
    for r in range(8):
        order = jnp.where(row == r, assign[0, r], order)

    def pack(peer):
        rows = teacher_in[:, pl.ds(pl.multiple_of(peer * 384, 384), 384)].astype(F32)
        picked = jnp.zeros((8, 384), F32)
        for r in range(8):
            picked = picked + jnp.where(order == r, rows[r : r + 1, :], 0.0)
        packed[peer] = picked.astype(BF16)

    loop(0, 32, pack)
    got[spot.d] = packed[spot.d]

    token = lax.broadcasted_iota(jnp.int32, (1, 256), 1)
    own_ids = jnp.full((1, 256), -1, jnp.int32)
    own_lengths = jnp.zeros((1, 256), jnp.int32)
    for r in range(8):
        here = token == 8 * spot.d + r
        own_ids = jnp.where(here, token_ids[r], own_ids)
        own_lengths = jnp.where(here, lengths[0, r // SLOT], own_lengths)
    live = (lax.rem(token, SLOT) < own_lengths).astype(jnp.int32)
    codes = jnp.where(own_ids >= 0, 2 * own_ids + live, 0).astype(F32)

    lax.fori_loop(1, 14, plane_start, 0)
    send_raw(1, resid_mid, raw_mid)
    pass_raw(0, raw_out)
    normalise(0, raw_out, full_out, final_gain)
    both(gather_out, 0)
    lax.fori_loop(14, 32, plane_start, 0)
    both(gather_out, 1)
    pass_raw(1, raw_mid)
    both(gather_out, 2)
    normalise(1, raw_mid, full_mid, mlp_gain)
    both(gather_out, 3)

    def products(left, right, out, core):
        def body(kk):
            columns = slice_columns(kk, core)
            out[...] += contract_cols(left[:, columns], right[:, columns])

        loop(0, 2, body)

    for kk in range(2):
        lay_out(full_out, final_rows, kk, c)
    loads[0].wait()
    logits_ref[...] = jnp.zeros_like(logits_ref)
    products(final_rows, head, logits_ref, c)
    both(gather_mid, 0)
    both(gather_out, 4)
    for kk in range(2):
        lay_out(full_out, final_rows, kk, other)
    products(final_rows, head, logits_ref, other)

    wait_bytes(got.at[pl.ds(0, 31)], plane_sems.at[1])
    logits = logits_ref[...]
    diff = logits - got[...].astype(F32).reshape(256, 384)
    local_max = jnp.max(logits, axis=1, keepdims=True)
    expd = jnp.exp(logits - local_max)
    total = jnp.sum(expd, axis=1, keepdims=True)
    moment = jnp.sum(expd * diff, axis=1, keepdims=True)
    logits_ref[...] = expd
    diff_ref[...] = diff
    lanes = lax.broadcasted_iota(jnp.int32, (256, 128), 1)
    columns = jnp.where(lanes == 0, local_max, jnp.where(lanes == 1, total, moment))
    first[0] = jnp.transpose(columns)[0:4]
    first[0, 3:4] = codes
    remote(first.at[0], first.at[1], stat_sems.at[0], stat_sems.at[1], spot.sibling()).start()

    def to_column(up):
        for flip in range(2):
            target = spot.column_peer(up, flip)
            remote(first.at[0], first.at[2 * up + flip], stat_sems.at[0], stat_sems.at[1], target).start()

    loop(1, 8, to_column)
    both(gather_mid, 1)

    place = lax.broadcasted_iota(jnp.int32, (4, 256), 0)

    def combine(ref, groups):
        top = ref[0, 0:1]
        for i in range(1, 16):
            top = jnp.maximum(top, ref[i, 0:1])
        sums = jnp.zeros((4, 256), F32)
        for i in range(16):
            sums = sums + ref[i] * jnp.exp(ref[i, 0:1] - top)
        coded = sum(ref[i] for i in range(groups))
        return jnp.where(place == 0, top, jnp.where(place == 3, coded, sums))

    wait_bytes(first.at[pl.ds(1, 15)], stat_sems.at[1])
    second[0] = combine(first, 2)

    def to_plane(i):
        target = (wrap(spot.chip + i, CHIPS) * 2 + c, spot.z)
        remote(second.at[0], second.at[i], stat_sems.at[2], stat_sems.at[3], target).start()

    loop(1, CHIPS, to_plane)
    both(gather_mid, 2)
    vocab = lax.broadcasted_iota(jnp.int32, (256, 384), 1) + (spot.z * 32 + spot.d) * 384
    stats_pad[...] = jnp.zeros_like(stats_pad)
    wait_bytes(second.at[pl.ds(1, 15)], stat_sems.at[3])
    stats_pad[0:4] = combine(second, 16)
    columns = jnp.transpose(stats_pad[...])
    global_max, totals, moments = columns[:, 0:1], columns[:, 1:2], columns[:, 2:3]
    code = columns[:, 3:4].astype(jnp.int32)
    ids_all = code >> 1
    live_mask = (code - 2 * ids_all).astype(F32)
    token_weight = live_mask * (LOSS_SCALE / jnp.sum(live_mask, axis=0, keepdims=True))
    share = token_weight * (jnp.exp(local_max - global_max) / totals)
    shift = CE_WEIGHT - moments / totals
    dlogits = share * logits_ref[...] * (diff_ref[...] + shift)
    dlogits = dlogits - jnp.where(ids_all == vocab, CE_WEIGHT * token_weight, 0.0)

    def turn(rows, out):
        for k in range(4):
            for chip in range(CHIPS):
                place = 16 * block_place(k, chip)
                out[k, place : place + 16, :] = rows[16 * chip : 16 * chip + 16]

    def spread(reduce, kk, core, half, left, right):
        k = 2 * core + kk
        rows = left[k, pl.ds(pl.multiple_of(half * 128, 128), 128)]
        part = jnp.dot(rows, right[:, slice_columns(kk, core)], preferred_element_type=F32).astype(BF16)
        reduce.partial[k, pl.ds(half * 8, 8)] = part.reshape(8, 16, SLICE)

    def partials(reduce, left, right):

        def sib_part(kk, sub):
            bit = spot.sib_bit(kk, 0)
            spread(reduce, kk, other, (1 - bit) if sub == 0 else bit, left, right)
            reduce.start(kk, sub)

        def own_part(kk, sub):
            bit = spot.bit(kk, 0)
            spread(reduce, kk, c, (1 - bit) if sub == 0 else bit, left, right)

        return sib_part, own_part

    dlog_b = dlogits.astype(BF16)
    turn(dlog_b, dlog_turned)
    dlog[...] = dlog_b

    def mid_rows(core):
        for kk in range(2):
            lay_out(full_mid, normed, kk, core)

    def mid_first():
        for load in loads[1:]:
            load.wait()
        gate_up_pre[...] = jnp.zeros_like(gate_up_pre)
        act_grad[...] = jnp.zeros_like(act_grad)
        mid_rows(c)
        products(w_gate_up, normed, gate_up_pre, c)

    def mid_third():
        both(gather_mid, 3)

    def mid_second():
        both(gather_mid, 4)
        mid_rows(other)
        products(w_gate_up, normed, gate_up_pre, other)

    def activate():
        gate, up = gate_up_pre[0:64], gate_up_pre[64:128]
        gate_sigmoid = jax.nn.sigmoid(gate)
        activated_t[...] = (gate * gate_sigmoid * up).astype(BF16)
        gate_up_pre[0:64] = up * gate_sigmoid * (1.0 + gate * (1.0 - gate_sigmoid))
        gate_up_pre[64:128] = gate * gate_sigmoid

    def turn_dlog():
        dlog_t[...] = jnp.transpose(dlog[...].astype(F32)).astype(BF16)

    sums = reduces[0].plane(partials(reduces[0], dlog_turned, head), {})
    grad_out = reduces[0].column(sums, raw_out, final_gain, scale_ref[0, c][:, 0:1], [mid_third, mid_first, turn_dlog])
    own_b[...] = grad_out.astype(BF16)
    grad_first[...] = grad_out

    target_core = spot.half
    own_place = spot.z_low * 2 + c

    def own_to_column(zdst):
        mine = jnp.logical_and(spot.z == zdst, target_core == c)

        @pl.when(jnp.logical_not(mine))
        def _():
            target = (spot.chip * 2 + target_core, zdst)
            remote(own_b, own_from.at[own_place], own_sems.at[0], own_sems.at[1], target).start()

        @pl.when(mine)
        def _():
            own_from[own_place] = own_b[...]

    loop(0, 8, own_to_column)
    mid_second()
    activate()
    wait_column(spot, own_from, own_sems.at[1])
    for kk in range(2):
        for j in range(2):
            zz = 2 * kk + j
            rows = jnp.concatenate([own_from[2 * zz + core].astype(F32) for core in range(2)], axis=0)
            full_grad[2 * c + kk, spot.place(kk), :, j * BLOCK : (j + 1) * BLOCK] = rows.astype(BF16)
    both(gather_grad, 0)
    for stage in range(1, 4):
        both(gather_grad, stage)
    for kk in range(2):
        lay_out(full_grad, grad_rows, kk, c)
    products(w_down, grad_rows, act_grad, c)
    both(gather_grad, 4)
    for kk in range(2):
        lay_out(full_grad, grad_rows, kk, other)
    products(w_down, grad_rows, act_grad, other)

    act = act_grad[...]
    both_grads = jnp.concatenate([act * gate_up_pre[0:64], act * gate_up_pre[64:128]], axis=0)
    turn(jnp.transpose(both_grads).astype(BF16), hidden_turned)
    hidden_t[...] = both_grads.astype(BF16)

    def left_earlier():
        for a in range(2):
            wait_bytes(raw_out.at[pl.ds(0, 7)], raw_sems.at[a, 0])
            wait_bytes(raw_out.at[pl.ds(0, 8)], raw_sems.at[a, 2])
        wait_bytes(got.at[pl.ds(0, 31)], plane_sems.at[0])
        wait_bytes(first.at[pl.ds(1, 15)], stat_sems.at[0])
        wait_bytes(second.at[pl.ds(1, 15)], stat_sems.at[2])
        for gather in gathers:
            gather.finish()
        reduces[0].finish()
        wait_column(spot, own_from, own_sems.at[0])

    sums = reduces[1].plane(partials(reduces[1], hidden_turned, w_gate_up), {})
    grad_second[...] = reduces[1].column(sums, raw_mid, mlp_gain, scale_ref[1, c][:, 0:1], [left_earlier])
    reduces[1].finish()


def weight_grads(
    grad_first,
    grad_second,
    dlog_t,
    hidden_t,
    activated_t,
    final_rows,
    normed,
    grad_rows,
    grad_resid,
    grad_head,
    grad_gate,
    grad_up,
    grad_down,
    head_rows,
    gate_up_rows,
    down_rows,
    sems,
):
    def product(left, right):
        return jnp.dot(left, right, preferred_element_type=F32).astype(BF16)

    grad_resid[...] = (grad_first[...] + grad_second[...]).astype(BF16)

    def copies(k):
        place = pl.ds(pl.multiple_of(k * BLOCK, BLOCK), BLOCK)
        return [
            pltpu.make_async_copy(head_rows.at[:, place], grad_head.at[:, place], sems.at[0, k]),
            pltpu.make_async_copy(gate_up_rows.at[pl.ds(0, 64), place], grad_gate.at[:, place], sems.at[1, k]),
            pltpu.make_async_copy(gate_up_rows.at[pl.ds(64, 64), place], grad_up.at[:, place], sems.at[2, k]),
            pltpu.make_async_copy(down_rows.at[:, place], grad_down.at[:, place], sems.at[3, k]),
        ]

    def chunk(k):
        place = pl.ds(pl.multiple_of(k * BLOCK, BLOCK), BLOCK)
        to_head, to_gate, to_up, to_down = copies(k)
        head_rows[:, place] = product(dlog_t[...], final_rows[:, place])
        to_head.start()
        gate_up_rows[:, place] = product(hidden_t[...], normed[:, place])
        to_gate.start()
        to_up.start()
        down_rows[:, place] = product(activated_t[...], grad_rows[:, place])
        to_down.start()

    def done(k):
        for copy in copies(k):
            copy.wait()

    loop(0, 8, chunk)
    loop(0, 8, done)


def shape(dims, dtype):
    return jax.ShapeDtypeStruct(dims, dtype)


def per_device(
    layer_out,
    resid_mid,
    final_gain,
    mlp_gain,
    head_weight,
    w_gate,
    w_up,
    w_down,
    teacher_logits,
    assign,
    lengths,
    token_ids,
):
    final_gain = final_gain.reshape(8, 1, BLOCK)
    mlp_gain = mlp_gain.reshape(8, 1, BLOCK)
    vmem = pl.BlockSpec(memory_space=pltpu.VMEM)
    smem = pl.BlockSpec(memory_space=pltpu.SMEM)
    hbm = pl.BlockSpec(memory_space=pl.ANY)
    full = pltpu.VMEM((4, 16, 16, SLICE), BF16)
    rows = pltpu.VMEM((256, D), BF16)
    dma = pltpu.SemaphoreType.DMA
    shared = pl.pallas_call(
        program,
        out_shape=[
            pltpu.VMEM((8, BLOCK), F32),
            pltpu.VMEM((8, BLOCK), F32),
            rows,
            rows,
            rows,
            pltpu.VMEM((384, 256), BF16),
            pltpu.VMEM((128, 256), BF16),
            pltpu.VMEM((64, 256), BF16),
        ],
        in_specs=[vmem] * 5 + [smem] * 3 + [hbm] * 4,
        out_specs=[vmem] * 8,
        scratch_shapes=[
            pltpu.VMEM((384, D), BF16),
            pltpu.VMEM((128, D), BF16),
            pltpu.VMEM((64, D), BF16),
            pltpu.VMEM((256, 384), BF16),
            pltpu.VMEM((4, 256, 384), BF16),
            pltpu.VMEM((4, 256, 128), BF16),
            pltpu.VMEM((16, 8, BLOCK), BF16),
            pltpu.VMEM((16, 8, BLOCK), BF16),
            full,
            full,
            full,
            pltpu.VMEM((32, 8, 384), BF16),
            pltpu.VMEM((32, 8, 384), BF16),
            pltpu.VMEM((256, 384), F32),
            pltpu.VMEM((256, 384), F32),
            pltpu.VMEM((128, 256), F32),
            pltpu.VMEM((64, 256), F32),
            pltpu.VMEM((16, 4, 256), F32),
            pltpu.VMEM((16, 4, 256), F32),
            pltpu.VMEM((128, 256), F32),
            pltpu.VMEM((8, BLOCK), BF16),
            pltpu.VMEM((8, 8, BLOCK), BF16),
            pltpu.VMEM((2, 2, 8, 128), F32),
            dma((4,)),
            dma((2, 4)),
            dma((2,)),
            dma((4,)),
            dma((2,)),
            dma((3, 2)),
            dma((3, 2, 8)),
            dma((3, 2)),
            dma((3, 2, 5)),
        ]
        + REDUCE_SCRATCH
        + REDUCE_SCRATCH,
        compiler_params=pltpu.CompilerParams(
            collective_id=0, has_side_effects=True, vmem_limit_bytes=VMEM_LIMIT
        ),
        name="backward",
    )(
        layer_out,
        resid_mid,
        final_gain,
        mlp_gain,
        teacher_logits,
        assign,
        lengths,
        token_ids,
        head_weight,
        w_gate,
        w_up,
        w_down,
    )
    return pl.pallas_call(
        weight_grads,
        out_shape=[
            shape((8, BLOCK), BF16),
            shape(head_weight.shape, BF16),
            shape(w_gate.shape, BF16),
            shape(w_up.shape, BF16),
            shape(w_down.shape, BF16),
        ],
        in_specs=[vmem] * 8,
        out_specs=[vmem] + [hbm] * 4,
        scratch_shapes=[
            pltpu.VMEM((384, D), BF16),
            pltpu.VMEM((128, D), BF16),
            pltpu.VMEM((64, D), BF16),
            dma((4, 8)),
        ],
        compiler_params=pltpu.CompilerParams(vmem_limit_bytes=GRADS_VMEM),
        cost_estimate=pl.CostEstimate(flops=2 * 256 * 576 * D, bytes_accessed=2 * 576 * D, transcendentals=0),
        name="weight_grads",
    )(shared[0], shared[1], shared[5], shared[6], shared[7], shared[2], shared[3], shared[4])


def solution(mesh):
    return jax.shard_map(
        per_device,
        mesh=mesh,
        in_specs=(
            P("dp", "tensor"),
            P("dp", "tensor"),
            P(),
            P(),
            P(("tensor", "dp"), None),
            P(("tensor", "dp"), None),
            P(("tensor", "dp"), None),
            P(("tensor", "dp"), None),
            P("dp", "tensor"),
            P("dp", None),
            P("dp", None),
            P("dp"),
        ),
        out_specs=(
            P("dp", "tensor"),
            P(("tensor", "dp"), None),
            P(("tensor", "dp"), None),
            P(("tensor", "dp"), None),
            P(("tensor", "dp"), None),
        ),
        check_vma=False,
    )
```

```python
import jax
import jax.numpy as jnp
from jax import lax
from jax.experimental import pallas as pl
from jax.experimental.pallas import tpu as pltpu
from jax.sharding import PartitionSpec as P

D = 5120
SLOT = 4
EPS = 1e-06
CE_WEIGHT = 0.5
LOSS_SCALE = 4096.0

BLOCK = 640
SLICE = 1280
CHIPS = 16
F32 = jnp.float32
BF16 = jnp.bfloat16
VMEM_LIMIT = 52 * 1024 * 1024
GRADS_VMEM = 20 * 1024 * 1024


def contract_cols(left, right):
    return lax.dot_general(left, right, (((1,), (1,)), ((), ())), preferred_element_type=F32)


def wrap(v, size):
    return jnp.where(v >= size, v - size, v)


def ring_bits(v):
    high = v // 2
    return v % 2 + high - 2 * (v % 2) * high, high


class Spot:
    def __init__(self):
        self.d = lax.axis_index("dp")
        self.z = lax.axis_index("tensor")
        self.chip = lax.div(self.d, 2)
        self.c = self.d - 2 * self.chip
        self.y = lax.div(self.chip, 4)
        self.x = self.chip - 4 * self.y
        c, other = self.c, 1 - self.c
        xv, yv = lax.div(self.x, 2), lax.div(self.y, 2)
        x_low, y_low = self.x - 2 * xv, self.y - 2 * yv
        xu, yu = x_low + xv - 2 * x_low * xv, y_low + yv - 2 * y_low * yv
        x_near, y_near = self.x + 1 - 2 * x_low, self.y + 1 - 2 * y_low
        x_far, y_far = 3 - self.x, 3 - self.y
        self.half = lax.div(self.z, 4)
        self.z_low = self.z - 4 * self.half
        bits = (xu, yu, xv, yv)
        moved = (x_near, y_near, x_far, y_far)
        self.own_bits = [bits[i] * other + bits[(i + 2) % 4] * c for i in range(4)]
        self.sib_bits = [bits[i] * c + bits[(i + 2) % 4] * other for i in range(4)]
        moved = [moved[i] * other + moved[(i + 2) % 4] * c for i in range(4)]
        self.chips = [self.y * 4 + moved[i] if i % 2 == 0 else moved[i] * 4 + self.x for i in range(4)]
        corner = []
        for i in range(4):
            j = (i + 1) % 4
            corner.append(moved[j] * 4 + moved[i] if i % 2 == 0 else moved[i] * 4 + moved[j])
        self.corners = corner

    def pick(self, values, kk, s):
        if isinstance(kk, int):
            return values[(kk + s) % 4]
        first, second = values[s % 4], values[(s + 1) % 4]
        return first + (second - first) * kk

    def bit(self, kk, s):
        return self.pick(self.own_bits, kk, s)

    def sib_bit(self, kk, s):
        return self.pick(self.sib_bits, kk, s)

    def base(self, kk, s):
        return sum((self.bit(kk, i) * (8 >> i) for i in range(s)), jnp.int32(0))

    def sib_base(self, kk, s):
        return sum((self.sib_bit(kk, i) * (8 >> i) for i in range(s)), jnp.int32(0))

    def place(self, kk):
        return self.base(kk, 4)

    def partner(self, kk, s):
        return (self.pick(self.chips, kk, s) * 2 + self.c, self.z)

    def diagonal(self, kk, s):
        return (self.pick(self.corners, kk, s) * 2 + self.c, self.z)

    def sibling(self):
        return (self.chip * 2 + 1 - self.c, self.z)

    def column_peer(self, up, flip=0):
        core = self.c if flip == 0 else 1 - self.c
        return (self.chip * 2 + core, wrap(self.z + up, 8))


def greet(spot):
    barrier = pltpu.get_barrier_semaphore()
    mesh = pl.DeviceIdType.MESH
    pl.semaphore_signal(barrier, inc=1, device_id=spot.sibling(), device_id_type=mesh)

    def column(up, carry):
        for flip in range(2):
            pl.semaphore_signal(barrier, inc=1, device_id=spot.column_peer(up, flip), device_id_type=mesh)
        return carry

    lax.fori_loop(1, 8, column, 0)

    def body(j, carry):
        chip = wrap(spot.chip + j, CHIPS)
        for core in range(2):
            pl.semaphore_signal(
                barrier, inc=1, device_id=(chip * 2 + core, spot.z), device_id_type=pl.DeviceIdType.MESH
            )
        return carry

    lax.fori_loop(1, CHIPS, body, 0)


def greeted():
    pl.semaphore_wait(pltpu.get_barrier_semaphore(), 45)


def remote(src, dst, send_sem, recv_sem, target):
    return pltpu.make_async_remote_copy(
        src_ref=src,
        dst_ref=dst,
        send_sem=send_sem,
        recv_sem=recv_sem,
        device_id=target,
        device_id_type=pl.DeviceIdType.MESH,
    )


def row_scale(raw, core):
    total = jnp.zeros((8, BLOCK), F32)
    for zb in range(8):
        part = raw[8 * core + zb].astype(F32)
        total = total + part * part
    return lax.rsqrt(jnp.sum(total, axis=1, keepdims=True) / D + EPS)


def loop(start, stop, body):
    def step(i, carry):
        body(i)
        return carry

    lax.fori_loop(start, stop, step, 0)


def wait_bytes(ref, sem):
    pltpu.make_async_copy(ref, ref, sem).wait()


class Gather:
    def __init__(self, spot, full, xy_send, xy_recv, sib_send, sib_recv):
        self.spot, self.full = spot, full
        self.xy_send, self.xy_recv, self.sib_send, self.sib_recv = xy_send, xy_recv, sib_send, sib_recv

    def view(self, kk, off, n, core=None):
        core = self.spot.c if core is None else core
        return self.full.at[2 * core + kk, pl.ds(off, n)]

    def send(self, kk, target, idx, off, n):
        view = self.view(kk, off, n)
        remote(view, view, self.xy_send.at[kk], self.xy_recv.at[kk, idx], target).start()

    def arrived(self, kk, idx, off, n):
        wait_bytes(self.view(kk, off, n), self.xy_recv.at[kk, idx])

    def pass_on(self, kk, idx, off, n):
        view = self.view(kk, off, n)
        remote(view, view, self.sib_send.at[kk], self.sib_recv.at[kk, idx], self.spot.sibling()).start()

    def step(self, stage, kk):
        spot = self.spot
        flip = [(8 >> s) * (1 - 2 * spot.bit(kk, s)) for s in range(4)]
        own, four = spot.place(kk), spot.base(kk, 2)
        if stage == 0:
            self.send(kk, spot.diagonal(kk, 2), 2, own, 1)
            self.send(kk, spot.partner(kk, 3), 0, own, 1)
            self.send(kk, spot.partner(kk, 2), 1, own, 1)
        elif stage == 1:
            self.arrived(kk, 0, own + flip[3], 1)
            self.arrived(kk, 1, own + flip[2], 1)
            self.arrived(kk, 2, own + flip[2] + flip[3], 1)
            self.send(kk, spot.partner(kk, 1), 3, four, 2)
            self.send(kk, spot.partner(kk, 1), 4, four + 2, 2)
            self.send(kk, spot.partner(kk, 0), 5, four, 4)
            self.pass_on(kk, 0, four, 4)
        elif stage == 2:
            new = four + flip[1]
            for i in range(2):
                self.arrived(kk, 3 + i, new + 2 * i, 2)
                self.send(kk, spot.partner(kk, 0), 6 + i, new + 2 * i, 2)
            self.pass_on(kk, 1, new, 4)
        elif stage == 3:
            new = four + flip[0]
            self.arrived(kk, 5, new, 4)
            self.pass_on(kk, 2, new, 4)
            new = new + flip[1]
            for i in range(2):
                self.arrived(kk, 6 + i, new + 2 * i, 2)
                self.pass_on(kk, 3 + i, new + 2 * i, 2)
        else:
            other = 1 - spot.c
            four = spot.sib_base(kk, 2)
            over_1 = four + 4 * (1 - 2 * spot.sib_bit(kk, 1))
            over_0 = 8 * (1 - 2 * spot.sib_bit(kk, 0))
            last = over_1 + over_0
            pieces = ((four, 4), (over_1, 4), (four + over_0, 4), (last, 2), (last + 2, 2))
            for idx, (off, n) in enumerate(pieces):
                wait_bytes(self.view(kk, off, n, other), self.sib_recv.at[kk, idx])

    def finish(self):
        for kk in range(2):
            wait_bytes(self.full.at[kk, pl.ds(0, 15)], self.xy_send.at[kk])
            wait_bytes(self.full.at[kk], self.sib_send.at[kk])


def block_place(k, chip):
    xu, xv = ring_bits(chip % 4)
    yu, yv = ring_bits(chip // 4)
    bits = (xu, yu, xv, yv)
    return sum(bits[(k + s) % 4] * (8 >> s) for s in range(4))


def slice_columns(kk, core):
    return pl.ds(pl.multiple_of((2 * core + kk) * SLICE, SLICE), SLICE)


def lay_out(full, out, kk, core):
    for chip in range(CHIPS):
        low, high = block_place(kk, chip), block_place(2 + kk, chip)
        out[16 * chip : 16 * chip + 16, slice_columns(kk, core)] = full[2 * core + kk, low + (high - low) * core]


REDUCE_SCRATCH = [
    pltpu.VMEM((4, 16, 16, SLICE), BF16),
    pltpu.VMEM((2, 16, 16, SLICE), BF16),
    pltpu.VMEM((2, 15, 16, SLICE), BF16),
    pltpu.VMEM((8, 8, BLOCK), BF16),
    pltpu.VMEM((8, 8, BLOCK), BF16),
    pltpu.VMEM((2, 1, 128), F32),
    pltpu.VMEM((9, 1, 128), F32),
    pltpu.SemaphoreType.DMA((2,)),
    pltpu.SemaphoreType.DMA((2, 2)),
    pltpu.SemaphoreType.DMA((2,)),
    pltpu.SemaphoreType.DMA((2, 7)),
    pltpu.SemaphoreType.DMA((6,)),
]


class Reduce:
    def __init__(self, spot, scratch):
        self.spot = spot
        (
            self.partial,
            self.from_sib,
            self.from_xy,
            self.to_col,
            self.from_col,
            self.inner_to,
            self.inner_from,
            self.sib_send,
            self.sib_recv,
            self.xy_send,
            self.xy_recv,
            self.col_sems,
        ) = scratch

    def sib_copy(self, kk, sub, core, bit):
        half = (1 - sub) * (1 - bit) + sub * bit
        return remote(
            self.partial.at[2 * core + kk, pl.ds(half * 8, 8)],
            self.from_sib.at[kk, pl.ds(half * 8, 8)],
            self.sib_send.at[kk],
            self.sib_recv.at[kk, sub],
            self.spot.sibling(),
        )

    def start(self, kk, sub):
        self.sib_copy(kk, sub, 1 - self.spot.c, self.spot.sib_bit(kk, 0)).start()

    def from_sibling(self, kk, sub):
        self.sib_copy(kk, sub, self.spot.c, self.spot.bit(kk, 0)).wait_recv()

    def add(self, kk, off, ref, ref_off, n):
        k = 2 * self.spot.c + kk

        def body(i, carry):
            self.partial[k, off + i] = self.partial[k, off + i] + ref[kk, ref_off + i]
            return carry

        if n == 1:
            body(0, 0)
        else:
            lax.fori_loop(0, n, body, 0)

    def plan(self, kk, s):
        n = 8 >> s
        landing = 16 - 2 * n
        bit = self.spot.bit(kk, s)
        gone = self.spot.base(kk, s) + (1 - bit) * n
        kept = self.spot.base(kk, s) + bit * n
        half = n // 2
        after = self.spot.bit(kk, s + 1)
        pieces = []
        for sub in range(2):
            shift = ((1 - after) if sub == 0 else after) * half
            pieces.append((gone + shift, kept + shift, landing + sub * half, half, 2 * s + sub))
        return pieces

    def xy_copy(self, kk, s, piece):
        gone, _, landing, n, idx = piece
        return remote(
            self.partial.at[2 * self.spot.c + kk, pl.ds(gone, n)],
            self.from_xy.at[kk, pl.ds(landing, n)],
            self.xy_send.at[kk],
            self.xy_recv.at[kk, idx],
            self.spot.partner(kk, s),
        )

    def xy_start(self, kk, s, piece):
        self.xy_copy(kk, s, piece).start()

    def plane(self, parts, beside):
        sib_part, own_part = parts
        spot = self.spot

        def first(kk):
            self.from_sibling(kk, 0)
            for piece in self.plan(kk, 0):
                self.add(kk, piece[0], self.from_sib, piece[0], piece[3])
                self.xy_start(kk, 0, piece)

        def kept(kk):
            self.from_sibling(kk, 1)
            self.add(kk, spot.bit(kk, 0) * 8, self.from_sib, spot.bit(kk, 0) * 8, 8)

        def arrive(kk, s, sub):
            piece = self.plan(kk, s)[sub]
            self.xy_copy(kk, s, piece).wait_recv()
            self.add(kk, piece[1], self.from_xy, piece[2], piece[3])

        def second(kk):
            arrive(kk, 0, 0)
            for follow in self.plan(kk, 1):
                self.xy_start(kk, 1, follow)

        def third(kk):
            arrive(kk, 1, 0)
            by_2 = spot.place(kk) + 2 * (1 - 2 * spot.bit(kk, 2))
            self.tail_copy(kk, by_2 + 1 - 2 * spot.bit(kk, 3), 2, spot.diagonal(kk, 2)).start()
            self.tail_copy(kk, by_2, 0, spot.partner(kk, 2)).start()

        def fourth(kk):
            arrive(kk, 1, 1)
            own = spot.place(kk)
            self.tail_copy(kk, own + 1 - 2 * spot.bit(kk, 3), 1, spot.partner(kk, 3)).start()

        for kk in range(2):
            sib_part(kk, 0)
        for kk in range(2):
            own_part(kk, 0)
            first(kk)
        for kk in range(2):
            sib_part(kk, 1)
        for kk in range(2):
            own_part(kk, 1)
        for kk in range(2):
            kept(kk)
        for work in beside.get(-1, ()):
            work()
        for kk in range(2):
            second(kk)
        for kk in range(2):
            arrive(kk, 0, 1)
        for work in beside.get(0, ()):
            work()
        for kk in range(2):
            third(kk)
        for kk in range(2):
            fourth(kk)
        for work in beside.get(1, ()):
            work()
        places = [spot.place(kk) for kk in range(2)]
        sums = []
        for kk in range(2):
            total = self.partial[2 * spot.c + kk, places[kk]].astype(F32)
            for i in range(3):
                self.tail_copy(kk, places[kk], i, spot.sibling()).wait_recv()
                total = total + self.from_xy[kk, 12 + i].astype(F32)
            sums.append(total)
        return sums

    def tail_copy(self, kk, block, i, target):
        return remote(
            self.partial.at[2 * self.spot.c + kk, pl.ds(block, 1)],
            self.from_xy.at[kk, pl.ds(12 + i, 1)],
            self.xy_send.at[kk],
            self.xy_recv.at[kk, 4 + i],
            target,
        )

    def column(self, sums, raw, gain, scale, beside=()):
        spot = self.spot
        for kk in range(2):
            for j in range(2):
                for core in range(2):
                    part = sums[kk][8 * core : 8 * core + 8, j * BLOCK : (j + 1) * BLOCK]
                    self.to_col[2 * (2 * kk + j) + core] = part.astype(BF16)

        def to_column(zz):
            zdst = 4 * spot.c + zz
            for core in range(2):
                mine = jnp.logical_and(zdst == spot.z, spot.c == core)

                @pl.when(jnp.logical_not(mine))
                def _(core=core):
                    remote(
                        self.to_col.at[2 * zz + core],
                        self.from_col.at[spot.z],
                        self.col_sems.at[0],
                        self.col_sems.at[1],
                        (spot.chip * 2 + core, zdst),
                    ).start()

                @pl.when(mine)
                def _(core=core):
                    self.from_col[spot.z] = self.to_col[2 * zz + core]

        loop(0, 4, to_column)
        row = lax.broadcasted_iota(jnp.int32, (8, 128), 0)
        diagonal = row == lax.broadcasted_iota(jnp.int32, (8, 128), 1)
        for core in range(2):
            total = jnp.zeros((8, BLOCK), F32)
            for kk in range(2):
                for j in range(2):
                    zb = 4 * spot.c + 2 * kk + j
                    part = sums[kk][8 * core : 8 * core + 8, j * BLOCK : (j + 1) * BLOCK]
                    total = total + raw[8 * core + zb].astype(F32) * gain[zb] * part
            inner = jnp.where(diagonal, jnp.sum(total, axis=1, keepdims=True), 0.0)
            self.inner_to[core] = jnp.sum(inner, axis=0, keepdims=True)
        to_sibling = remote(
            self.inner_to.at[1 - spot.c],
            self.inner_from.at[8],
            self.col_sems.at[4],
            self.col_sems.at[5],
            spot.sibling(),
        )
        to_sibling.start()
        to_sibling.wait_recv()
        self.inner_from[0] = self.inner_to[spot.c] + self.inner_from[8]
        loop(
            1,
            8,
            lambda up: remote(
                self.inner_from.at[0],
                self.inner_from.at[up],
                self.col_sems.at[2],
                self.col_sems.at[3],
                spot.column_peer(up),
            ).start(),
        )
        for work in beside:
            work()
        own = raw[8 * spot.c + spot.z].astype(F32)
        own_gain = gain[spot.z]
        wait_column(spot, self.from_col, self.col_sems.at[1])
        grad = jnp.zeros((8, BLOCK), F32)
        for zsrc in range(8):
            grad = grad + self.from_col[zsrc].astype(F32)
        wait_bytes(self.inner_from.at[pl.ds(1, 7)], self.col_sems.at[3])
        inner = jnp.zeros((1, 128), F32)
        for i in range(8):
            inner = inner + self.inner_from[i]
        inner = jnp.sum(jnp.where(diagonal, inner, 0.0), axis=1, keepdims=True) / D
        return scale * own_gain * grad - own * (scale * scale * scale) * inner

    def finish(self):
        for kk in range(2):
            wait_bytes(self.partial.at[kk], self.sib_send.at[kk])
            wait_bytes(self.partial.at[kk, pl.ds(0, 15)], self.xy_send.at[kk])
        wait_column(self.spot, self.to_col, self.col_sems.at[0])
        wait_bytes(self.inner_from.at[pl.ds(1, 7)], self.col_sems.at[2])
        wait_bytes(self.inner_from.at[pl.ds(8, 1)], self.col_sems.at[4])


def wait_column(spot, ref, sem):
    own = spot.half == spot.c

    @pl.when(own)
    def _():
        wait_bytes(ref.at[pl.ds(0, 7)], sem)

    @pl.when(jnp.logical_not(own))
    def _():
        wait_bytes(ref, sem)


def program(
    layer_out,
    resid_mid,
    final_gain,
    mlp_gain,
    teacher_in,
    assign,
    lengths,
    token_ids,
    head_hbm,
    gate_hbm,
    up_hbm,
    down_hbm,
    grad_first,
    grad_second,
    final_rows,
    normed,
    grad_rows,
    dlog_t,
    hidden_t,
    activated_t,
    head,
    w_gate_up,
    w_down,
    dlog,
    dlog_turned,
    hidden_turned,
    raw_out,
    raw_mid,
    full_out,
    full_mid,
    full_grad,
    packed,
    got,
    logits_ref,
    diff_ref,
    gate_up_pre,
    act_grad,
    first,
    second,
    stats_pad,
    own_b,
    own_from,
    scale_ref,
    load_sem,
    raw_sems,
    plane_sems,
    stat_sems,
    own_sems,
    xy_send,
    xy_recv,
    sib_send,
    sib_recv,
    *scratch,
):
    spot = Spot()
    c, other = spot.c, 1 - spot.c
    loads = [
        pltpu.make_async_copy(src, dst, load_sem.at[i])
        for i, (src, dst) in enumerate(
            (
                (head_hbm, head),
                (gate_hbm, w_gate_up.at[pl.ds(0, 64)]),
                (up_hbm, w_gate_up.at[pl.ds(64, 64)]),
                (down_hbm, w_down),
            )
        )
    ]
    for load in loads:
        load.start()
    reduces = [Reduce(spot, scratch[: len(REDUCE_SCRATCH)]), Reduce(spot, scratch[len(REDUCE_SCRATCH) :])]
    gathers = [
        Gather(spot, full, xy_send.at[a], xy_recv.at[a], sib_send.at[a], sib_recv.at[a])
        for a, full in enumerate((full_out, full_mid, full_grad))
    ]
    gather_out, gather_mid, gather_grad = gathers

    greet(spot)
    mine = 8 * c + spot.z
    raw_out[mine] = layer_out[...]
    raw_mid[mine] = resid_mid[...]

    greeted()

    def send_raw(a, own, raw):
        loop(
            1,
            8,
            lambda up: remote(
                own, raw.at[mine], raw_sems.at[a, 0], raw_sems.at[a, 1], spot.column_peer(up)
            ).start(),
        )

    def pass_raw(a, raw):
        wait_bytes(raw.at[pl.ds(0, 7)], raw_sems.at[a, 1])
        rows = raw.at[pl.ds(8 * c, 8)]
        remote(rows, rows, raw_sems.at[a, 2], raw_sems.at[a, 3], spot.sibling()).start()

    def plane_start(i, carry):
        peer = wrap(spot.d + i, 32)
        remote(packed.at[peer], got.at[spot.d], plane_sems.at[0], plane_sems.at[1], (peer, spot.z)).start()
        return carry

    def normalise(a, raw, full, gain):
        wait_bytes(raw.at[pl.ds(0, 8)], raw_sems.at[a, 3])
        scales = [row_scale(raw, core) for core in range(2)]
        for kk in range(2):
            place = spot.place(kk)
            for j in range(2):
                zb = 4 * c + 2 * kk + j
                rows = jnp.concatenate(
                    [raw[8 * core + zb].astype(F32) * scales[core] * gain[zb] for core in range(2)], axis=0
                )
                full[2 * c + kk, place, :, j * BLOCK : (j + 1) * BLOCK] = rows.astype(BF16)
        for core in range(2):
            scale_ref[a, core] = jnp.broadcast_to(scales[core], (8, 128))

    def both(gather, stage):
        for kk in range(2):
            gather.step(stage, kk)

    send_raw(0, layer_out, raw_out)

    row = lax.broadcasted_iota(jnp.int32, (8, 1), 0)
    order = jnp.zeros((8, 1), jnp.int32)
    for r in range(8):
        order = jnp.where(row == r, assign[0, r], order)

    def pack(peer):
        rows = teacher_in[:, pl.ds(pl.multiple_of(peer * 384, 384), 384)].astype(F32)
        picked = jnp.zeros((8, 384), F32)
        for r in range(8):
            picked = picked + jnp.where(order == r, rows[r : r + 1, :], 0.0)
        packed[peer] = picked.astype(BF16)

    loop(0, 32, pack)
    got[spot.d] = packed[spot.d]

    token = lax.broadcasted_iota(jnp.int32, (1, 256), 1)
    own_ids = jnp.full((1, 256), -1, jnp.int32)
    own_lengths = jnp.zeros((1, 256), jnp.int32)
    for r in range(8):
        here = token == 8 * spot.d + r
        own_ids = jnp.where(here, token_ids[r], own_ids)
        own_lengths = jnp.where(here, lengths[0, r // SLOT], own_lengths)
    live = (lax.rem(token, SLOT) < own_lengths).astype(jnp.int32)
    codes = jnp.where(own_ids >= 0, 2 * own_ids + live, 0).astype(F32)

    lax.fori_loop(1, 14, plane_start, 0)
    send_raw(1, resid_mid, raw_mid)
    pass_raw(0, raw_out)
    normalise(0, raw_out, full_out, final_gain)
    both(gather_out, 0)
    lax.fori_loop(14, 32, plane_start, 0)
    both(gather_out, 1)
    pass_raw(1, raw_mid)
    both(gather_out, 2)
    normalise(1, raw_mid, full_mid, mlp_gain)
    both(gather_out, 3)

    def products(left, right, out, core):
        def body(kk):
            columns = slice_columns(kk, core)
            out[...] += contract_cols(left[:, columns], right[:, columns])

        loop(0, 2, body)

    for kk in range(2):
        lay_out(full_out, final_rows, kk, c)
    loads[0].wait()
    logits_ref[...] = jnp.zeros_like(logits_ref)
    products(final_rows, head, logits_ref, c)
    both(gather_mid, 0)
    both(gather_out, 4)
    for kk in range(2):
        lay_out(full_out, final_rows, kk, other)
    products(final_rows, head, logits_ref, other)

    wait_bytes(got.at[pl.ds(0, 31)], plane_sems.at[1])
    logits = logits_ref[...]
    diff = logits - got[...].astype(F32).reshape(256, 384)
    local_max = jnp.max(logits, axis=1, keepdims=True)
    expd = jnp.exp(logits - local_max)
    total = jnp.sum(expd, axis=1, keepdims=True)
    moment = jnp.sum(expd * diff, axis=1, keepdims=True)
    logits_ref[...] = expd
    diff_ref[...] = diff
    lanes = lax.broadcasted_iota(jnp.int32, (256, 128), 1)
    columns = jnp.where(lanes == 0, local_max, jnp.where(lanes == 1, total, moment))
    first[0] = jnp.transpose(columns)[0:4]
    first[0, 3:4] = codes
    remote(first.at[0], first.at[1], stat_sems.at[0], stat_sems.at[1], spot.sibling()).start()

    def to_column(up):
        for flip in range(2):
            target = spot.column_peer(up, flip)
            remote(first.at[0], first.at[2 * up + flip], stat_sems.at[0], stat_sems.at[1], target).start()

    loop(1, 8, to_column)
    both(gather_mid, 1)

    place = lax.broadcasted_iota(jnp.int32, (4, 256), 0)

    def combine(ref, groups):
        top = ref[0, 0:1]
        for i in range(1, 16):
            top = jnp.maximum(top, ref[i, 0:1])
        sums = jnp.zeros((4, 256), F32)
        for i in range(16):
            sums = sums + ref[i] * jnp.exp(ref[i, 0:1] - top)
        coded = sum(ref[i] for i in range(groups))
        return jnp.where(place == 0, top, jnp.where(place == 3, coded, sums))

    wait_bytes(first.at[pl.ds(1, 15)], stat_sems.at[1])
    second[0] = combine(first, 2)

    def to_plane(i):
        target = (wrap(spot.chip + i, CHIPS) * 2 + c, spot.z)
        remote(second.at[0], second.at[i], stat_sems.at[2], stat_sems.at[3], target).start()

    loop(1, CHIPS, to_plane)
    both(gather_mid, 2)
    vocab = lax.broadcasted_iota(jnp.int32, (256, 384), 1) + (spot.z * 32 + spot.d) * 384
    stats_pad[...] = jnp.zeros_like(stats_pad)
    wait_bytes(second.at[pl.ds(1, 15)], stat_sems.at[3])
    stats_pad[0:4] = combine(second, 16)
    columns = jnp.transpose(stats_pad[...])
    global_max, totals, moments = columns[:, 0:1], columns[:, 1:2], columns[:, 2:3]
    code = columns[:, 3:4].astype(jnp.int32)
    ids_all = code >> 1
    live_mask = (code - 2 * ids_all).astype(F32)
    token_weight = live_mask * (LOSS_SCALE / jnp.sum(live_mask, axis=0, keepdims=True))
    share = token_weight * (jnp.exp(local_max - global_max) / totals)
    shift = CE_WEIGHT - moments / totals
    dlogits = share * logits_ref[...] * (diff_ref[...] + shift)
    dlogits = dlogits - jnp.where(ids_all == vocab, CE_WEIGHT * token_weight, 0.0)

    def turn(rows, out):
        for k in range(4):
            for chip in range(CHIPS):
                place = 16 * block_place(k, chip)
                out[k, place : place + 16, :] = rows[16 * chip : 16 * chip + 16]

    def spread(reduce, kk, core, half, left, right):
        k = 2 * core + kk
        rows = left[k, pl.ds(pl.multiple_of(half * 128, 128), 128)]
        part = jnp.dot(rows, right[:, slice_columns(kk, core)], preferred_element_type=F32).astype(BF16)
        reduce.partial[k, pl.ds(half * 8, 8)] = part.reshape(8, 16, SLICE)

    def partials(reduce, left, right):

        def sib_part(kk, sub):
            bit = spot.sib_bit(kk, 0)
            spread(reduce, kk, other, (1 - bit) if sub == 0 else bit, left, right)
            reduce.start(kk, sub)

        def own_part(kk, sub):
            bit = spot.bit(kk, 0)
            spread(reduce, kk, c, (1 - bit) if sub == 0 else bit, left, right)

        return sib_part, own_part

    dlog_b = dlogits.astype(BF16)
    turn(dlog_b, dlog_turned)
    dlog[...] = dlog_b

    def mid_rows(core):
        for kk in range(2):
            lay_out(full_mid, normed, kk, core)

    def mid_first():
        for load in loads[1:]:
            load.wait()
        gate_up_pre[...] = jnp.zeros_like(gate_up_pre)
        act_grad[...] = jnp.zeros_like(act_grad)
        mid_rows(c)
        products(w_gate_up, normed, gate_up_pre, c)

    def mid_third():
        both(gather_mid, 3)

    def mid_second():
        both(gather_mid, 4)
        mid_rows(other)
        products(w_gate_up, normed, gate_up_pre, other)

    def activate():
        gate, up = gate_up_pre[0:64], gate_up_pre[64:128]
        gate_sigmoid = jax.nn.sigmoid(gate)
        activated_t[...] = (gate * gate_sigmoid * up).astype(BF16)
        gate_up_pre[0:64] = up * gate_sigmoid * (1.0 + gate * (1.0 - gate_sigmoid))
        gate_up_pre[64:128] = gate * gate_sigmoid

    def turn_dlog():
        dlog_t[...] = jnp.transpose(dlog[...].astype(F32)).astype(BF16)

    sums = reduces[0].plane(partials(reduces[0], dlog_turned, head), {})
    grad_out = reduces[0].column(sums, raw_out, final_gain, scale_ref[0, c][:, 0:1], [mid_third, mid_first, turn_dlog])
    own_b[...] = grad_out.astype(BF16)
    grad_first[...] = grad_out

    target_core = spot.half
    own_place = spot.z_low * 2 + c

    def own_to_column(zdst):
        mine = jnp.logical_and(spot.z == zdst, target_core == c)

        @pl.when(jnp.logical_not(mine))
        def _():
            target = (spot.chip * 2 + target_core, zdst)
            remote(own_b, own_from.at[own_place], own_sems.at[0], own_sems.at[1], target).start()

        @pl.when(mine)
        def _():
            own_from[own_place] = own_b[...]

    loop(0, 8, own_to_column)
    mid_second()
    activate()
    wait_column(spot, own_from, own_sems.at[1])
    for kk in range(2):
        for j in range(2):
            zz = 2 * kk + j
            rows = jnp.concatenate([own_from[2 * zz + core].astype(F32) for core in range(2)], axis=0)
            full_grad[2 * c + kk, spot.place(kk), :, j * BLOCK : (j + 1) * BLOCK] = rows.astype(BF16)
    both(gather_grad, 0)
    for stage in range(1, 4):
        both(gather_grad, stage)
    for kk in range(2):
        lay_out(full_grad, grad_rows, kk, c)
    products(w_down, grad_rows, act_grad, c)
    both(gather_grad, 4)
    for kk in range(2):
        lay_out(full_grad, grad_rows, kk, other)
    products(w_down, grad_rows, act_grad, other)

    act = act_grad[...]
    both_grads = jnp.concatenate([act * gate_up_pre[0:64], act * gate_up_pre[64:128]], axis=0)
    turn(jnp.transpose(both_grads).astype(BF16), hidden_turned)
    hidden_t[...] = both_grads.astype(BF16)

    def left_earlier():
        for a in range(2):
            wait_bytes(raw_out.at[pl.ds(0, 7)], raw_sems.at[a, 0])
            wait_bytes(raw_out.at[pl.ds(0, 8)], raw_sems.at[a, 2])
        wait_bytes(got.at[pl.ds(0, 31)], plane_sems.at[0])
        wait_bytes(first.at[pl.ds(1, 15)], stat_sems.at[0])
        wait_bytes(second.at[pl.ds(1, 15)], stat_sems.at[2])
        for gather in gathers:
            gather.finish()
        reduces[0].finish()
        wait_column(spot, own_from, own_sems.at[0])

    sums = reduces[1].plane(partials(reduces[1], hidden_turned, w_gate_up), {})
    grad_second[...] = reduces[1].column(sums, raw_mid, mlp_gain, scale_ref[1, c][:, 0:1], [left_earlier])
    reduces[1].finish()


def weight_grads(
    grad_first,
    grad_second,
    dlog_t,
    hidden_t,
    activated_t,
    final_rows,
    normed,
    grad_rows,
    grad_resid,
    grad_head,
    grad_gate,
    grad_up,
    grad_down,
    head_rows,
    gate_up_rows,
    down_rows,
    sems,
):
    def product(left, right):
        return jnp.dot(left, right, preferred_element_type=F32).astype(BF16)

    grad_resid[...] = (grad_first[...] + grad_second[...]).astype(BF16)

    def copies(k):
        place = pl.ds(pl.multiple_of(k * SLICE, SLICE), SLICE)
        return [
            pltpu.make_async_copy(head_rows.at[:, place], grad_head.at[:, place], sems.at[0, k]),
            pltpu.make_async_copy(gate_up_rows.at[pl.ds(0, 64), place], grad_gate.at[:, place], sems.at[1, k]),
            pltpu.make_async_copy(gate_up_rows.at[pl.ds(64, 64), place], grad_up.at[:, place], sems.at[2, k]),
            pltpu.make_async_copy(down_rows.at[:, place], grad_down.at[:, place], sems.at[3, k]),
        ]

    def chunk(k):
        place = pl.ds(pl.multiple_of(k * SLICE, SLICE), SLICE)
        to_head, to_gate, to_up, to_down = copies(k)
        head_rows[:, place] = product(dlog_t[...], final_rows[:, place])
        to_head.start()
        gate_up_rows[:, place] = product(hidden_t[...], normed[:, place])
        to_gate.start()
        to_up.start()
        down_rows[:, place] = product(activated_t[...], grad_rows[:, place])
        to_down.start()

    def done(k):
        for copy in copies(k):
            copy.wait()

    loop(0, 4, chunk)
    loop(0, 4, done)


def shape(dims, dtype):
    return jax.ShapeDtypeStruct(dims, dtype)


def per_device(
    layer_out,
    resid_mid,
    final_gain,
    mlp_gain,
    head_weight,
    w_gate,
    w_up,
    w_down,
    teacher_logits,
    assign,
    lengths,
    token_ids,
):
    final_gain = final_gain.reshape(8, 1, BLOCK)
    mlp_gain = mlp_gain.reshape(8, 1, BLOCK)
    vmem = pl.BlockSpec(memory_space=pltpu.VMEM)
    smem = pl.BlockSpec(memory_space=pltpu.SMEM)
    hbm = pl.BlockSpec(memory_space=pl.ANY)
    full = pltpu.VMEM((4, 16, 16, SLICE), BF16)
    rows = pltpu.VMEM((256, D), BF16)
    dma = pltpu.SemaphoreType.DMA
    shared = pl.pallas_call(
        program,
        out_shape=[
            pltpu.VMEM((8, BLOCK), F32),
            pltpu.VMEM((8, BLOCK), F32),
            rows,
            rows,
            rows,
            pltpu.VMEM((384, 256), BF16),
            pltpu.VMEM((128, 256), BF16),
            pltpu.VMEM((64, 256), BF16),
        ],
        in_specs=[vmem] * 5 + [smem] * 3 + [hbm] * 4,
        out_specs=[vmem] * 8,
        scratch_shapes=[
            pltpu.VMEM((384, D), BF16),
            pltpu.VMEM((128, D), BF16),
            pltpu.VMEM((64, D), BF16),
            pltpu.VMEM((256, 384), BF16),
            pltpu.VMEM((4, 256, 384), BF16),
            pltpu.VMEM((4, 256, 128), BF16),
            pltpu.VMEM((16, 8, BLOCK), BF16),
            pltpu.VMEM((16, 8, BLOCK), BF16),
            full,
            full,
            full,
            pltpu.VMEM((32, 8, 384), BF16),
            pltpu.VMEM((32, 8, 384), BF16),
            pltpu.VMEM((256, 384), F32),
            pltpu.VMEM((256, 384), F32),
            pltpu.VMEM((128, 256), F32),
            pltpu.VMEM((64, 256), F32),
            pltpu.VMEM((16, 4, 256), F32),
            pltpu.VMEM((16, 4, 256), F32),
            pltpu.VMEM((128, 256), F32),
            pltpu.VMEM((8, BLOCK), BF16),
            pltpu.VMEM((8, 8, BLOCK), BF16),
            pltpu.VMEM((2, 2, 8, 128), F32),
            dma((4,)),
            dma((2, 4)),
            dma((2,)),
            dma((4,)),
            dma((2,)),
            dma((3, 2)),
            dma((3, 2, 8)),
            dma((3, 2)),
            dma((3, 2, 5)),
        ]
        + REDUCE_SCRATCH
        + REDUCE_SCRATCH,
        compiler_params=pltpu.CompilerParams(
            collective_id=0, has_side_effects=True, vmem_limit_bytes=VMEM_LIMIT
        ),
        name="backward",
    )(
        layer_out,
        resid_mid,
        final_gain,
        mlp_gain,
        teacher_logits,
        assign,
        lengths,
        token_ids,
        head_weight,
        w_gate,
        w_up,
        w_down,
    )
    return pl.pallas_call(
        weight_grads,
        out_shape=[
            shape((8, BLOCK), BF16),
            shape(head_weight.shape, BF16),
            shape(w_gate.shape, BF16),
            shape(w_up.shape, BF16),
            shape(w_down.shape, BF16),
        ],
        in_specs=[vmem] * 8,
        out_specs=[vmem] + [hbm] * 4,
        scratch_shapes=[
            pltpu.VMEM((384, D), BF16),
            pltpu.VMEM((128, D), BF16),
            pltpu.VMEM((64, D), BF16),
            dma((4, 4)),
        ],
        compiler_params=pltpu.CompilerParams(vmem_limit_bytes=GRADS_VMEM),
        cost_estimate=pl.CostEstimate(flops=2 * 256 * 576 * D, bytes_accessed=2 * 576 * D, transcendentals=0),
        name="weight_grads",
    )(shared[0], shared[1], shared[5], shared[6], shared[7], shared[2], shared[3], shared[4])


def solution(mesh):
    return jax.shard_map(
        per_device,
        mesh=mesh,
        in_specs=(
            P("dp", "tensor"),
            P("dp", "tensor"),
            P(),
            P(),
            P(("tensor", "dp"), None),
            P(("tensor", "dp"), None),
            P(("tensor", "dp"), None),
            P(("tensor", "dp"), None),
            P("dp", "tensor"),
            P("dp", None),
            P("dp", None),
            P("dp"),
        ),
        out_specs=(
            P("dp", "tensor"),
            P(("tensor", "dp"), None),
            P(("tensor", "dp"), None),
            P(("tensor", "dp"), None),
            P(("tensor", "dp"), None),
        ),
        check_vma=False,
    )
```
